32 devices in a mesh: seq: 16 (over z, y, x), wa: 2 (over core).
Axes of the slice: x: 2, y: 2, z: 4, core: 2. Of those that a mesh axis runs over, the one named last changes fastest.
Arguments:
- tokens: bfloat16 [16384, 1024], P(('seq', 'wa')), may hold values from -6 to 6
- cotangent: bfloat16 [16384, 1024], P(('seq', 'wa')), may hold values from -6 to 6
- doc_lengths: int32 [32], replicated, may hold values from 1 to 4096, as said below
- norm_gain: bfloat16 [1024], P('wa'), may hold values from 0.25 to 1.75
- in_weight: bfloat16 [1024, 3072], P('wa'), may hold values from -0.1875 to 0.1875
- conv_taps: bfloat16 [1024, 3], P('wa'), may hold values from -3.5 to 3.5
- out_weight: bfloat16 [1024, 1024], P('wa'), may hold values from -0.1875 to 0.1875
- ffn_gain: bfloat16 [1024], P('wa'), may hold values from 0.25 to 1.75
- gate_weight: bfloat16 [1024, 4608], P('wa'), may hold values from -0.1875 to 0.1875
- up_weight: bfloat16 [1024, 4608], P('wa'), may hold values from -0.1875 to 0.1875
- down_weight: bfloat16 [4608, 1024], P('wa'), may hold values from -0.09375 to 0.09375
Outputs:
- block_out: bfloat16 [16384, 1024], P(('seq', 'wa'))
- input_grad: bfloat16 [16384, 1024], P(('seq', 'wa'))
- norm_gain_grad: float32 [1024], P(('seq', 'wa'))
- in_weight_grad: float32 [1024, 3072], P(('seq', 'wa'))
- conv_taps_grad: float32 [1024, 3], P(('seq', 'wa'))
- out_weight_grad: float32 [1024, 1024], P(('seq', 'wa'))
- ffn_gain_grad: float32 [1024], P(('seq', 'wa'))
- gate_weight_grad: float32 [1024, 4608], P(('seq', 'wa'))
- up_weight_grad: float32 [1024, 4608], P(('seq', 'wa'))
- down_weight_grad: float32 [4608, 1024], P(('seq', 'wa'))
The draws below stay inside these ranges and needn't reach their ends.
Inputs may be any that keep to these rules, and one draw needn't show every extreme that they name: `doc_lengths`: lengths of the 32 documents laid end to end in stream order, summing to 16384; the first document has exactly 4096 tokens.
All inputs are finite; a program needn't handle non-finite values.
Results may differ from the reference program's by a relative error of at most 0.0086.
Values may be sent and summed in bfloat16 or wider, within the bound.
No kernel may reach another device: no remote copies, remote signals or barrier semaphores. Data moves between devices by JAX's collectives and lax.ppermute only.
A program may use at most 256 MiB of HBM per device.

```python
import jax
import jax.numpy as jnp
from jax import lax

D = 1024
FF = 4608
TAPS = 3
NDOCS = 32
TOKENS = 16384
DOC_MAX = 4096


def draw_doc_lengths(key, part):
    key = jax.random.fold_in(key, 11)
    remain = TOKENS - DOC_MAX
    others = NDOCS - 1
    spacing = remain // others
    spread = max(spacing // 3, 1)
    marks = jnp.arange(1, others, dtype=jnp.int32)
    base = marks * remain // others
    offsets = jax.random.randint(key, (others - 1,), -spread, spread + 1, dtype=jnp.int32)
    cuts = jnp.concatenate([jnp.zeros((1,), jnp.int32), base + offsets, jnp.full((1,), remain, jnp.int32)])
    lengths = cuts[1:] - cuts[:-1]
    return jnp.concatenate([jnp.full((1,), DOC_MAX, jnp.int32), lengths]).astype(jnp.int32)


def levels(stream_key, shape, cuts, low, largest):
    loudness = 1.0
    for position, blocks in cuts:
        draws = jax.random.uniform(jax.random.fold_in(jax.random.fold_in(stream_key, 6), position), (blocks,), jnp.float32, low / len(cuts), largest / len(cuts))
        loudness = loudness * jnp.repeat(jnp.exp(draws), shape[position] // blocks).reshape((-1,) + (1,) * (len(shape) - 1 - position))
    return loudness


def gaussian(rng, dims, scale, most, shards=(), kind=jnp.bfloat16):
    loudness = levels(rng, dims, shards, -0.22, 0.18) if shards else 1.0
    array = jax.random.normal(rng, dims, jnp.float32) * scale * loudness
    return jnp.minimum(jnp.maximum(array, -most), most).astype(kind)


def setup_inputs(seed: int = 0) -> dict:
    key_of = jax.random.split(jax.random.key(seed), 12)
    tokens = gaussian(key_of[0], (TOKENS, D), 1.0, 6.0, ((0, 32),))
    cotangent = gaussian(key_of[1], (TOKENS, D), 1.0, 6.0, ((0, 32),))
    doc_lengths = draw_doc_lengths(jax.random.fold_in(key_of[11], 71), 0)
    norm_gain = jnp.clip(1.0 + 0.15 * jax.random.normal(key_of[3], (D,), jnp.float32), 0.25, 1.75).astype(jnp.bfloat16)
    in_weight = gaussian(key_of[4], (D, 3 * D), D ** -0.5, 0.1875, ((0, 2),))
    conv_taps = gaussian(key_of[5], (D, TAPS), TAPS ** -0.5, 3.5, ((0, 2),))
    out_weight = gaussian(key_of[6], (D, D), D ** -0.5, 0.1875, ((0, 2),))
    ffn_gain = jnp.clip(1.0 + 0.15 * jax.random.normal(key_of[7], (D,), jnp.float32), 0.25, 1.75).astype(jnp.bfloat16)
    gate_weight = gaussian(key_of[8], (D, FF), D ** -0.5, 0.1875, ((0, 2),))
    up_weight = gaussian(key_of[9], (D, FF), D ** -0.5, 0.1875, ((0, 2),))
    down_weight = gaussian(key_of[10], (FF, D), FF ** -0.5, 0.09375, ((0, 2),))
    return dict(tokens=tokens, cotangent=cotangent, doc_lengths=doc_lengths, norm_gain=norm_gain, in_weight=in_weight, conv_taps=conv_taps, out_weight=out_weight, ffn_gain=ffn_gain, gate_weight=gate_weight, up_weight=up_weight, down_weight=down_weight)


@jax.custom_vjp
def low(v):
    return lax.optimization_barrier(v.astype(jnp.bfloat16)).astype(jnp.float32)

@jax.custom_vjp
def low_back(v):
    return v

def low_keep(v):
    return (low(v), None)

def low_pass(kept, grad):
    return (grad,)

def back_keep(v):
    return (v, None)

def back_low(kept, grad):
    return (low(grad),)
low.defvjp(low_keep, low_pass)
low_back.defvjp(back_keep, back_low)
epsilon = 1e-05

def matmul(left, right):
    return jnp.dot(left, right, precision=lax.Precision.HIGHEST, preferred_element_type=jnp.float32)

def mixer_block(params, carry, item):
    gain_one, w_in, taps, w_out, gain_two, w_gate, w_up, w_down = params
    resid, keep_one, keep_two = item
    width = resid.shape[1]
    scale_one = lax.rsqrt(lax.optimization_barrier(jnp.mean(resid * resid, axis=-1, keepdims=True)) + epsilon)
    norm_in = low(resid * scale_one * gain_one)
    proj = low_back(matmul(norm_in, w_in))
    mixed_in = proj[:, :width] * proj[:, 2 * width:]
    extended = jnp.concatenate([carry, mixed_in], axis=0)
    conv = taps[:, 0] * mixed_in + keep_one * taps[:, 1] * extended[1:-1] + keep_two * taps[:, 2] * extended[:-2]
    gated = low(proj[:, width:2 * width] * conv)
    branch = low_back(matmul(gated, w_out))
    hidden_res = resid + branch
    scale_two = lax.rsqrt(lax.optimization_barrier(jnp.mean(hidden_res * hidden_res, axis=-1, keepdims=True)) + epsilon)
    norm_ffn = low(hidden_res * scale_two * gain_two)
    gate = low_back(matmul(norm_ffn, w_gate))
    up_val = low_back(matmul(norm_ffn, w_up))
    act = low(jax.nn.silu(gate) * up_val)
    ffn_out = low_back(matmul(act, w_down))
    return (mixed_in[-2:], hidden_res + ffn_out)

def reference(tokens, cotangent, doc_lengths, norm_gain, in_weight, conv_taps, out_weight, ffn_gain, gate_weight, up_weight, down_weight):
    total, width = tokens.shape
    block_rows = min(4096, total)
    blocks = total // block_rows
    starts = (jnp.cumsum(doc_lengths) - doc_lengths).astype(jnp.int32)
    place = jnp.arange(total, dtype=jnp.int32)
    first = jnp.any(place[:, None] == starts[None, :], axis=1)
    before = jnp.any((place - 1)[:, None] == starts[None, :], axis=1)
    keep_one = jnp.where(first, 0.0, 1.0).astype(jnp.float32).reshape(blocks, block_rows, 1)
    keep_two = jnp.where(jnp.logical_or(first, before), 0.0, 1.0).astype(jnp.float32).reshape(blocks, block_rows, 1)
    params = tuple((w.astype(jnp.float32) for w in (norm_gain, in_weight, conv_taps, out_weight, ffn_gain, gate_weight, up_weight, down_weight)))

    def forward(resid, weights):
        step_fn = jax.checkpoint(lambda carry, item: mixer_block(weights, carry, item))
        carry_init = jnp.zeros((2, width), jnp.float32)
        _, outputs = lax.scan(step_fn, carry_init, (resid.reshape(blocks, block_rows, width), keep_one, keep_two))
        return outputs.reshape(total, width)
    block_out, pull = jax.vjp(forward, tokens.astype(jnp.float32), params)
    input_grad, weight_grads = pull(cotangent.astype(jnp.float32))
    gain_one_g, in_g, taps_g, out_g, gain_two_g, gate_g, up_g, down_g = weight_grads
    return (block_out.astype(jnp.bfloat16), input_grad.astype(jnp.bfloat16), gain_one_g, in_g, taps_g, out_g, gain_two_g, gate_g, up_g, down_g)
```

```python
import jax
import jax.numpy as jnp
from jax import lax
from jax.sharding import PartitionSpec as P

epsilon = 1e-05
AXES = ("seq", "wa")


def shifted(value, axis, steps):
    count = lax.axis_size(axis)
    first, last = (max(0, -steps), min(count, count - steps))
    return lax.ppermute(value, axis, [(source, source + steps) for source in range(first, last)])


def partner(value):
    return lax.ppermute(value, "wa", [(0, 1), (1, 0)])


def across(value, bit):
    count = lax.axis_size("seq")
    return lax.ppermute(value, "seq", [(place, place ^ (1 << bit)) for place in range(count)])


def left_dot(left, right):
    return lax.dot_general(
        left, right, (((0,), (0,)), ((), ())), preferred_element_type=jnp.float32
    )


def right_dot(left, right):
    return lax.dot_general(
        left, right, (((1,), (1,)), ((), ())), preferred_element_type=jnp.float32
    )


def plain_dot(left, right):
    return jnp.dot(left, right, preferred_element_type=jnp.float32)


def norm_back(grad_norm, normed, scale, gain):
    inner = grad_norm * gain
    return scale * (inner - normed * jnp.mean(inner * normed, axis=-1, keepdims=True))


def take(value, index, axis):
    return lax.dynamic_index_in_dim(value, index, axis, keepdims=False)


def total(terms):
    result = terms[0].astype(jnp.float32)
    for term in terms[1:]:
        result = result + term.astype(jnp.float32)
    return result


def exchange_sum(value, names, order, coords, move):
    names = list(names)
    terms = [value]
    for name in order:
        axis = names.index(name)
        mine = coords[name]
        send = total([take(term, 1 - mine, axis) for term in terms]).astype(jnp.bfloat16)
        terms = [take(term, mine, axis) for term in terms] + [move(send, name)]
        names.pop(axis)
    return terms


def local(
    tokens,
    cotangent,
    doc_lengths,
    norm_gain,
    in_weight,
    conv_taps,
    out_weight,
    ffn_gain,
    gate_weight,
    up_weight,
    down_weight,
):
    rows, width = tokens.shape
    hidden = down_weight.shape[0]
    chips = lax.axis_size("seq")
    top = chips.bit_length() - 2
    lower = list(range(top))
    chip = lax.axis_index("seq")
    core = lax.axis_index("wa")
    coords = {bit: (chip >> bit) & 1 for bit in range(top + 1)}
    coords["core"] = core

    def move(value, name):
        return partner(value) if name == "core" else across(value, name)

    def ordered(low, high):
        return jnp.where(core == 0, low, high)

    def both(own, axis):
        other = partner(own)
        return ordered(
            jnp.concatenate([own, other], axis=axis), jnp.concatenate([other, own], axis=axis)
        )

    def column_half(weight):
        halves = weight.reshape(weight.shape[0], 2, hidden)
        mine, other = take(halves, core, 1), partner(take(halves, 1 - core, 1))
        return ordered(
            jnp.concatenate([mine, other], axis=0), jnp.concatenate([other, mine], axis=0)
        )

    place = lax.axis_index(AXES) * rows + jnp.arange(rows, dtype=jnp.int32)
    starts = jnp.cumsum(doc_lengths) - doc_lengths
    first = jnp.any(place[:, None] == starts[None, :], axis=1)
    before = jnp.any((place - 1)[:, None] == starts[None, :], axis=1)
    keep_one = jnp.where(first, 0.0, 1.0).astype(jnp.float32)[:, None]
    keep_two = jnp.where(jnp.logical_or(first, before), 0.0, 1.0).astype(jnp.float32)[:, None]
    w_in = both(in_weight, 0)
    small = jnp.concatenate([norm_gain[:, None], ffn_gain[:, None], conv_taps], axis=1)
    small = both(small, 0).astype(jnp.float32)
    gain_one, gain_two, taps = small[:, 0], small[:, 1], small[:, 2:]
    w_out = both(out_weight, 0)
    w_gate = column_half(gate_weight)
    w_up = column_half(up_weight)
    cot_both = jnp.concatenate([cotangent, partner(cotangent)], axis=0)

    resid = tokens.astype(jnp.float32)
    scale_one = lax.rsqrt(jnp.mean(resid * resid, axis=-1, keepdims=True) + epsilon)
    normed_one = resid * scale_one
    norm_in = (normed_one * gain_one).astype(jnp.bfloat16)
    proj = plain_dot(norm_in, w_in)
    b_part = proj[:, :width]
    c_part = proj[:, width : 2 * width]
    x_part = proj[:, 2 * width :]
    mixed_in = b_part * x_part
    previous = shifted(mixed_in[-2:], AXES, 1)
    extended = jnp.concatenate([previous, mixed_in], axis=0)
    back_one = extended[1:-1]
    back_two = extended[:-2]
    conv = (
        taps[:, 0] * mixed_in + keep_one * taps[:, 1] * back_one + keep_two * taps[:, 2] * back_two
    )
    gated = (c_part * conv).astype(jnp.bfloat16)
    hidden_res = resid + plain_dot(gated, w_out)
    scale_two = lax.rsqrt(jnp.mean(hidden_res * hidden_res, axis=-1, keepdims=True) + epsilon)
    normed_two = hidden_res * scale_two
    norm_ffn = (normed_two * gain_two).astype(jnp.bfloat16)

    norm_both = jnp.concatenate([norm_ffn, partner(norm_ffn)], axis=0)
    gate = plain_dot(norm_both, w_gate)
    up_val = plain_dot(norm_both, w_up)
    sigma = jax.nn.sigmoid(gate)
    silu_gate = gate * sigma
    act = (silu_gate * up_val).astype(jnp.bfloat16)
    d_act = right_dot(cot_both, down_weight)
    d_up = (d_act * silu_gate).astype(jnp.bfloat16)
    d_gate = (d_act * up_val * sigma * (1.0 + gate * (1.0 - sigma))).astype(jnp.bfloat16)

    bits = list(range(top, -1, -1))

    def spread(grad, names):
        return grad.astype(jnp.bfloat16).reshape([2] * len(names) + [-1, grad.shape[1]])

    turn = [lower[step % top :] + lower[: step % top] for step in range(3)]
    down_terms = exchange_sum(
        spread(left_dot(act, cot_both), bits[1:]), bits[1:], turn[2], coords, move
    )
    gate_terms = exchange_sum(
        spread(left_dot(norm_both, d_gate), bits), bits, turn[0] + [top], coords, move
    )
    up_terms = exchange_sum(
        spread(left_dot(norm_both, d_up), bits), bits, turn[1] + [top], coords, move
    )

    def finish_columns(terms):
        mine = total(terms)
        mine = mine.reshape(2, mine.shape[0] // 2, mine.shape[1])
        kept, other = take(mine, core, 0), partner(take(mine, 1 - core, 0))
        return ordered(
            jnp.concatenate([kept, other], axis=1), jnp.concatenate([other, kept], axis=1)
        )

    gate_out = finish_columns(gate_terms)
    up_out = finish_columns(up_terms)
    part = total(down_terms)
    pairs = [
        (place * 2 + side, (place ^ (1 << top)) * 2 + side)
        for place in range(chips)
        for side in range(2)
        if (place >> top) & 1 != side
    ]
    part = part + lax.ppermute(part.astype(jnp.bfloat16), AXES, pairs).astype(jnp.float32)
    part = part.reshape(2, part.shape[0] // 2, part.shape[1])
    down_out = jnp.where(
        coords[top] == core, take(part, core, 0), partner(take(part, 1 - core, 0))
    )

    d_norm_both = right_dot(d_gate, w_gate) + right_dot(d_up, w_up)
    d_norm_ffn = d_norm_both[:rows] + partner(d_norm_both[rows:])
    ffn_both = plain_dot(act, down_weight)
    block_out = (hidden_res + ffn_both[:rows] + partner(ffn_both[rows:])).astype(jnp.bfloat16)
    gain_two_grad = jnp.sum(d_norm_ffn * normed_two, axis=0)
    d_hidden = cotangent.astype(jnp.float32) + norm_back(
        d_norm_ffn, normed_two, scale_two, gain_two
    )
    d_branch = d_hidden.astype(jnp.bfloat16)
    out_grad = left_dot(gated, d_branch)
    d_gated = right_dot(d_branch, w_out)
    d_c = d_gated * conv
    d_conv = d_gated * c_part
    tap_terms = [
        jnp.sum(d_conv * mixed_in, axis=0),
        jnp.sum(keep_one * d_conv * back_one, axis=0),
        jnp.sum(keep_two * d_conv * back_two, axis=0),
    ]
    along_one = keep_one * d_conv * taps[:, 1]
    along_two = keep_two * d_conv * taps[:, 2]
    zero_row = jnp.zeros((1, width), jnp.float32)
    d_mixed = (
        taps[:, 0] * d_conv
        + jnp.concatenate([along_one[1:], zero_row], axis=0)
        + jnp.concatenate([along_two[2:], zero_row, zero_row], axis=0)
    )
    head_grad = jnp.concatenate([along_two[0:1], along_one[0:1] + along_two[1:2]], axis=0)
    returned = shifted(head_grad, AXES, -1)
    d_mixed = jnp.concatenate([d_mixed[:-2], d_mixed[-2:] + returned], axis=0)
    d_proj = jnp.concatenate([d_mixed * x_part, d_c, d_mixed * b_part], axis=1).astype(jnp.bfloat16)
    in_grad = left_dot(norm_in, d_proj)
    d_norm_in = right_dot(d_proj, w_in)
    gain_one_grad = jnp.sum(d_norm_in * normed_one, axis=0)
    input_grad = (d_hidden + norm_back(d_norm_in, normed_one, scale_one, gain_one)).astype(
        jnp.bfloat16
    )
    vectors = jnp.stack([gain_one_grad, gain_two_grad] + tap_terms, axis=0).T
    vectors = jnp.pad(vectors, ((0, 0), (0, 128 - vectors.shape[1])))
    joint = jnp.concatenate([in_grad, out_grad, vectors], axis=1)
    third = joint.shape[1] // 3
    names = bits + ["core"]
    joint_out = jnp.concatenate(
        [
            total(
                exchange_sum(
                    spread(joint[:, step * third : (step + 1) * third], names),
                    names,
                    ["core"] + turn[step] + [top],
                    coords,
                    move,
                )
            )
            for step in range(3)
        ],
        axis=1,
    )
    in_out = joint_out[:, : 3 * width]
    out_out = joint_out[:, 3 * width : 4 * width]
    vectors_out = joint_out[:, 4 * width :]
    return (
        block_out,
        input_grad,
        vectors_out[:, 0],
        in_out,
        vectors_out[:, 2:5],
        out_out,
        vectors_out[:, 1],
        gate_out,
        up_out,
        down_out,
    )


def solution(mesh):
    placed = (
        P(AXES, None),
        P(AXES, None),
        P(),
        P("wa"),
        P("wa", None),
        P("wa", None),
        P("wa", None),
        P("wa"),
        P("wa", None),
        P("wa", None),
        P("wa", None),
    )
    return jax.shard_map(
        local,
        mesh=mesh,
        in_specs=placed,
        out_specs=(
            P(AXES, None),
            P(AXES, None),
            P(AXES),
            P(AXES, None),
            P(AXES, None),
            P(AXES, None),
            P(AXES),
            P(AXES, None),
            P(AXES, None),
            P(AXES, None),
        ),
        check_vma=False,
    )
```

```python
import functools

import jax
import jax.numpy as jnp
from jax import lax
from jax.experimental import pallas as pl
from jax.experimental.pallas import tpu as pltpu
from jax.sharding import PartitionSpec as P

epsilon = 1e-05
AXES = ("seq", "wa")
HALO = 16
TILE = 256
NN = ((1,), (0,))
NT = ((1,), (1,))
TN = ((0,), (0,))


def shifted(value, steps):
    count = lax.axis_size(AXES)
    first, last = (max(0, -steps), min(count, count - steps))
    return lax.ppermute(value, AXES, [(source, source + steps) for source in range(first, last)])


def partner(value):
    return lax.ppermute(value, "wa", [(0, 1), (1, 0)])


def across(value, bit):
    count = lax.axis_size("seq")
    return lax.ppermute(value, "seq", [(place, place ^ (1 << bit)) for place in range(count)])


def dot(left, right, dims):
    return lax.dot_general(left, right, (dims, ((), ())), preferred_element_type=jnp.float32)


def norm_back(grad_norm, normed, scale, gain):
    inner = grad_norm * gain
    return scale * (inner - normed * jnp.mean(inner * normed, axis=-1, keepdims=True))


def take(value, index, axis):
    return lax.dynamic_index_in_dim(value, index, axis, keepdims=False)


def total(terms):
    result = terms[0].astype(jnp.float32)
    for term in terms[1:]:
        result = result + term.astype(jnp.float32)
    return result


def exchange_sum(terms, names, order, coords, move):
    names = list(names)
    for name in order:
        axis = names.index(name)
        mine = coords[name]
        send = total([take(term, 1 - mine, axis) for term in terms]).astype(jnp.bfloat16)
        terms = [take(term, mine, axis) for term in terms] + [move(send, name)]
        names.pop(axis)
    return terms


def ffn_kernel(
    real,
    pieces,
    info,
    n_ref,
    g_ref,
    gate_own,
    gate_other,
    up_own,
    up_other,
    down_ref,
    act_ref,
    gate_send,
    gate_keep,
    up_send,
    up_keep,
    back_ref,
    weights,
    grads,
):
    half = gate_own.shape[0]
    rows = n_ref.shape[0]
    tile = down_ref.shape[0]
    weights[:half, :tile] = gate_own[...]
    weights[half:, :tile] = gate_other[...]
    weights[:half, tile:] = up_own[...]
    weights[half:, tile:] = up_other[...]

    @pl.when(pl.program_id(0) == 0)
    def _():
        back_ref[...] = jnp.zeros(back_ref.shape, jnp.float32)

    size = -(-rows // pieces // 16) * 16
    for start in range(0, rows, size):
        part = pl.ds(start, min(size, rows - start))
        proj = dot(n_ref[part, :], weights[...], NN)
        d_act = dot(g_ref[part, :], down_ref[...], NT)
        gate = proj[:, :tile]
        up_val = proj[:, tile:]
        sigma = 0.5 * jnp.tanh(0.5 * gate) + 0.5
        silu = gate * sigma
        act_ref[part, :] = (silu * up_val).astype(jnp.bfloat16)
        grads[part, tile:] = (d_act * silu).astype(jnp.bfloat16)
        grads[part, :tile] = (d_act * up_val * (sigma + silu * (1.0 - sigma))).astype(jnp.bfloat16)
        back_ref[part, :] += dot(grads[part, :], weights[...], NT)
    summed = dot(n_ref[:real, :], grads[:real, :], TN).astype(jnp.bfloat16)
    outs = (
        (summed[:, :tile], gate_send, gate_keep, info[1]),
        (summed[:, tile:], up_send, up_keep, info[2]),
    )
    for grad, send, keep, mine in outs:
        groups, per, columns = send.shape
        both = grad.reshape(groups, 2, per, columns)
        for value in range(2):

            @pl.when(mine == value)
            def _():
                send[...] = both[:, 1 - value]
                keep[...] = both[:, value]


def ffn_part(info, n, g, gate_own, gate_other, up_own, up_other, down, first, count, real, pers):
    rows, width = n.shape
    half = width // 2
    blocks = down.shape[0] // TILE
    own = pl.BlockSpec((half, TILE), lambda j, info: (0, info[0] * blocks + first + j))
    other = pl.BlockSpec((half, TILE), lambda j, info: (0, first + j))
    whole = pl.BlockSpec((rows, width), lambda j, info: (0, 0))
    shapes = [jax.ShapeDtypeStruct((rows, count * TILE), jnp.bfloat16)]
    specs = [pl.BlockSpec((rows, TILE), lambda j, info: (0, j))]
    for per in pers:
        for _ in range(2):
            groups = width // (2 * per)
            shapes.append(jax.ShapeDtypeStruct((groups, per, count * TILE), jnp.bfloat16))
            specs.append(pl.BlockSpec((groups, per, TILE), lambda j, info: (0, 0, j)))
    shapes.append(jax.ShapeDtypeStruct((rows, width), jnp.float32))
    specs.append(whole)
    return pl.pallas_call(
        functools.partial(ffn_kernel, real, 2),
        out_shape=shapes,
        grid_spec=pltpu.PrefetchScalarGridSpec(
            num_scalar_prefetch=1,
            grid=(count,),
            in_specs=[
                whole,
                whole,
                own,
                other,
                own,
                other,
                pl.BlockSpec((TILE, width), lambda j, info: (first + j, 0)),
            ],
            out_specs=specs,
            scratch_shapes=[
                pltpu.VMEM((width, 2 * TILE), jnp.bfloat16),
                pltpu.VMEM((rows, 2 * TILE), jnp.bfloat16),
            ],
        ),
        compiler_params=pltpu.CompilerParams(vmem_limit_bytes=48 * 2**20),
        cost_estimate=pl.CostEstimate(
            flops=14 * rows * width * TILE * count,
            bytes_accessed=16 * rows * width + 14 * width * TILE * count,
            transcendentals=rows * TILE * count,
        ),
        name="ffn",
    )(info, n, g, gate_own, gate_other, up_own, up_other, down)


def local(
    tokens,
    cotangent,
    doc_lengths,
    norm_gain,
    in_weight,
    conv_taps,
    out_weight,
    ffn_gain,
    gate_weight,
    up_weight,
    down_weight,
):
    rows, width = tokens.shape
    half = width // 2
    hidden = down_weight.shape[0]
    chips = lax.axis_size("seq")
    top = chips.bit_length() - 2
    lower = list(range(top))
    bits = list(range(top, -1, -1))
    chip = lax.axis_index("seq")
    core = lax.axis_index("wa")
    coords = {bit: (chip >> bit) & 1 for bit in range(top + 1)}
    coords["core"] = core
    turned = dict(coords)
    turned[top] = coords[top] ^ core

    def move(value, name):
        return partner(value) if name == "core" else across(value, name)

    def ordered(low, high):
        return jnp.where(core == 0, low, high)

    def both(own, other, axis):
        return ordered(
            jnp.concatenate([own, other], axis=axis), jnp.concatenate([other, own], axis=axis)
        )

    def own_first(value):
        return ordered(value, jnp.concatenate([value[:, half:], value[:, :half]], axis=1))

    w_in_other = partner(in_weight)
    small = jnp.concatenate([norm_gain[:, None], ffn_gain[:, None], conv_taps], axis=1)
    small = both(small, partner(small), 0).astype(jnp.float32)
    gain_one, gain_two, taps = small[:, 0], small[:, 1], small[:, 2:]
    before_rows = shifted(tokens[rows - HALO :], 1)
    after_rows = shifted(jnp.concatenate([tokens[:HALO], cotangent[:HALO]], axis=1), -1)
    w_out_other = partner(out_weight)
    gate_other = partner(lax.dynamic_slice_in_dim(gate_weight, (1 - core) * hidden, hidden, 1))
    up_other = partner(lax.dynamic_slice_in_dim(up_weight, (1 - core) * hidden, hidden, 1))
    cot_other = partner(cotangent)

    place = lax.axis_index(AXES) * rows + jnp.arange(-HALO, rows + HALO, dtype=jnp.int32)
    starts = jnp.cumsum(doc_lengths) - doc_lengths
    first = jnp.any(place[:, None] == starts[None, :], axis=1)
    before = jnp.any((place - 1)[:, None] == starts[None, :], axis=1)
    keep_one = jnp.where(first, 0.0, 1.0).astype(jnp.float32)[HALO:, None]
    keep_two = jnp.where(jnp.logical_or(first, before), 0.0, 1.0).astype(jnp.float32)[HALO:, None]

    resid_all = jnp.concatenate([before_rows, tokens, after_rows[:, :width]], axis=0)
    resid_all = resid_all.astype(jnp.float32)
    scale_all = lax.rsqrt(jnp.mean(resid_all * resid_all, axis=-1, keepdims=True) + epsilon)
    norm_in_all = (resid_all * scale_all * gain_one).astype(jnp.bfloat16)
    turned_in = own_first(norm_in_all)
    proj = dot(turned_in[:, :half], in_weight, NN) + dot(turned_in[:, half:], w_in_other, NN)
    b_part = proj[HALO:, :width]
    c_part = proj[HALO:, width : 2 * width]
    x_part = proj[HALO:, 2 * width :]
    mixed_all = proj[:, :width] * proj[:, 2 * width :]
    mixed_in = mixed_all[HALO:]
    back_one = mixed_all[HALO - 1 : -1]
    back_two = mixed_all[HALO - 2 : -2]
    conv = (
        taps[:, 0] * mixed_in + keep_one * taps[:, 1] * back_one + keep_two * taps[:, 2] * back_two
    )
    gated = (c_part * conv).astype(jnp.bfloat16)
    turned_gated = own_first(gated)
    resid = resid_all[HALO:]
    hidden_res = (
        resid
        + dot(turned_gated[:, :half], out_weight, NN)
        + dot(turned_gated[:, half:], w_out_other, NN)
    )
    scale_two = lax.rsqrt(jnp.mean(hidden_res * hidden_res, axis=-1, keepdims=True) + epsilon)
    normed_two = hidden_res * scale_two
    norm_ffn = (normed_two * gain_two).astype(jnp.bfloat16)

    norm_other = partner(norm_ffn)
    norm_both = own_first(
        jnp.concatenate(
            [norm_ffn[:rows], norm_other[:rows], ordered(norm_other[rows:], norm_ffn[rows:])], axis=0
        )
    )
    cot_after = after_rows[:, width:]
    cot_after_other = partner(cot_after)
    cot_both = jnp.concatenate(
        [cotangent, cot_other, ordered(cot_after_other, cot_after)], axis=0
    )
    info = jnp.stack([core, coords[lower[0]], coords[lower[1]]]).astype(jnp.int32)
    per_chip = width // chips
    pers = (per_chip << lower[0], per_chip << lower[1])
    tiles = hidden // TILE
    split = tiles * 4 // 9
    acts, backs, gate_terms, up_terms = [], [], [], []
    turn = [lower[step % top :] + lower[: step % top] for step in range(3)]
    for start, count in ((0, split), (split, tiles - split)):
        act, gate_send, gate_keep, up_send, up_keep, back = ffn_part(
            info,
            norm_both,
            cot_both,
            gate_weight,
            gate_other,
            up_weight,
            up_other,
            down_weight,
            start,
            count,
            2 * rows,
            pers,
        )
        acts.append(act)
        backs.append(back)
        for terms, send, keep, order in (
            (gate_terms, gate_send, gate_keep, turn[0]),
            (up_terms, up_send, up_keep, turn[1]),
        ):
            names = [bit for bit in bits if bit != order[0]]
            shape = [2] * len(names) + [per_chip, count * TILE]
            halves = [keep.reshape(shape), across(send, order[0]).reshape(shape)]
            terms.append(exchange_sum(halves, names, order[1:], coords, move))

    joined = [
        jnp.concatenate([total(terms) for terms in parts], axis=2) for parts in (gate_terms, up_terms)
    ]
    joined = jnp.concatenate(joined, axis=2)
    mine = turned[top]
    far = across(take(joined, 1 - mine, 0).astype(jnp.bfloat16), top)
    columns = take(joined, mine, 0) + far.astype(jnp.float32)
    columns = columns.reshape(2, per_chip // 2, 2 * hidden)
    kept, other = take(columns, core, 0), partner(take(columns, 1 - core, 0))
    gate_out = both(kept[:, :hidden], other[:, :hidden], 1)
    up_out = both(kept[:, hidden:], other[:, hidden:], 1)

    act = jnp.concatenate(acts, axis=1)
    down_grad = dot(act[: 2 * rows], cot_both[: 2 * rows], TN).astype(jnp.bfloat16)
    down_grad = down_grad.reshape([2] * top + [-1, width])
    part = total(exchange_sum([down_grad], bits[1:], turn[2], coords, move))
    pairs = [
        (place * 2 + side, (place ^ (1 << top)) * 2 + side)
        for place in range(chips)
        for side in range(2)
        if (place >> top) & 1 != side
    ]
    part = part + lax.ppermute(part.astype(jnp.bfloat16), AXES, pairs).astype(jnp.float32)
    part = part.reshape(2, part.shape[0] // 2, width)
    down_out = jnp.where(
        coords[top] == core, take(part, core, 0), partner(take(part, 1 - core, 0))
    )

    back = backs[0] + backs[1]
    back_own, back_other, back_after = back[:rows], back[rows : 2 * rows], back[2 * rows :]
    sent = jnp.concatenate([back_other, ordered(back_after, back_own[:HALO])], axis=0)
    came = partner(sent)
    d_norm_ffn = jnp.concatenate(
        [back_own, ordered(back_other[:HALO], back_after)], axis=0
    )
    d_norm_ffn = own_first(d_norm_ffn + jnp.concatenate([came[:, half:], came[:, :half]], axis=1))
    ffn_both = dot(act[: 2 * rows], down_weight, NN)
    block_out = (hidden_res[:rows] + ffn_both[:rows] + partner(ffn_both[rows:])).astype(
        jnp.bfloat16
    )
    gain_two_grad = jnp.sum((d_norm_ffn * normed_two)[:rows], axis=0)
    cot_own = jnp.concatenate([cotangent, cot_after], axis=0).astype(jnp.float32)
    d_hidden = cot_own + norm_back(d_norm_ffn, normed_two, scale_two, gain_two)
    d_branch = d_hidden.astype(jnp.bfloat16)
    out_grad = dot(gated[:rows], d_branch[:rows], TN)
    d_gated = both(dot(d_branch, out_weight, NT), dot(d_branch, w_out_other, NT), 1)
    d_c = (d_gated * conv)[:rows]
    d_conv = d_gated * c_part
    tap_terms = [
        jnp.sum((d_conv * mixed_in)[:rows], axis=0),
        jnp.sum((keep_one * d_conv * back_one)[:rows], axis=0),
        jnp.sum((keep_two * d_conv * back_two)[:rows], axis=0),
    ]
    along_one = keep_one * d_conv * taps[:, 1]
    along_two = keep_two * d_conv * taps[:, 2]
    d_mixed = taps[:, 0] * d_conv[:rows] + along_one[1 : rows + 1] + along_two[2 : rows + 2]
    d_proj = jnp.concatenate(
        [d_mixed * x_part[:rows], d_c, d_mixed * b_part[:rows]], axis=1
    ).astype(jnp.bfloat16)
    in_grad = dot(norm_in_all[HALO : HALO + rows], d_proj, TN)
    d_norm_in = both(dot(d_proj, in_weight, NT), dot(d_proj, w_in_other, NT), 1)
    scale_one = scale_all[HALO : HALO + rows]
    normed_one = resid[:rows] * scale_one
    gain_one_grad = jnp.sum(d_norm_in * normed_one, axis=0)
    input_grad = (d_hidden[:rows] + norm_back(d_norm_in, normed_one, scale_one, gain_one)).astype(
        jnp.bfloat16
    )
    vectors = jnp.stack([gain_one_grad, gain_two_grad] + tap_terms, axis=0).T
    vectors = jnp.pad(vectors, ((0, 0), (0, 128 - vectors.shape[1])))
    joint = jnp.concatenate([in_grad, out_grad, vectors], axis=1).astype(jnp.bfloat16)
    cuts = (0, joint.shape[1] * 6 // 11, joint.shape[1])
    names = bits + ["core"]
    joint_parts = []
    for step in range(2):
        grad = joint[:, cuts[step] : cuts[step + 1]]
        grad = grad.reshape([2] * len(names) + [-1, grad.shape[1]])
        order = ["core"] + turn[step] + [top]
        joint_parts.append(total(exchange_sum([grad], names, order, coords, move)))
    joint_out = jnp.concatenate(joint_parts, axis=1)
    in_out = joint_out[:, : 3 * width]
    out_out = joint_out[:, 3 * width : 4 * width]
    vectors_out = joint_out[:, 4 * width :]
    return (
        block_out,
        input_grad,
        vectors_out[:, 0],
        in_out,
        vectors_out[:, 2:5],
        out_out,
        vectors_out[:, 1],
        gate_out,
        up_out,
        down_out,
    )


def solution(mesh):
    placed = (
        P(AXES, None),
        P(AXES, None),
        P(),
        P("wa"),
        P("wa", None),
        P("wa", None),
        P("wa", None),
        P("wa"),
        P("wa", None),
        P("wa", None),
        P("wa", None),
    )
    return jax.shard_map(
        local,
        mesh=mesh,
        in_specs=placed,
        out_specs=(
            P(AXES, None),
            P(AXES, None),
            P(AXES),
            P(AXES, None),
            P(AXES, None),
            P(AXES, None),
            P(AXES),
            P(AXES, None),
            P(AXES, None),
            P(AXES, None),
        ),
        check_vma=False,
    )
```

```python
import functools
import math

import jax
import jax.numpy as jnp
from jax import lax
from jax.experimental import pallas as pl
from jax.experimental.pallas import tpu as pltpu
from jax.sharding import PartitionSpec as P

epsilon = 1e-05
AXES = ("seq", "wa")
HALO = 16
TILE = 256
VMEM_LIMIT = 58 * 2**20
NN = ((1,), (0,))
NT = ((1,), (1,))
TN = ((0,), (0,))


def shifted(value, steps):
    count = lax.axis_size(AXES)
    first, last = (max(0, -steps), min(count, count - steps))
    return lax.ppermute(value, AXES, [(source, source + steps) for source in range(first, last)])


def partner(value):
    return lax.ppermute(value, "wa", [(0, 1), (1, 0)])


def across(value, bit):
    count = lax.axis_size("seq")
    return lax.ppermute(value, "seq", [(place, place ^ (1 << bit)) for place in range(count)])


def dot(left, right, dims):
    return lax.dot_general(left, right, (dims, ((), ())), preferred_element_type=jnp.float32)


def take(value, index, axis):
    return lax.dynamic_index_in_dim(value, index, axis, keepdims=False)


def total(terms):
    result = terms[0].astype(jnp.float32)
    for term in terms[1:]:
        result = result + term.astype(jnp.float32)
    return result


def chosen(test, value, other):
    return jnp.where(test, value, other)


def swapped(value):
    half = value.shape[1] // 2
    return jnp.concatenate([value[:, half:], value[:, :half]], axis=1)


def params(**extra):
    return dict(
        compiler_params=pltpu.CompilerParams(vmem_limit_bytes=VMEM_LIMIT),
        cost_estimate=pl.CostEstimate(flops=1000, bytes_accessed=1000, transcendentals=0),
        **extra,
    )


def conv_rows(mixed, keep_one, keep_two, taps, count):
    now = mixed[pl.ds(HALO, count), :]
    one = mixed[pl.ds(HALO - 1, count), :] * keep_one
    two = mixed[pl.ds(HALO - 2, count), :] * keep_two
    conv = taps[2:3, :] * now + taps[3:4, :] * one + taps[4:5, :] * two
    return now, one, two, conv


def join_rows(weights, own, other):
    half = own[0].shape[0]
    for index, (upper, lower) in enumerate(zip(own, other)):
        weights[:half, index * TILE : (index + 1) * TILE] = upper[...]
        weights[half:, index * TILE : (index + 1) * TILE] = lower[...]


def forward_kernel(
    info,
    tokens,
    before,
    after,
    small,
    taps,
    keeps,
    own_b,
    own_c,
    own_x,
    other_b,
    other_c,
    other_x,
    out_own,
    out_other,
    b_ref,
    c_ref,
    x_ref,
    hidden,
    norm_own,
    norm_send,
    normed,
    weights,
    mixed,
    gated,
    total_ref,
):
    step = pl.program_id(0)
    first_core = info[0] == 0
    rows, width = tokens.shape
    half = width // 2
    ext = rows + HALO

    @pl.when(step == 0)
    def _():
        for start, ref in ((0, before), (HALO, tokens), (HALO + rows, after)):
            resid = ref[:, :width].astype(jnp.float32)
            scale = lax.rsqrt(jnp.mean(resid * resid, axis=-1, keepdims=True) + epsilon)
            norm = resid * scale * small[0:1, :]
            place = pl.ds(start, ref.shape[0])
            normed[place, :half] = chosen(first_core, norm[:, :half], norm[:, half:]).astype(
                jnp.bfloat16
            )
            normed[place, half:] = chosen(first_core, norm[:, half:], norm[:, :half]).astype(
                jnp.bfloat16
            )
        total_ref[:rows, :] = tokens[...].astype(jnp.float32)
        total_ref[rows:, :] = after[:, :width].astype(jnp.float32)

    join_rows(weights, (own_b, own_c, own_x), (other_b, other_c, other_x))
    proj = dot(normed[...], weights[...], NN)
    b_part, c_part, x_part = proj[:, :TILE], proj[:, TILE : 2 * TILE], proj[:, 2 * TILE :]
    b_ref[...] = b_part
    c_ref[...] = c_part
    x_ref[...] = x_part
    mixed[...] = b_part * x_part
    conv = conv_rows(mixed, keeps[:, 0:1], keeps[:, 1:2], taps, ext)[3]
    gated[...] = (c_ref[pl.ds(HALO, ext), :] * conv).astype(jnp.bfloat16)
    here = pl.num_programs(0) // 2

    @pl.when(step < here)
    def _():
        total_ref[...] += dot(gated[...], out_own[...], NN)

    @pl.when(step >= here)
    def _():
        total_ref[...] += dot(gated[...], out_other[...], NN)

    @pl.when(step == pl.num_programs(0) - 1)
    def _():
        resid = total_ref[...]
        hidden[...] = resid
        scale = lax.rsqrt(jnp.mean(resid * resid, axis=-1, keepdims=True) + epsilon)
        norm = resid * scale * small[1:2, :]
        low = chosen(first_core, norm[:, :half], norm[:, half:]).astype(jnp.bfloat16)
        high = chosen(first_core, norm[:, half:], norm[:, :half]).astype(jnp.bfloat16)
        norm_own[:, :half] = low
        norm_own[:, half:] = high
        norm_send[:, :half] = high
        norm_send[:, half:] = low


def channel_specs(width):
    steps = width // TILE
    half = width // 2

    def at(j, info):
        return lax.rem(info[0] * (steps // 2) + j, steps)

    thirds = [
        pl.BlockSpec((half, TILE), lambda j, info, k=k: (0, k * steps + at(j, info)))
        for k in range(3)
    ]
    out_own = pl.BlockSpec((TILE, width), lambda j, info: (jnp.minimum(j, steps // 2 - 1), 0))
    out_other = pl.BlockSpec((TILE, width), lambda j, info: (jnp.maximum(j - steps // 2, 0), 0))
    return steps, at, thirds * 2 + [out_own, out_other]


def fixed(*shape):
    return pl.BlockSpec(shape, lambda j, info: (0,) * len(shape))


def conv_forward(info, tokens, before, after, small, keeps, w_in, w_in_other, w_out, w_out_other):
    rows, width = tokens.shape
    ext = rows + HALO
    steps, at, weight_specs = channel_specs(width)
    column = pl.BlockSpec((ext + HALO, TILE), lambda j, info: (0, at(j, info)))
    return pl.pallas_call(
        forward_kernel,
        out_shape=[jax.ShapeDtypeStruct((ext + HALO, width), jnp.float32)] * 3
        + [jax.ShapeDtypeStruct((ext, width), jnp.float32)]
        + [jax.ShapeDtypeStruct((ext, width), jnp.bfloat16)] * 2,
        grid_spec=pltpu.PrefetchScalarGridSpec(
            num_scalar_prefetch=1,
            grid=(steps,),
            in_specs=[
                fixed(rows, width),
                fixed(HALO, width),
                fixed(*after.shape),
                fixed(*small.shape),
                pl.BlockSpec((small.shape[0], TILE), lambda j, info: (0, at(j, info))),
                fixed(*keeps.shape),
            ]
            + weight_specs,
            out_specs=[column] * 3 + [fixed(ext, width)] * 3,
            scratch_shapes=[
                pltpu.VMEM((ext + HALO, width), jnp.bfloat16),
                pltpu.VMEM((width, 3 * TILE), jnp.bfloat16),
                pltpu.VMEM((ext + HALO, TILE), jnp.float32),
                pltpu.VMEM((ext, TILE), jnp.bfloat16),
                pltpu.VMEM((ext, width), jnp.float32),
            ],
        ),
        name="conv_forward",
        **params(),
    )(
        info,
        tokens,
        before,
        after,
        small,
        small,
        keeps,
        *[w_in] * 3,
        *[w_in_other] * 3,
        w_out,
        w_out_other,
    )


def backward_kernel(
    info,
    tokens,
    hidden,
    cotangent,
    back,
    came,
    small,
    taps,
    keeps,
    b_ref,
    c_ref,
    x_ref,
    own_b,
    own_c,
    own_x,
    other_b,
    other_c,
    other_x,
    out_own,
    out_other,
    input_grad,
    send,
    b_keep,
    out_keep,
    c_keep,
    x_keep,
    vector_keep,
    vectors,
    d_hidden,
    d_branch,
    norm_in,
    d_norm_in,
    weights,
    mixed,
    d_gated,
    along_one,
    along_two,
    d_proj,
):
    step = pl.program_id(0)
    core = info[0]
    first_core = core == 0
    rows, width = tokens.shape
    half = width // 2
    ext = rows + HALO

    def token_norm():
        resid = tokens[...].astype(jnp.float32)
        scale = lax.rsqrt(jnp.mean(resid * resid, axis=-1, keepdims=True) + epsilon)
        return resid * scale, scale

    def back_through(grad, normed, scale, gain):
        inner = grad * gain
        return scale * (inner - normed * jnp.mean(inner * normed, axis=-1, keepdims=True))

    def in_order(own, other):
        return jnp.concatenate(
            [chosen(first_core, own, other), chosen(first_core, other, own)], axis=1
        )

    @pl.when(step == 0)
    def _():
        vectors[...] = jnp.zeros(vectors.shape, jnp.float32)
        grad = in_order(back[:, :half] + came[:, half:], back[:, half:] + came[:, :half])
        resid = hidden[...]
        scale = lax.rsqrt(jnp.mean(resid * resid, axis=-1, keepdims=True) + epsilon)
        normed = resid * scale
        vectors[1:2, :] = jnp.sum(grad[:rows] * normed[:rows], axis=0, keepdims=True)
        result = cotangent[...].astype(jnp.float32) + back_through(
            grad, normed, scale, small[1:2, :]
        )
        d_hidden[...] = result
        d_branch[...] = result.astype(jnp.bfloat16)
        norm_in[...] = (token_norm()[0] * small[0:1, :]).astype(jnp.bfloat16)
        d_norm_in[...] = jnp.zeros(d_norm_in.shape, jnp.float32)

    here = pl.num_programs(0) // 2

    @pl.when(step < here)
    def _():
        d_gated[...] = dot(d_branch[...], out_own[...], NT)

    @pl.when(step >= here)
    def _():
        d_gated[...] = dot(d_branch[...], out_other[...], NT)

    join_rows(weights, (own_b, own_c, own_x), (other_b, other_c, other_x))
    mixed[...] = b_ref[...] * x_ref[...]
    now, one, two, conv = conv_rows(mixed, keeps[:, 0:1], keeps[:, 1:2], taps, ext)
    c_part = c_ref[pl.ds(HALO, ext), :]
    grad = d_gated[...]
    gated = (c_part[:rows] * conv[:rows]).astype(jnp.bfloat16)
    d_conv = grad * c_part
    block = lax.rem(core * here + step, pl.num_programs(0))
    lanes = pl.ds(pl.multiple_of(block * TILE, TILE), TILE)
    for index, view in enumerate((now, one, two)):
        vectors[2 + index : 3 + index, lanes] = jnp.sum(
            d_conv[:rows] * view[:rows], axis=0, keepdims=True
        )
    along_one[...] = keeps[:, 0:1] * d_conv * taps[3:4, :]
    along_two[...] = keeps[:, 1:2] * d_conv * taps[4:5, :]
    d_mixed = (
        taps[2:3, :] * d_conv[:rows] + along_one[pl.ds(1, rows), :] + along_two[pl.ds(2, rows), :]
    )
    d_proj[:, :TILE] = (d_mixed * x_ref[pl.ds(HALO, rows), :]).astype(jnp.bfloat16)
    d_proj[:, TILE : 2 * TILE] = (grad[:rows] * conv[:rows]).astype(jnp.bfloat16)
    d_proj[:, 2 * TILE :] = (d_mixed * b_ref[pl.ds(HALO, rows), :]).astype(jnp.bfloat16)
    out_grad = dot(gated, d_branch[:rows, :], TN)
    in_grad = dot(norm_in[...], d_proj[...], TN)
    d_norm_in[...] += dot(d_proj[...], weights[...], NT)
    groups, per, _ = send.shape
    few = groups // pl.num_programs(0)

    def divide(value, keep, group, at):
        pair = value.reshape(value.shape[0] // (2 * per), 2, per, value.shape[1]).astype(send.dtype)
        for side in range(2):

            @pl.when(core == side)
            def _():
                send[group, :, at] = pair[:, 1 - side]
                keep[...] = pair[:, side]

    every = slice(None)
    for index, keep in enumerate((b_keep, None, c_keep, x_keep)):
        if keep is None:
            divide(out_grad, out_keep, pl.ds(block * few, few), pl.ds(width, width))
        else:
            third = index and index - 1
            at = pl.multiple_of(index * width + block * TILE, TILE)
            divide(in_grad[:, third * TILE : (third + 1) * TILE], keep, every, pl.ds(at, TILE))

    @pl.when(step == pl.num_programs(0) - 1)
    def _():
        final = in_order(d_norm_in[:, :half], d_norm_in[:, half:])
        normed, scale = token_norm()
        vectors[0:1, :] = jnp.sum(final * normed, axis=0, keepdims=True)
        input_grad[...] = (
            d_hidden[:rows, :] + back_through(final, normed, scale, small[0:1, :])
        ).astype(jnp.bfloat16)
        divide(vectors[...].T, vector_keep, every, pl.ds(4 * width, vectors.shape[0]))


def conv_backward(
    info,
    tokens,
    hidden,
    cotangent,
    back,
    came,
    small,
    keeps,
    parts,
    w_in,
    w_in_other,
    w_out,
    w_out_other,
    devices,
):
    rows, width = tokens.shape
    ext = rows + HALO
    steps, at, weight_specs = channel_specs(width)
    column = pl.BlockSpec((ext + HALO, TILE), lambda j, info: (0, at(j, info)))
    per = width // devices
    kind = jnp.bfloat16 if per % 16 == 0 else jnp.float32
    groups = devices // 2
    by_columns = pl.BlockSpec((groups, per, TILE), lambda j, info: (0, 0, at(j, info)))
    by_rows = pl.BlockSpec((groups // steps, per, width), lambda j, info: (at(j, info), 0, 0))
    return pl.pallas_call(
        backward_kernel,
        out_shape=[
            jax.ShapeDtypeStruct((rows, width), jnp.bfloat16),
            jax.ShapeDtypeStruct((groups, per, 4 * width + 128), kind),
        ]
        + [jax.ShapeDtypeStruct((groups, per, width), kind)] * 4
        + [jax.ShapeDtypeStruct((groups, per, 128), kind)],
        grid_spec=pltpu.PrefetchScalarGridSpec(
            num_scalar_prefetch=1,
            grid=(steps,),
            in_specs=[
                fixed(rows, width),
                fixed(ext, width),
                fixed(ext, width),
                fixed(ext, width),
                fixed(ext, width),
                fixed(*small.shape),
                pl.BlockSpec((small.shape[0], TILE), lambda j, info: (0, at(j, info))),
                fixed(*keeps.shape),
            ]
            + [column] * 3
            + weight_specs,
            out_specs=[
                fixed(rows, width),
                fixed(groups, per, 4 * width + 128),
                by_columns,
                by_rows,
                by_columns,
                by_columns,
                fixed(groups, per, 128),
            ],
            scratch_shapes=[
                pltpu.VMEM((128, width), jnp.float32),
                pltpu.VMEM((ext, width), jnp.float32),
                pltpu.VMEM((ext, width), jnp.bfloat16),
                pltpu.VMEM((rows, width), jnp.bfloat16),
                pltpu.VMEM((rows, width), jnp.float32),
                pltpu.VMEM((width, 3 * TILE), jnp.bfloat16),
                pltpu.VMEM((ext + HALO, TILE), jnp.float32),
                pltpu.VMEM((ext, TILE), jnp.float32),
                pltpu.VMEM((ext, TILE), jnp.float32),
                pltpu.VMEM((ext, TILE), jnp.float32),
                pltpu.VMEM((rows, 3 * TILE), jnp.bfloat16),
            ],
        ),
        name="conv_backward",
        **params(),
    )(
        info,
        tokens,
        hidden,
        cotangent,
        back,
        came,
        small,
        small,
        keeps,
        *parts,
        *[w_in] * 3,
        *[w_in_other] * 3,
        w_out,
        w_out_other,
    )


def ffn_kernel(
    real,
    pieces,
    chained,
    joined,
    info,
    n_own,
    n_other,
    g_own,
    g_other,
    gate_own,
    gate_other,
    up_own,
    up_other,
    down_ref,
    *refs,
):
    before, refs = (refs[:2], refs[2:]) if chained else ((), refs)
    act_ref, back_keep, back_send = refs[:3]
    results, (n_all, g_all, back, weights, grads) = refs[3:-5], refs[-5:]
    rows = n_all.shape[0]
    block = real // 2
    tile = down_ref.shape[0]
    places = (
        (pl.ds(0, block), 0, pl.ds(0, block)),
        (pl.ds(real, HALO), 0, pl.ds(block, HALO)),
        (pl.ds(block, block), 1, pl.ds(0, block)),
        (pl.ds(real + HALO, HALO), 1, pl.ds(block, HALO)),
    )

    @pl.when(pl.program_id(0) == 0)
    def _():
        for place, which, source in places:
            n_all[place, :] = (n_own, n_other)[which][source, :]
            g_all[place, :] = (g_own, g_other)[which][source, :]
            if chained:
                back[place, :] = before[which][source, :]
            else:
                back[place, :] = jnp.zeros((place.size, back.shape[1]), jnp.float32)

    join_rows(weights, (gate_own, up_own), (gate_other, up_other))
    size = -(-rows // pieces // 16) * 16
    for start in range(0, rows, size):
        part = pl.ds(start, min(size, rows - start))
        proj = dot(n_all[part, :], weights[...], NN)
        d_act = dot(g_all[part, :], down_ref[...], NT)
        gate = proj[:, :tile]
        up_val = proj[:, tile:]
        sigma = 0.5 * jnp.tanh(0.5 * gate) + 0.5
        silu = gate * sigma
        act_ref[part, :] = (silu * up_val).astype(jnp.bfloat16)
        grads[part, tile:] = (d_act * silu).astype(jnp.bfloat16)
        grads[part, :tile] = (d_act * up_val * (sigma + silu * (1.0 - sigma))).astype(jnp.bfloat16)
        back[part, :] += dot(grads[part, :], weights[...], NT)
    summed = dot(n_all[:real, :], grads[:real, :], TN).astype(jnp.bfloat16)
    if joined:
        (out,) = results
        half = summed.shape[0] // 2

        @pl.when(info[0] == 0)
        def _():
            out[...] = summed

        @pl.when(info[0] != 0)
        def _():
            out[:half, :] = summed[half:, :]
            out[half:, :] = summed[:half, :]

    else:
        for index, grad in enumerate((summed[:, :tile], summed[:, tile:])):
            send, keep = results[2 * index : 2 * index + 2]
            groups, per, columns = send.shape
            pair = grad.reshape(groups, 2, per, columns)
            for value in range(2):

                @pl.when(info[1 + index] == value)
                def _():
                    send[...] = pair[:, 1 - value]
                    keep[...] = pair[:, value]

    @pl.when(pl.program_id(0) == pl.num_programs(0) - 1)
    def _():
        for place, which, source in places:
            (back_keep, back_send)[which][source, :] = back[place, :]


def ffn_part(info, acts, weights, down, before, first, count, pers):
    ext, width = acts[0].shape
    rows, real = 2 * ext, 2 * (ext - HALO)
    half = width // 2
    blocks = down.shape[0] // TILE
    own = pl.BlockSpec((half, TILE), lambda j, info: (0, info[0] * blocks + first + j))
    other = pl.BlockSpec((half, TILE), lambda j, info: (0, first + j))
    shapes = [jax.ShapeDtypeStruct((rows, count * TILE), jnp.bfloat16)]
    specs = [pl.BlockSpec((rows, TILE), lambda j, info: (0, j))]
    for _ in range(2):
        shapes.append(jax.ShapeDtypeStruct((ext, width), jnp.float32))
        specs.append(fixed(ext, width))
    for per in pers:
        for _ in range(2):
            groups = width // (2 * per)
            shapes.append(jax.ShapeDtypeStruct((groups, per, count * TILE), jnp.bfloat16))
            specs.append(pl.BlockSpec((groups, per, TILE), lambda j, info: (0, 0, j)))
    if not pers:
        shapes.append(jax.ShapeDtypeStruct((width, 2 * count * TILE), jnp.bfloat16))
        specs.append(pl.BlockSpec((width, 2 * TILE), lambda j, info: (0, j)))
    return pl.pallas_call(
        functools.partial(ffn_kernel, real, 2, bool(before), not pers),
        out_shape=shapes,
        grid_spec=pltpu.PrefetchScalarGridSpec(
            num_scalar_prefetch=1,
            grid=(count,),
            in_specs=[fixed(ext, width)] * 4
            + [own, other, own, other]
            + [pl.BlockSpec((TILE, width), lambda j, info: (first + j, 0))]
            + [fixed(ext, width)] * len(before),
            out_specs=specs,
            scratch_shapes=[
                pltpu.VMEM((rows, width), jnp.bfloat16),
                pltpu.VMEM((rows, width), jnp.bfloat16),
                pltpu.VMEM((rows, width), jnp.float32),
                pltpu.VMEM((width, 2 * TILE), jnp.bfloat16),
                pltpu.VMEM((rows, 2 * TILE), jnp.bfloat16),
            ],
        ),
        name="ffn",
        **params(),
    )(info, *acts, *weights, down, *before)


def down_kernel(
    info,
    act_one,
    act_two,
    g_own,
    g_other,
    down_ref,
    out_keep,
    out_send,
    low_send,
    low_keep,
    high_send,
    high_keep,
    rhs,
    grad,
):
    step = pl.program_id(0)
    block = out_keep.shape[0]
    real = 2 * block
    cut = act_one.shape[1]
    rhs[:block, :] = g_own[:block, :]
    rhs[block:, :] = g_other[:block, :]
    result = dot(act_one[:real, :], down_ref[:cut, :], NN) + dot(
        act_two[:real, :], down_ref[cut:, :], NN
    )
    out_keep[...] = result[:block]
    out_send[...] = result[block:]
    grad[:cut, :] = dot(act_one[:real, :], rhs[...], TN).astype(grad.dtype)
    grad[cut:, :] = dot(act_two[:real, :], rhs[...], TN).astype(grad.dtype)
    here = pl.num_programs(0) // 2
    outs = ((step < here, low_send, low_keep, info[1]), (step >= here, high_send, high_keep, info[2]))
    for now, send, keep, mine in outs:
        groups, per, _ = send.shape
        for value in range(2):

            @pl.when(jnp.logical_and(now, mine == value))
            def _():
                for group in range(groups):
                    start = 2 * group * per
                    send[group] = grad[pl.ds(start + (1 - value) * per, per), :]
                    keep[group] = grad[pl.ds(start + value * per, per), :]


def down_part(info, act_one, act_two, g_own, g_other, down, pers, block):
    hidden, width = down.shape
    steps = width // TILE
    here = steps // 2
    kind = jnp.bfloat16 if min(pers) % 16 == 0 else jnp.float32
    tile = pl.BlockSpec((block, TILE), lambda j, info: (0, j))
    shapes = [jax.ShapeDtypeStruct((block, width), jnp.float32)] * 2
    specs = [tile] * 2
    for index, per in enumerate(pers):
        groups = hidden // (2 * per)
        for _ in range(2):
            shapes.append(jax.ShapeDtypeStruct((groups, per, width // 2), kind))
            if index == 0:
                specs.append(
                    pl.BlockSpec(
                        (groups, per, TILE), lambda j, info: (0, 0, jnp.minimum(j, here - 1))
                    )
                )
            else:
                specs.append(
                    pl.BlockSpec((groups, per, TILE), lambda j, info: (0, 0, jnp.maximum(j - here, 0)))
                )
    ext = g_own.shape[0]
    return pl.pallas_call(
        down_kernel,
        out_shape=shapes,
        grid_spec=pltpu.PrefetchScalarGridSpec(
            num_scalar_prefetch=1,
            grid=(steps,),
            in_specs=[
                fixed(*act_one.shape),
                fixed(*act_two.shape),
                pl.BlockSpec((ext, TILE), lambda j, info: (0, j)),
                pl.BlockSpec((ext, TILE), lambda j, info: (0, j)),
                pl.BlockSpec((hidden, TILE), lambda j, info: (0, j)),
            ],
            out_specs=specs,
            scratch_shapes=[
                pltpu.VMEM((2 * block, TILE), jnp.bfloat16),
                pltpu.VMEM((hidden, TILE), kind),
            ],
        ),
        name="down",
        **params(),
    )(info, act_one, act_two, g_own, g_other, down)


def combine_kernel(plan, info, *refs):
    refs = list(refs)
    inputs = [[[refs.pop(0) for _ in range(count)] for count in counts] for counts in plan]
    for members, out in zip(inputs, refs):
        edge = 0
        for terms in members:
            size = terms[0].shape[-1]
            value = terms[0][...].astype(jnp.float32)
            for term in terms[1:]:
                value = value + term[...].astype(jnp.float32)
            out[..., edge : edge + size] = value.reshape(out.shape[:-1] + (size,)).astype(out.dtype)
            edge += size


def combine(info, slots, jobs, flip=False):
    plan, arrays, specs, shapes, out_specs = [], [], [], [], []
    lefts = []
    for bit, members in jobs:
        common = members[0][0][1]
        for terms in members:
            for _, names, _, _ in terms:
                common = [name for name in common if name in names]
        lefts.append([name for name in common if name != bit])
    gridded = all(lefts)
    for (bit, members), left in zip(jobs, lefts):
        for terms in members:
            for array, names, block, size in terms:
                rows = array.size // array.shape[-1] >> len(names)
                arrays.append(array.reshape([2] * len(names) + [rows, array.shape[-1]]))
                shape, picks = [], []
                for name in names:
                    if name == bit:
                        shape.append(None)
                        picks.append(("other", slots[name]))
                    elif name not in left:
                        shape.append(None)
                        picks.append(("mine", slots[name]))
                    elif gridded and name == left[0]:
                        shape.append(None)
                        picks.append(("step", 0))
                    else:
                        shape.append(2)
                        picks.append(("all", 0))

                def index_map(j, info, picks=picks, block=block):
                    where = []
                    for kind, slot in picks:
                        if kind == "all":
                            where.append(0)
                        elif kind == "step":
                            where.append(lax.rem(j + info[0], 2) if flip else j)
                        else:
                            where.append(info[slot] if kind == "mine" else 1 - info[slot])
                    return (*where, 0, block)

                specs.append(pl.BlockSpec((*shape, rows, size), index_map))
        width = sum(terms[0][3] for terms in members)
        kind = jnp.bfloat16 if rows % 16 == 0 else jnp.float32
        outer = 1 << len(left)
        shapes.append(jax.ShapeDtypeStruct((outer, rows, width), kind))
        inner = outer // 2 if gridded else outer
        out_specs.append(pl.BlockSpec((inner, rows, width), lambda j, info: (j, 0, 0)))
        plan.append([len(terms) for terms in members])
    results = pl.pallas_call(
        functools.partial(combine_kernel, plan),
        out_shape=shapes,
        grid_spec=pltpu.PrefetchScalarGridSpec(
            num_scalar_prefetch=1,
            grid=(2 if gridded else 1,),
            in_specs=specs,
            out_specs=out_specs,
        ),
        name="combine",
        **params(),
    )(info, *arrays)
    return list(zip(results, lefts))


def finish_kernel(counts, tiles, info, *refs):
    *inputs, mine, send, scratch = refs
    place = 0
    for count in counts:
        value = inputs[0][...].astype(jnp.float32)
        for term in inputs[1:count]:
            value = value + term[...].astype(jnp.float32)
        inputs = inputs[count:]
        for tile in range(value.shape[1] // TILE):
            start = tiles[place] * TILE
            scratch[:, start : start + TILE] = value[:, tile * TILE : (tile + 1) * TILE]
            place += 1
    rows = mine.shape[0]
    for side, out in ((info[0], mine), (1 - info[0], send)):
        out[...] = scratch[pl.ds(pl.multiple_of(side * rows, rows), rows), :]


def picked(slots, terms):
    arrays, specs = [], []
    for array, names, block, size in terms:
        rows = array.size // array.shape[-1] >> len(names)
        arrays.append(array.reshape([2] * len(names) + [rows, array.shape[-1]]))
        specs.append(
            pl.BlockSpec(
                (*[None] * len(names), rows, size),
                lambda j, info, names=names, block=block: (
                    *[info[slots[name]] for name in names],
                    0,
                    block,
                ),
            )
        )
    return arrays, specs


def settle_kernel(plan, info, *refs):
    refs = list(refs)
    inputs = [[[refs.pop(0) for _ in range(count)] for count in counts] for counts, _ in plan]
    for members, (_, kinds) in zip(inputs, plan):
        outs = [refs.pop(0) for _ in kinds]
        edge = 0
        for terms in members:
            size = terms[0].shape[-1]
            value = terms[0][...].astype(jnp.float32)
            for term in terms[1:]:
                value = value + term[...].astype(jnp.float32)
            for out in outs:
                out[:, edge : edge + size] = value.astype(out.dtype)
            edge += size


def settle(info, slots, groups):
    arrays, specs, shapes, plan = [], [], [], []
    for members, kinds in groups:
        for terms in members:
            views, view_specs = picked(slots, terms)
            arrays += views
            specs += view_specs
        rows = views[0].shape[-2]
        width = sum(terms[0][3] for terms in members)
        shapes += [jax.ShapeDtypeStruct((rows, width), kind) for kind in kinds]
        plan.append(([len(terms) for terms in members], kinds))
    return pl.pallas_call(
        functools.partial(settle_kernel, plan),
        out_shape=shapes,
        grid_spec=pltpu.PrefetchScalarGridSpec(
            num_scalar_prefetch=1,
            grid=(1,),
            in_specs=specs,
            out_specs=[fixed(*shape.shape) for shape in shapes],
        ),
        name="settle",
        **params(),
    )(info, *arrays)


def finish(info, slots, members, tiles):
    columns = len(tiles) * TILE
    arrays, specs = [], []
    for terms in members:
        views, view_specs = picked(slots, terms)
        rows = views[0].shape[-2]
        arrays += views
        specs += view_specs
    return pl.pallas_call(
        functools.partial(finish_kernel, [len(terms) for terms in members], tiles),
        out_shape=[jax.ShapeDtypeStruct((rows // 2, columns), jnp.float32)] * 2,
        grid_spec=pltpu.PrefetchScalarGridSpec(
            num_scalar_prefetch=1,
            grid=(1,),
            in_specs=specs,
            out_specs=[fixed(rows // 2, columns)] * 2,
            scratch_shapes=[pltpu.VMEM((rows, columns), jnp.float32)],
        ),
        name="finish",
        **params(),
    )(info, *arrays)


def local(
    tokens,
    cotangent,
    doc_lengths,
    norm_gain,
    in_weight,
    conv_taps,
    out_weight,
    ffn_gain,
    gate_weight,
    up_weight,
    down_weight,
):
    rows, width = tokens.shape
    hidden = down_weight.shape[0]
    chips = lax.axis_size("seq")
    top = chips.bit_length() - 2
    lower = list(range(top))
    bits = list(range(top, -1, -1))
    chip = lax.axis_index("seq")
    core = lax.axis_index("wa")
    coords = {bit: (chip >> bit) & 1 for bit in range(top + 1)}
    turned = dict(coords)
    turned[top] = coords[top] ^ core
    ordering = lax.optimization_barrier

    def after(value, *gates):
        return ordering((value, gates))[0]

    def ordered(low, high):
        return jnp.where(core == 0, low, high)

    def both(own, other, axis):
        return ordered(
            jnp.concatenate([own, other], axis=axis), jnp.concatenate([other, own], axis=axis)
        )

    w_in_other = partner(in_weight)
    small = jnp.concatenate([norm_gain[None], ffn_gain[None], conv_taps.T], axis=0)
    small = jnp.pad(small, ((0, 3), (0, 0)))
    small = both(small, partner(small), 1).astype(jnp.float32)
    before_rows = shifted(tokens[rows - HALO :], 1)
    after_rows = shifted(jnp.concatenate([tokens[:HALO], cotangent[:HALO]], axis=1), -1)
    w_out_other = partner(out_weight)
    gate_late, up_late = after((gate_weight, up_weight), before_rows, after_rows, w_out_other)
    gate_other = partner(lax.dynamic_slice_in_dim(gate_late, (1 - core) * hidden, hidden, 1))
    up_other = partner(lax.dynamic_slice_in_dim(up_late, (1 - core) * hidden, hidden, 1))
    cot_own = jnp.concatenate([cotangent, after_rows[:, width:]], axis=0)
    cot_other = partner(cot_own)

    place = lax.axis_index(AXES) * rows + jnp.arange(rows + HALO, dtype=jnp.int32)
    starts = jnp.cumsum(doc_lengths) - doc_lengths
    first = jnp.any(place[:, None] == starts[None, :], axis=1)
    before = jnp.any((place - 1)[:, None] == starts[None, :], axis=1)
    keep_one = jnp.where(first, 0.0, 1.0)
    keep_two = jnp.where(jnp.logical_or(first, before), 0.0, 1.0)
    keeps = jnp.stack([keep_one, keep_two], axis=1).astype(jnp.float32)
    info = [core] + [coords[bit] for bit in lower] + [coords[top], turned[top]]
    info = jnp.stack(info).astype(jnp.int32)

    *parts, hidden_res, norm_own, norm_send = conv_forward(
        info,
        tokens,
        before_rows,
        after_rows,
        small,
        keeps,
        in_weight,
        w_in_other,
        out_weight,
        w_out_other,
    )
    norm_other = partner(norm_send)
    per_chip = width // chips
    pers = (per_chip << lower[0], per_chip << lower[1])
    tiles = hidden // TILE
    split = tiles * 5 // 9
    counts = (split, tiles - split)
    orders = (lower, [lower[1], lower[0]] + lower[2:])

    acts = (norm_own, norm_other, cot_own, cot_other)
    weights = (gate_weight, gate_other, up_weight, up_other)
    one = ffn_part(info, acts, weights, down_weight, (), 0, counts[0], pers)
    one_x = across(one[3], orders[0][0])
    one_y = across(one[5], orders[1][0])
    two = ffn_part(info, acts, weights, down_weight, one[1:3], split, counts[1], ())
    two, one_x, one_y = ordering((two, one_x, one_y))
    came = partner(two[2])

    groups = [
        [low + (level << (top - 1)) for level in range(4)] for low in range(1 << (top - 1))
    ]
    quarter = lax.psum_scatter(
        two[3], "seq", scatter_dimension=0, axis_index_groups=groups, tiled=True
    )

    slots = {bit: 1 + bit for bit in bits}
    turned_slots = dict(slots)
    turned_slots[top] = 2 + top

    def plain(array, names):
        return (array, names, 0, array.shape[-1])

    def gated(streams, *gates):
        held = after([terms[-1][0] for terms in streams], gates)
        return [
            terms[:-1] + [(array, *terms[-1][1:])] for terms, array in zip(streams, held)
        ]

    def without(names, *taken):
        return [name for name in names if name not in taken]

    def send_on(streams, names, use=slots):
        results = combine(info, use, streams)
        return [send for send, _ in results], [
            (across(send, bit), left) for (bit, _), (send, left) in zip(streams, results)
        ]

    def upper_sum(value):
        value = value.reshape(-1, value.shape[-1])
        return lax.psum_scatter(
            value, "seq", scatter_dimension=0, axis_index_groups=groups, tiled=True
        )

    one_terms = [
        [plain(keep, without(bits, order[0])), plain(got, without(bits, order[0]))]
        for keep, got, order in ((one[4], one_x, orders[0]), (one[6], one_y, orders[1]))
    ]
    one_sent, one_got = send_on(
        [(order[1], [terms]) for terms, order in zip(one_terms, orders)], bits, turned_slots
    )
    down_pers = [2 * hidden // chips << bit for bit in (lower[0], lower[1])]
    out_keep, out_send, *down_halves = down_part(
        info, one[0], after(two[0], one_sent), cot_own, cot_other, down_weight, down_pers, rows
    )
    one_got = [got for got, _ in one_got]
    came, one_got, out_send, down_halves = ordering((came, one_got, out_send, down_halves))

    down_x = across(down_halves[0], orders[0][0])
    down_y = across(down_halves[2], orders[1][0])
    out_came = partner(out_send)

    def side_by_side(streams, order, use=slots):
        sent = None
        for bit in order:
            sent, ((got, left),) = send_on([(bit, streams)], None, use)
            edge, members = 0, []
            for terms in streams:
                size = terms[0][3]
                members.append(terms + [(got, left, edge, size)])
                edge += size
            for terms in members:
                array, left, edge, size = terms[-1]
                if edge % size:
                    array, edge = array[..., edge : edge + size], 0
                terms[-1] = (array, left, edge // size, size)
            streams = members
        return sent, streams

    one_streams = [
        terms + [plain(got, without(bits, *order[:2]))]
        for terms, got, order in zip(one_terms, one_got, orders)
    ]
    _, one_streams = side_by_side(one_streams, lower[2 : top - 1], turned_slots)
    ((one_all, _),) = combine(info, turned_slots, [(None, one_streams)], flip=True)
    came, one_all = ordering((came, one_all))
    one_done = upper_sum(one_all)
    input_grad, conv_send, *conv_keeps = conv_backward(
        info,
        tokens,
        hidden_res,
        cot_own,
        two[1],
        came,
        small,
        keeps,
        parts,
        in_weight,
        w_in_other,
        out_weight,
        w_out_other,
        2 * chips,
    )
    conv_send, conv_keeps, down_x, down_y = ordering((conv_send, conv_keeps, down_x, down_y))

    conv_came = partner(conv_send)
    down_bits = bits[1:]
    down_terms = [
        [plain(keep, without(down_bits, order[0])), plain(got, without(down_bits, order[0]))]
        for keep, got, order in (
            (down_halves[1], down_x, orders[0]),
            (down_halves[3], down_y, orders[1]),
        )
    ]
    down_sent, down_got = send_on(
        [(order[1], [terms]) for terms, order in zip(down_terms, orders)], down_bits
    )
    down_got = [got for got, _ in down_got]
    conv_came, down_got = ordering((conv_came, down_got))

    conv_members = [
        [
            [plain(conv_keeps[member], bits), (conv_came, bits, member * width // size, size)]
            for member, size in members
        ]
        for members in (((0, width), (1, width)), ((2, width), (3, width), (4, 128)))
    ]
    conv_sent, conv_got = send_on(
        [(order[0], members) for members, order in zip(conv_members, orders)], bits
    )
    conv_got = [got for got, _ in conv_got]

    block_out = (hidden_res[:rows] + out_keep + out_came).astype(jnp.bfloat16)
    down_streams = [
        terms + [plain(got, without(down_bits, *order[:2]))]
        for terms, got, order in zip(down_terms, down_got, orders)
    ]
    down_sent, down_streams = side_by_side(down_streams, lower[2:])
    conv_got = after(conv_got, block_out)

    for index, (members, order) in enumerate(zip(conv_members, orders)):
        edge = 0
        for terms in members:
            size = terms[0][3]
            terms.append((conv_got[index], without(bits, order[0]), edge // size, size))
            edge += size
    conv_sent, conv_two = send_on(
        [(order[1], members) for members, order in zip(conv_members, orders)], bits
    )
    quarter = after(quarter, conv_sent)
    down_streams = gated(down_streams, conv_sent)
    part, down_last = settle(info, slots, [(down_streams, (jnp.float32, jnp.bfloat16))])
    pairs = [
        (source * 2 + side, (source ^ (1 << top)) * 2 + side)
        for source in range(chips)
        for side in range(2)
        if (source >> top) & 1 != side
    ]
    down_far = lax.ppermute(down_last, AXES, pairs)
    edge = counts[1] * TILE
    two_terms = [[(quarter, bits[2:], block, edge)] for block in range(2)]
    two_sent, two_got = send_on(
        [(order[0], [terms]) for terms, order in zip(two_terms, orders)], bits[2:]
    )
    two_got = [got for got, _ in two_got]

    conv_two, down_far = ordering(([got for got, _ in conv_two], down_far))
    part = part + down_far.astype(jnp.float32)
    part = part.reshape(2, -1, width)
    down_out = jnp.where(
        coords[top] == core, take(part, core, 0), partner(take(part, 1 - core, 0))
    )

    conv_streams = []
    for members, got, order in zip(conv_members, conv_two, orders):
        edge = 0
        for terms in members:
            size = terms[0][3]
            conv_streams.append(terms + [(got, without(bits, *order[:2]), edge // size, size)])
            edge += size
    _, conv_streams = side_by_side(conv_streams, lower[2 : top - 1])
    ((conv_all, _),) = combine(info, slots, [(None, conv_streams)])
    two_got = after(two_got, conv_all)
    two_terms = [
        terms + [plain(got, without(bits[2:], order[0]))]
        for terms, got, order in zip(two_terms, two_got, orders)
    ]
    two_sent, two_got = send_on(
        [(order[1], [terms]) for terms, order in zip(two_terms, orders)], bits[2:]
    )
    two_streams = [terms + [plain(*got)] for terms, got in zip(two_terms, two_got)]
    _, two_streams = side_by_side(two_streams, lower[2 : top - 1])

    conv_done = upper_sum(conv_all)
    two_streams = gated(two_streams, conv_all)
    b_out, out_out, c_out, x_out, vectors = (
        [(conv_done, [], member * width // size, size)]
        for member, size in enumerate([width] * 4 + [128])
    )
    in_out, out_out, vectors = settle(
        info,
        slots,
        [
            ([b_out, c_out, x_out], (jnp.float32,)),
            ([out_out], (jnp.float32,)),
            ([vectors], (jnp.float32,)),
        ],
    )

    gate_tiles = [tile for tile in range(counts[0])] + [tiles + tile for tile in range(counts[0])]
    for tile in range(counts[1]):
        gate_tiles += [counts[0] + tile, tiles + counts[0] + tile]
    two_streams = gated(two_streams, conv_sent)
    kept, send = finish(info, slots, [[plain(one_done, [])]] + two_streams, gate_tiles)
    other = partner(send)
    gate_out = both(kept[:, :hidden], other[:, :hidden], 1)
    up_out = both(kept[:, hidden:], other[:, hidden:], 1)
    return (
        block_out,
        input_grad,
        vectors[:, 0],
        in_out,
        vectors[:, 2:5],
        out_out,
        vectors[:, 1],
        gate_out,
        up_out,
        down_out,
    )


def solution(mesh):
    placed = (
        P(AXES, None),
        P(AXES, None),
        P(),
        P("wa"),
        P("wa", None),
        P("wa", None),
        P("wa", None),
        P("wa"),
        P("wa", None),
        P("wa", None),
        P("wa", None),
    )
    return jax.shard_map(
        local,
        mesh=mesh,
        in_specs=placed,
        out_specs=(
            P(AXES, None),
            P(AXES, None),
            P(AXES),
            P(AXES, None),
            P(AXES, None),
            P(AXES, None),
            P(AXES),
            P(AXES, None),
            P(AXES, None),
            P(AXES, None),
        ),
        check_vma=False,
    )
```

```python
import functools
import math

import jax
import jax.numpy as jnp
from jax import lax
from jax.experimental import pallas as pl
from jax.experimental.pallas import tpu as pltpu
from jax.sharding import PartitionSpec as P

epsilon = 1e-05
AXES = ("seq", "wa")
HALO = 16
TILE = 256
VMEM_LIMIT = 63 * 2**20
NN = ((1,), (0,))
NT = ((1,), (1,))
TN = ((0,), (0,))


def shifted(value, steps):
    count = lax.axis_size(AXES)
    first, last = (max(0, -steps), min(count, count - steps))
    return lax.ppermute(value, AXES, [(source, source + steps) for source in range(first, last)])


def partner(value):
    return lax.ppermute(value, "wa", [(0, 1), (1, 0)])


def across(value, bit):
    count = lax.axis_size("seq")
    return lax.ppermute(value, "seq", [(place, place ^ (1 << bit)) for place in range(count)])


def dot(left, right, dims):
    return lax.dot_general(left, right, (dims, ((), ())), preferred_element_type=jnp.float32)


def take(value, index, axis):
    return lax.dynamic_index_in_dim(value, index, axis, keepdims=False)


def total(terms):
    result = terms[0].astype(jnp.float32)
    for term in terms[1:]:
        result = result + term.astype(jnp.float32)
    return result


def chosen(test, value, other):
    return jnp.where(test, value, other)


def swapped(value):
    half = value.shape[1] // 2
    return jnp.concatenate([value[:, half:], value[:, :half]], axis=1)


def params(**extra):
    return dict(
        compiler_params=pltpu.CompilerParams(vmem_limit_bytes=VMEM_LIMIT),
        cost_estimate=pl.CostEstimate(flops=1000, bytes_accessed=1000, transcendentals=0),
        **extra,
    )


def conv_rows(mixed, keep_one, keep_two, taps, count):
    now = mixed[pl.ds(HALO, count), :]
    one = mixed[pl.ds(HALO - 1, count), :] * keep_one
    two = mixed[pl.ds(HALO - 2, count), :] * keep_two
    conv = taps[2:3, :] * now + taps[3:4, :] * one + taps[4:5, :] * two
    return now, one, two, conv


def join_rows(weights, own, other):
    half = own[0].shape[0]
    for index, (upper, lower) in enumerate(zip(own, other)):
        weights[:half, index * TILE : (index + 1) * TILE] = upper[...]
        weights[half:, index * TILE : (index + 1) * TILE] = lower[...]


def forward_kernel(
    info,
    tokens,
    before,
    after,
    small,
    taps,
    keeps,
    own_b,
    own_c,
    own_x,
    other_b,
    other_c,
    other_x,
    out_own,
    out_other,
    b_ref,
    c_ref,
    x_ref,
    hidden,
    norm_own,
    norm_send,
    normed,
    weights,
    mixed,
    gated,
    total_ref,
):
    step = pl.program_id(0)
    first_core = info[0] == 0
    rows, width = tokens.shape
    half = width // 2
    ext = rows + HALO

    @pl.when(step == 0)
    def _():
        for start, ref in ((0, before), (HALO, tokens), (HALO + rows, after)):
            resid = ref[:, :width].astype(jnp.float32)
            scale = lax.rsqrt(jnp.mean(resid * resid, axis=-1, keepdims=True) + epsilon)
            norm = resid * scale * small[0:1, :]
            place = pl.ds(start, ref.shape[0])
            normed[place, :half] = chosen(first_core, norm[:, :half], norm[:, half:]).astype(
                jnp.bfloat16
            )
            normed[place, half:] = chosen(first_core, norm[:, half:], norm[:, :half]).astype(
                jnp.bfloat16
            )
        total_ref[:rows, :] = tokens[...].astype(jnp.float32)
        total_ref[rows:, :] = after[:, :width].astype(jnp.float32)

    join_rows(weights, (own_b, own_c, own_x), (other_b, other_c, other_x))
    proj = dot(normed[...], weights[...], NN)
    b_part, c_part, x_part = proj[:, :TILE], proj[:, TILE : 2 * TILE], proj[:, 2 * TILE :]
    b_ref[...] = b_part
    c_ref[...] = c_part
    x_ref[...] = x_part
    mixed[...] = b_part * x_part
    conv = conv_rows(mixed, keeps[:, 0:1], keeps[:, 1:2], taps, ext)[3]
    gated[...] = (c_ref[pl.ds(HALO, ext), :] * conv).astype(jnp.bfloat16)
    here = pl.num_programs(0) // 2

    @pl.when(step < here)
    def _():
        total_ref[...] += dot(gated[...], out_own[...], NN)

    @pl.when(step >= here)
    def _():
        total_ref[...] += dot(gated[...], out_other[...], NN)

    @pl.when(step == pl.num_programs(0) - 1)
    def _():
        resid = total_ref[...]
        hidden[...] = resid
        scale = lax.rsqrt(jnp.mean(resid * resid, axis=-1, keepdims=True) + epsilon)
        norm = resid * scale * small[1:2, :]
        low = chosen(first_core, norm[:, :half], norm[:, half:]).astype(jnp.bfloat16)
        high = chosen(first_core, norm[:, half:], norm[:, :half]).astype(jnp.bfloat16)
        norm_own[:, :half] = low
        norm_own[:, half:] = high
        norm_send[:, :half] = high
        norm_send[:, half:] = low


def channel_specs(width):
    steps = width // TILE
    half = width // 2

    def at(j, info):
        return lax.rem(info[0] * (steps // 2) + j, steps)

    thirds = [
        pl.BlockSpec((half, TILE), lambda j, info, k=k: (0, k * steps + at(j, info)))
        for k in range(3)
    ]
    out_own = pl.BlockSpec((TILE, width), lambda j, info: (jnp.minimum(j, steps // 2 - 1), 0))
    out_other = pl.BlockSpec((TILE, width), lambda j, info: (jnp.maximum(j - steps // 2, 0), 0))
    return steps, at, thirds * 2 + [out_own, out_other]


def fixed(*shape):
    return pl.BlockSpec(shape, lambda j, info: (0,) * len(shape))


def conv_forward(info, tokens, before, after, small, keeps, w_in, w_in_other, w_out, w_out_other):
    rows, width = tokens.shape
    ext = rows + HALO
    steps, at, weight_specs = channel_specs(width)
    column = pl.BlockSpec((ext + HALO, TILE), lambda j, info: (0, at(j, info)))
    return pl.pallas_call(
        forward_kernel,
        out_shape=[jax.ShapeDtypeStruct((ext + HALO, width), jnp.float32)] * 3
        + [jax.ShapeDtypeStruct((ext, width), jnp.float32)]
        + [jax.ShapeDtypeStruct((ext, width), jnp.bfloat16)] * 2,
        grid_spec=pltpu.PrefetchScalarGridSpec(
            num_scalar_prefetch=1,
            grid=(steps,),
            in_specs=[
                fixed(rows, width),
                fixed(HALO, width),
                fixed(*after.shape),
                fixed(*small.shape),
                pl.BlockSpec((small.shape[0], TILE), lambda j, info: (0, at(j, info))),
                fixed(*keeps.shape),
            ]
            + weight_specs,
            out_specs=[column] * 3 + [fixed(ext, width)] * 3,
            scratch_shapes=[
                pltpu.VMEM((ext + HALO, width), jnp.bfloat16),
                pltpu.VMEM((width, 3 * TILE), jnp.bfloat16),
                pltpu.VMEM((ext + HALO, TILE), jnp.float32),
                pltpu.VMEM((ext, TILE), jnp.bfloat16),
                pltpu.VMEM((ext, width), jnp.float32),
            ],
        ),
        name="conv_forward",
        **params(),
    )(
        info,
        tokens,
        before,
        after,
        small,
        small,
        keeps,
        *[w_in] * 3,
        *[w_in_other] * 3,
        w_out,
        w_out_other,
    )


def backward_kernel(
    info,
    tokens,
    hidden,
    cotangent,
    after,
    back,
    came,
    small,
    taps,
    keeps,
    b_ref,
    c_ref,
    x_ref,
    own_b,
    own_c,
    own_x,
    other_b,
    other_c,
    other_x,
    out_own,
    out_other,
    input_grad,
    send,
    b_keep,
    out_keep,
    c_keep,
    x_keep,
    vector_keep,
    vectors,
    d_hidden,
    d_branch,
    norm_in,
    d_norm_in,
    weights,
    mixed,
    d_gated,
    along_one,
    along_two,
    d_proj,
):
    step = pl.program_id(0)
    core = info[0]
    first_core = core == 0
    rows, width = tokens.shape
    half = width // 2
    ext = rows + HALO

    def token_norm():
        resid = tokens[...].astype(jnp.float32)
        scale = lax.rsqrt(jnp.mean(resid * resid, axis=-1, keepdims=True) + epsilon)
        return resid * scale, scale

    def back_through(grad, normed, scale, gain):
        inner = grad * gain
        return scale * (inner - normed * jnp.mean(inner * normed, axis=-1, keepdims=True))

    def in_order(own, other):
        return jnp.concatenate(
            [chosen(first_core, own, other), chosen(first_core, other, own)], axis=1
        )

    @pl.when(step == 0)
    def _():
        vectors[...] = jnp.zeros(vectors.shape, jnp.float32)
        grad = in_order(back[:, :half] + came[:, half:], back[:, half:] + came[:, :half])
        resid = hidden[...]
        scale = lax.rsqrt(jnp.mean(resid * resid, axis=-1, keepdims=True) + epsilon)
        normed = resid * scale
        vectors[1:2, :] = jnp.sum(grad[:rows] * normed[:rows], axis=0, keepdims=True)
        result = back_through(grad, normed, scale, small[1:2, :])
        result = result + jnp.concatenate([cotangent[...], after[...]], axis=0).astype(jnp.float32)
        d_hidden[...] = result
        d_branch[...] = result.astype(jnp.bfloat16)
        norm_in[...] = (token_norm()[0] * small[0:1, :]).astype(jnp.bfloat16)
        d_norm_in[...] = jnp.zeros(d_norm_in.shape, jnp.float32)

    here = pl.num_programs(0) // 2

    @pl.when(step < here)
    def _():
        d_gated[...] = dot(d_branch[...], out_own[...], NT)

    @pl.when(step >= here)
    def _():
        d_gated[...] = dot(d_branch[...], out_other[...], NT)

    join_rows(weights, (own_b, own_c, own_x), (other_b, other_c, other_x))
    mixed[...] = b_ref[...] * x_ref[...]
    now, one, two, conv = conv_rows(mixed, keeps[:, 0:1], keeps[:, 1:2], taps, ext)
    c_part = c_ref[pl.ds(HALO, ext), :]
    grad = d_gated[...]
    gated = (c_part[:rows] * conv[:rows]).astype(jnp.bfloat16)
    d_conv = grad * c_part
    block = lax.rem(core * here + step, pl.num_programs(0))
    lanes = pl.ds(pl.multiple_of(block * TILE, TILE), TILE)
    for index, view in enumerate((now, one, two)):
        vectors[2 + index : 3 + index, lanes] = jnp.sum(
            d_conv[:rows] * view[:rows], axis=0, keepdims=True
        )
    along_one[...] = keeps[:, 0:1] * d_conv * taps[3:4, :]
    along_two[...] = keeps[:, 1:2] * d_conv * taps[4:5, :]
    d_mixed = (
        taps[2:3, :] * d_conv[:rows] + along_one[pl.ds(1, rows), :] + along_two[pl.ds(2, rows), :]
    )
    d_proj[:, :TILE] = (d_mixed * x_ref[pl.ds(HALO, rows), :]).astype(jnp.bfloat16)
    d_proj[:, TILE : 2 * TILE] = (grad[:rows] * conv[:rows]).astype(jnp.bfloat16)
    d_proj[:, 2 * TILE :] = (d_mixed * b_ref[pl.ds(HALO, rows), :]).astype(jnp.bfloat16)
    out_grad = dot(gated, d_branch[:rows, :], TN)
    in_grad = dot(norm_in[...], d_proj[...], TN)
    d_norm_in[...] += dot(d_proj[...], weights[...], NT)
    groups, per, _ = send.shape
    few = groups // pl.num_programs(0)

    def divide(value, keep, group, at):
        pair = value.reshape(value.shape[0] // (2 * per), 2, per, value.shape[1]).astype(send.dtype)
        for side in range(2):

            @pl.when(core == side)
            def _():
                send[group, :, at] = pair[:, 1 - side]
                keep[...] = pair[:, side]

    every = slice(None)
    for index, keep in enumerate((b_keep, None, c_keep, x_keep)):
        if keep is None:
            divide(out_grad, out_keep, pl.ds(block * few, few), pl.ds(width, width))
        else:
            third = index and index - 1
            at = pl.multiple_of(index * width + block * TILE, TILE)
            divide(in_grad[:, third * TILE : (third + 1) * TILE], keep, every, pl.ds(at, TILE))

    @pl.when(step == pl.num_programs(0) - 1)
    def _():
        final = in_order(d_norm_in[:, :half], d_norm_in[:, half:])
        normed, scale = token_norm()
        vectors[0:1, :] = jnp.sum(final * normed, axis=0, keepdims=True)
        input_grad[...] = (
            d_hidden[:rows, :] + back_through(final, normed, scale, small[0:1, :])
        ).astype(jnp.bfloat16)
        divide(vectors[...].T, vector_keep, every, pl.ds(4 * width, vectors.shape[0]))


def conv_backward(
    info,
    tokens,
    hidden,
    cotangent,
    after,
    back,
    came,
    small,
    keeps,
    parts,
    w_in,
    w_in_other,
    w_out,
    w_out_other,
    devices,
):
    rows, width = tokens.shape
    ext = rows + HALO
    steps, at, weight_specs = channel_specs(width)
    column = pl.BlockSpec((ext + HALO, TILE), lambda j, info: (0, at(j, info)))
    per = width // devices
    kind = jnp.bfloat16 if per % 16 == 0 else jnp.float32
    groups = devices // 2
    by_columns = pl.BlockSpec((groups, per, TILE), lambda j, info: (0, 0, at(j, info)))
    by_rows = pl.BlockSpec((groups // steps, per, width), lambda j, info: (at(j, info), 0, 0))
    return pl.pallas_call(
        backward_kernel,
        out_shape=[
            jax.ShapeDtypeStruct((rows, width), jnp.bfloat16),
            jax.ShapeDtypeStruct((groups, per, 4 * width + 128), kind),
        ]
        + [jax.ShapeDtypeStruct((groups, per, width), kind)] * 4
        + [jax.ShapeDtypeStruct((groups, per, 128), kind)],
        grid_spec=pltpu.PrefetchScalarGridSpec(
            num_scalar_prefetch=1,
            grid=(steps,),
            in_specs=[
                fixed(rows, width),
                fixed(ext, width),
                fixed(rows, width),
                pl.BlockSpec((HALO, width), lambda j, info: (0, 1)),
                fixed(ext, width),
                fixed(ext, width),
                fixed(*small.shape),
                pl.BlockSpec((small.shape[0], TILE), lambda j, info: (0, at(j, info))),
                fixed(*keeps.shape),
            ]
            + [column] * 3
            + weight_specs,
            out_specs=[
                fixed(rows, width),
                fixed(groups, per, 4 * width + 128),
                by_columns,
                by_rows,
                by_columns,
                by_columns,
                fixed(groups, per, 128),
            ],
            scratch_shapes=[
                pltpu.VMEM((128, width), jnp.float32),
                pltpu.VMEM((ext, width), jnp.float32),
                pltpu.VMEM((ext, width), jnp.bfloat16),
                pltpu.VMEM((rows, width), jnp.bfloat16),
                pltpu.VMEM((rows, width), jnp.float32),
                pltpu.VMEM((width, 3 * TILE), jnp.bfloat16),
                pltpu.VMEM((ext + HALO, TILE), jnp.float32),
                pltpu.VMEM((ext, TILE), jnp.float32),
                pltpu.VMEM((ext, TILE), jnp.float32),
                pltpu.VMEM((ext, TILE), jnp.float32),
                pltpu.VMEM((rows, 3 * TILE), jnp.bfloat16),
            ],
        ),
        name="conv_backward",
        **params(),
    )(
        info,
        tokens,
        hidden,
        cotangent,
        after,
        back,
        came,
        small,
        small,
        keeps,
        *parts,
        *[w_in] * 3,
        *[w_in_other] * 3,
        w_out,
        w_out_other,
    )


def ffn_kernel(
    pieces,
    split,
    info,
    n_own,
    n_other,
    g_own,
    g_after,
    g_other,
    g_other_after,
    gate_own,
    gate_other,
    up_own,
    up_other,
    down_ref,
    act_ref,
    back_keep,
    back_send,
    gate_send,
    gate_keep,
    up_send,
    up_keep,
    whole,
    n_all,
    g_all,
    back,
    weights,
    grads,
):
    step = pl.program_id(0)
    rows = n_all.shape[0]
    block = g_own.shape[0]
    real = 2 * block
    tile = down_ref.shape[0]
    places = (
        (pl.ds(0, block), 0, pl.ds(0, block), g_own),
        (pl.ds(real, HALO), 0, pl.ds(block, HALO), g_after),
        (pl.ds(block, block), 1, pl.ds(0, block), g_other),
        (pl.ds(real + HALO, HALO), 1, pl.ds(block, HALO), g_other_after),
    )

    @pl.when(step == 0)
    def _():
        back[...] = jnp.zeros(back.shape, jnp.float32)
        for place, which, source, grad in places:
            n_all[place, :] = (n_own, n_other)[which][source, :]
            g_all[place, :] = grad[...]

    join_rows(weights, (gate_own, up_own), (gate_other, up_other))
    size = -(-rows // pieces // 16) * 16
    for start in range(0, rows, size):
        part = pl.ds(start, min(size, rows - start))
        proj = dot(n_all[part, :], weights[...], NN)
        d_act = dot(g_all[part, :], down_ref[...], NT)
        gate = proj[:, :tile]
        up_val = proj[:, tile:]
        sigma = 0.5 * jnp.tanh(0.5 * gate) + 0.5
        silu = gate * sigma
        act_ref[part, :] = (silu * up_val).astype(jnp.bfloat16)
        grads[part, tile:] = (d_act * silu).astype(jnp.bfloat16)
        grads[part, :tile] = (d_act * up_val * (sigma + silu * (1.0 - sigma))).astype(jnp.bfloat16)
        back[part, :] += dot(grads[part, :], weights[...], NT)
    summed = dot(n_all[:real, :], grads[:real, :], TN).astype(jnp.bfloat16)
    half = summed.shape[0] // 2
    for core in range(2):

        @pl.when(jnp.logical_and(step >= split, info[0] == core))
        def _():
            whole[:half, :] = summed[core * half : (core + 1) * half, :]
            whole[half:, :] = summed[(1 - core) * half : (2 - core) * half, :]

    for index, (send, keep) in enumerate(((gate_send, gate_keep), (up_send, up_keep))):
        groups, per, columns = send.shape
        pair = summed[:, index * tile : (index + 1) * tile].reshape(groups, 2, per, columns)
        for value in range(2):

            @pl.when(jnp.logical_and(step < split, info[1 + index] == value))
            def _():
                send[...] = pair[:, 1 - value]
                keep[...] = pair[:, value]

    @pl.when(step == pl.num_programs(0) - 1)
    def _():
        for place, which, source, _ in places:
            (back_keep, back_send)[which][source, :] = back[place, :]


def ffn(info, norms, grads, weights, down, split, pers):
    ext, width = norms[0].shape
    rows = 2 * ext
    half = width // 2
    count = down.shape[0] // TILE
    column = pl.BlockSpec((half, TILE), lambda j, info: (0, info[0] * count + j))
    shapes = [jax.ShapeDtypeStruct((rows, count * TILE), jnp.bfloat16)]
    specs = [pl.BlockSpec((rows, TILE), lambda j, info: (0, j))]
    for _ in range(2):
        shapes.append(jax.ShapeDtypeStruct((ext, width), jnp.float32))
        specs.append(fixed(ext, width))
    for per in pers:
        for _ in range(2):
            groups = width // (2 * per)
            shapes.append(jax.ShapeDtypeStruct((groups, per, split * TILE), jnp.bfloat16))
            specs.append(
                pl.BlockSpec(
                    (groups, per, TILE), lambda j, info: (0, 0, jnp.minimum(j, split - 1))
                )
            )
    shapes.append(jax.ShapeDtypeStruct((width, 2 * (count - split) * TILE), jnp.bfloat16))
    specs.append(pl.BlockSpec((width, 2 * TILE), lambda j, info: (0, jnp.maximum(j - split, 0))))
    after = pl.BlockSpec((HALO, width), lambda j, info: (0, 1))
    return pl.pallas_call(
        functools.partial(ffn_kernel, 2, split),
        out_shape=shapes,
        grid_spec=pltpu.PrefetchScalarGridSpec(
            num_scalar_prefetch=1,
            grid=(count,),
            in_specs=[fixed(ext, width)] * 2
            + [fixed(ext - HALO, width), after] * 2
            + [column] * 4
            + [pl.BlockSpec((TILE, width), lambda j, info: (j, 0))],
            out_specs=specs,
            scratch_shapes=[
                pltpu.VMEM((rows, width), jnp.bfloat16),
                pltpu.VMEM((rows, width), jnp.bfloat16),
                pltpu.VMEM((rows, width), jnp.float32),
                pltpu.VMEM((width, 2 * TILE), jnp.bfloat16),
                pltpu.VMEM((rows, 2 * TILE), jnp.bfloat16),
            ],
        ),
        name="ffn",
        **params(),
    )(info, *norms, *grads, *weights, down)


def down_kernel(
    info,
    act,
    g_own,
    g_other,
    down_ref,
    out_keep,
    out_send,
    low_send,
    low_keep,
    high_send,
    high_keep,
    rhs,
    grad,
):
    step = pl.program_id(0)
    block = out_keep.shape[0]
    real = 2 * block
    rhs[:block, :] = g_own[...]
    rhs[block:, :] = g_other[...]
    result = dot(act[:real, :], down_ref[...], NN)
    out_keep[...] = result[:block]
    out_send[...] = result[block:]
    grad[...] = dot(act[:real, :], rhs[...], TN).astype(grad.dtype)
    here = pl.num_programs(0) // 2
    outs = ((step < here, low_send, low_keep, info[1]), (step >= here, high_send, high_keep, info[2]))
    for now, send, keep, mine in outs:
        groups, per, _ = send.shape
        for value in range(2):

            @pl.when(jnp.logical_and(now, mine == value))
            def _():
                for group in range(groups):
                    start = 2 * group * per
                    send[group] = grad[pl.ds(start + (1 - value) * per, per), :]
                    keep[group] = grad[pl.ds(start + value * per, per), :]


def down_part(info, act, g_own, g_other, down, pers):
    hidden, width = down.shape
    steps = width // TILE
    here = steps // 2
    block = g_own.shape[0]
    kind = jnp.bfloat16 if min(pers) % 16 == 0 else jnp.float32
    tile = pl.BlockSpec((block, TILE), lambda j, info: (0, j))
    shapes = [jax.ShapeDtypeStruct((block, width), jnp.float32)] * 2
    specs = [tile] * 2
    for index, per in enumerate(pers):
        groups = hidden // (2 * per)
        for _ in range(2):
            shapes.append(jax.ShapeDtypeStruct((groups, per, width // 2), kind))
            if index == 0:
                specs.append(
                    pl.BlockSpec(
                        (groups, per, TILE), lambda j, info: (0, 0, jnp.minimum(j, here - 1))
                    )
                )
            else:
                specs.append(
                    pl.BlockSpec((groups, per, TILE), lambda j, info: (0, 0, jnp.maximum(j - here, 0)))
                )
    return pl.pallas_call(
        down_kernel,
        out_shape=shapes,
        grid_spec=pltpu.PrefetchScalarGridSpec(
            num_scalar_prefetch=1,
            grid=(steps,),
            in_specs=[
                fixed(*act.shape),
                tile,
                tile,
                pl.BlockSpec((hidden, TILE), lambda j, info: (0, j)),
            ],
            out_specs=specs,
            scratch_shapes=[
                pltpu.VMEM((2 * block, TILE), jnp.bfloat16),
                pltpu.VMEM((hidden, TILE), kind),
            ],
        ),
        name="down",
        **params(),
    )(info, act, g_own, g_other, down)


def combine_kernel(plan, info, *refs):
    refs = list(refs)
    inputs = [[[refs.pop(0) for _ in range(count)] for count in counts] for counts in plan]
    for members, out in zip(inputs, refs):
        edge = 0
        for terms in members:
            size = terms[0].shape[-1]
            value = terms[0][...].astype(jnp.float32)
            for term in terms[1:]:
                value = value + term[...].astype(jnp.float32)
            out[..., edge : edge + size] = value.reshape(out.shape[:-1] + (size,)).astype(out.dtype)
            edge += size


def combine(info, slots, jobs, flip=False):
    plan, arrays, specs, shapes, out_specs = [], [], [], [], []
    lefts = []
    for bit, members in jobs:
        common = members[0][0][1]
        for terms in members:
            for _, names, _, _ in terms:
                common = [name for name in common if name in names]
        lefts.append([name for name in common if name != bit])
    gridded = all(lefts)
    for (bit, members), left in zip(jobs, lefts):
        for terms in members:
            for array, names, block, size in terms:
                rows = array.size // array.shape[-1] >> len(names)
                arrays.append(array.reshape([2] * len(names) + [rows, array.shape[-1]]))
                shape, picks = [], []
                for name in names:
                    if name == bit:
                        shape.append(None)
                        picks.append(("other", slots[name]))
                    elif name not in left:
                        shape.append(None)
                        picks.append(("mine", slots[name]))
                    elif gridded and name == left[0]:
                        shape.append(None)
                        picks.append(("step", 0))
                    else:
                        shape.append(2)
                        picks.append(("all", 0))

                def index_map(j, info, picks=picks, block=block):
                    where = []
                    for kind, slot in picks:
                        if kind == "all":
                            where.append(0)
                        elif kind == "step":
                            where.append(lax.rem(j + info[0], 2) if flip else j)
                        else:
                            where.append(info[slot] if kind == "mine" else 1 - info[slot])
                    return (*where, 0, block)

                specs.append(pl.BlockSpec((*shape, rows, size), index_map))
        width = sum(terms[0][3] for terms in members)
        kind = jnp.bfloat16 if rows % 16 == 0 else jnp.float32
        outer = 1 << len(left)
        shapes.append(jax.ShapeDtypeStruct((outer, rows, width), kind))
        inner = outer // 2 if gridded else outer
        out_specs.append(pl.BlockSpec((inner, rows, width), lambda j, info: (j, 0, 0)))
        plan.append([len(terms) for terms in members])
    results = pl.pallas_call(
        functools.partial(combine_kernel, plan),
        out_shape=shapes,
        grid_spec=pltpu.PrefetchScalarGridSpec(
            num_scalar_prefetch=1,
            grid=(2 if gridded else 1,),
            in_specs=specs,
            out_specs=out_specs,
        ),
        name="combine",
        **params(),
    )(info, *arrays)
    return list(zip(results, lefts))


def finish_kernel(counts, tiles, info, *refs):
    *inputs, mine, send, scratch = refs
    place = 0
    for count in counts:
        value = inputs[0][...].astype(jnp.float32)
        for term in inputs[1:count]:
            value = value + term[...].astype(jnp.float32)
        inputs = inputs[count:]
        for tile in range(value.shape[1] // TILE):
            start = tiles[place] * TILE
            scratch[:, start : start + TILE] = value[:, tile * TILE : (tile + 1) * TILE]
            place += 1
    rows = mine.shape[0]
    for side, out in ((info[0], mine), (1 - info[0], send)):
        out[...] = scratch[pl.ds(pl.multiple_of(side * rows, rows), rows), :]


def picked(slots, terms):
    arrays, specs = [], []
    for array, names, block, size in terms:
        rows = array.size // array.shape[-1] >> len(names)
        arrays.append(array.reshape([2] * len(names) + [rows, array.shape[-1]]))
        specs.append(
            pl.BlockSpec(
                (*[None] * len(names), rows, size),
                lambda j, info, names=names, block=block: (
                    *[info[slots[name]] for name in names],
                    0,
                    block,
                ),
            )
        )
    return arrays, specs


def settle_kernel(plan, info, *refs):
    refs = list(refs)
    inputs = [[[refs.pop(0) for _ in range(count)] for count in counts] for counts, _ in plan]
    for members, (_, kinds) in zip(inputs, plan):
        outs = [refs.pop(0) for _ in kinds]
        edge = 0
        for terms in members:
            size = terms[0].shape[-1]
            value = terms[0][...].astype(jnp.float32)
            for term in terms[1:]:
                value = value + term[...].astype(jnp.float32)
            for out in outs:
                out[:, edge : edge + size] = value.astype(out.dtype)
            edge += size


def settle(info, slots, groups):
    arrays, specs, shapes, plan = [], [], [], []
    for members, kinds in groups:
        for terms in members:
            views, view_specs = picked(slots, terms)
            arrays += views
            specs += view_specs
        rows = views[0].shape[-2]
        width = sum(terms[0][3] for terms in members)
        shapes += [jax.ShapeDtypeStruct((rows, width), kind) for kind in kinds]
        plan.append(([len(terms) for terms in members], kinds))
    return pl.pallas_call(
        functools.partial(settle_kernel, plan),
        out_shape=shapes,
        grid_spec=pltpu.PrefetchScalarGridSpec(
            num_scalar_prefetch=1,
            grid=(1,),
            in_specs=specs,
            out_specs=[fixed(*shape.shape) for shape in shapes],
        ),
        name="settle",
        **params(),
    )(info, *arrays)


def finish(info, slots, members, tiles):
    columns = len(tiles) * TILE
    arrays, specs = [], []
    for terms in members:
        views, view_specs = picked(slots, terms)
        rows = views[0].shape[-2]
        arrays += views
        specs += view_specs
    return pl.pallas_call(
        functools.partial(finish_kernel, [len(terms) for terms in members], tiles),
        out_shape=[jax.ShapeDtypeStruct((rows // 2, columns), jnp.float32)] * 2,
        grid_spec=pltpu.PrefetchScalarGridSpec(
            num_scalar_prefetch=1,
            grid=(1,),
            in_specs=specs,
            out_specs=[fixed(rows // 2, columns)] * 2,
            scratch_shapes=[pltpu.VMEM((rows, columns), jnp.float32)],
        ),
        name="finish",
        **params(),
    )(info, *arrays)


def local(
    tokens,
    cotangent,
    doc_lengths,
    norm_gain,
    in_weight,
    conv_taps,
    out_weight,
    ffn_gain,
    gate_weight,
    up_weight,
    down_weight,
):
    rows, width = tokens.shape
    hidden = down_weight.shape[0]
    chips = lax.axis_size("seq")
    top = chips.bit_length() - 2
    lower = list(range(top))
    bits = list(range(top, -1, -1))
    chip = lax.axis_index("seq")
    core = lax.axis_index("wa")
    coords = {bit: (chip >> bit) & 1 for bit in range(top + 1)}
    turned = dict(coords)
    turned[top] = coords[top] ^ core
    ordering = lax.optimization_barrier

    def after(value, *gates):
        return ordering((value, gates))[0]

    def ordered(low, high):
        return jnp.where(core == 0, low, high)

    def both(own, other, axis):
        return ordered(
            jnp.concatenate([own, other], axis=axis), jnp.concatenate([other, own], axis=axis)
        )

    w_in_other = partner(in_weight)
    small = jnp.concatenate([norm_gain[None], ffn_gain[None], conv_taps.T], axis=0)
    small = jnp.pad(small, ((0, 3), (0, 0)))
    small = both(small, partner(small), 1).astype(jnp.float32)
    before_rows = shifted(tokens[rows - HALO :], 1)
    after_rows = shifted(jnp.concatenate([tokens[:HALO], cotangent[:HALO]], axis=1), -1)
    w_out_other = partner(out_weight)
    cot_other = partner(cotangent)
    after_other = partner(after_rows)
    gate_other = partner(gate_weight)
    up_other = partner(up_weight)

    place = lax.axis_index(AXES) * rows + jnp.arange(rows + HALO, dtype=jnp.int32)
    starts = jnp.cumsum(doc_lengths) - doc_lengths
    first = jnp.any(place[:, None] == starts[None, :], axis=1)
    before = jnp.any((place - 1)[:, None] == starts[None, :], axis=1)
    keep_one = jnp.where(first, 0.0, 1.0)
    keep_two = jnp.where(jnp.logical_or(first, before), 0.0, 1.0)
    keeps = jnp.stack([keep_one, keep_two], axis=1).astype(jnp.float32)
    info = [core] + [coords[bit] for bit in lower] + [coords[top], turned[top]]
    info = jnp.stack(info).astype(jnp.int32)

    *parts, hidden_res, norm_own, norm_send = conv_forward(
        info,
        tokens,
        before_rows,
        after_rows,
        small,
        keeps,
        in_weight,
        w_in_other,
        out_weight,
        w_out_other,
    )
    norm_other = partner(norm_send)
    per_chip = width // chips
    pers = (per_chip << lower[0], per_chip << lower[1])
    tiles = hidden // TILE
    split = tiles * 4 // 9
    counts = (split, tiles - split)
    orders = (lower, [lower[1], lower[0]] + lower[2:])

    act, back_keep, back_send, *one, whole = ffn(
        info,
        (norm_own, norm_other),
        (cotangent, after_rows, cot_other, after_other),
        (gate_weight, gate_other, up_weight, up_other),
        down_weight,
        split,
        pers,
    )
    one_x = across(one[0], orders[0][0])
    one_y = across(one[2], orders[1][0])
    came = partner(back_send)

    groups = [
        [low + (level << (top - 1)) for level in range(4)] for low in range(1 << (top - 1))
    ]
    quarter = lax.psum_scatter(
        whole, "seq", scatter_dimension=0, axis_index_groups=groups, tiled=True
    )

    slots = {bit: 1 + bit for bit in bits}
    turned_slots = dict(slots)
    turned_slots[top] = 2 + top

    def plain(array, names):
        return (array, names, 0, array.shape[-1])

    def gated(streams, *gates):
        held = after([terms[-1][0] for terms in streams], gates)
        return [
            terms[:-1] + [(array, *terms[-1][1:])] for terms, array in zip(streams, held)
        ]

    def without(names, *taken):
        return [name for name in names if name not in taken]

    def send_on(streams, names, use=slots):
        results = combine(info, use, streams)
        return [send for send, _ in results], [
            (across(send, bit), left) for (bit, _), (send, left) in zip(streams, results)
        ]

    def upper_sum(value):
        value = value.reshape(-1, value.shape[-1])
        return lax.psum_scatter(
            value, "seq", scatter_dimension=0, axis_index_groups=groups, tiled=True
        )

    down_pers = [2 * hidden // chips << bit for bit in (lower[0], lower[1])]
    out_keep, out_send, *down_halves = down_part(
        info, act, cotangent, cot_other, down_weight, down_pers
    )
    came, out_send, down_halves, one_x, one_y = ordering(
        (came, out_send, down_halves, one_x, one_y)
    )

    down_x = across(down_halves[0], orders[0][0])
    down_y = across(down_halves[2], orders[1][0])
    out_came = partner(out_send)
    one_terms = [
        [plain(keep, without(bits, order[0])), plain(got, without(bits, order[0]))]
        for keep, got, order in ((one[1], one_x, orders[0]), (one[3], one_y, orders[1]))
    ]
    one_sent, one_got = send_on(
        [(order[1], [terms]) for terms, order in zip(one_terms, orders)], bits, turned_slots
    )
    one_got = [got for got, _ in one_got]
    came = after(came, one_sent)

    def side_by_side(streams, order, use=slots):
        sent = None
        for bit in order:
            sent, ((got, left),) = send_on([(bit, streams)], None, use)
            edge, members = 0, []
            for terms in streams:
                size = terms[0][3]
                members.append(terms + [(got, left, edge, size)])
                edge += size
            for terms in members:
                array, left, edge, size = terms[-1]
                if edge % size:
                    array, edge = array[..., edge : edge + size], 0
                terms[-1] = (array, left, edge // size, size)
            streams = members
        return sent, streams

    input_grad, conv_send, *conv_keeps = conv_backward(
        info,
        tokens,
        hidden_res,
        cotangent,
        after_rows,
        back_keep,
        came,
        small,
        keeps,
        parts,
        in_weight,
        w_in_other,
        out_weight,
        w_out_other,
        2 * chips,
    )
    conv_send, conv_keeps, down_x, down_y, out_came = ordering(
        (conv_send, conv_keeps, down_x, down_y, out_came)
    )
    conv_came = partner(conv_send)

    down_bits = bits[1:]
    down_terms = [
        [plain(keep, without(down_bits, order[0])), plain(got, without(down_bits, order[0]))]
        for keep, got, order in (
            (down_halves[1], down_x, orders[0]),
            (down_halves[3], down_y, orders[1]),
        )
    ]
    down_sent, down_got = send_on(
        [(order[1], [terms]) for terms, order in zip(down_terms, orders)], down_bits
    )
    down_got = [got for got, _ in down_got]

    conv_came = after(conv_came, down_sent)
    conv_members = [
        [
            [plain(conv_keeps[member], bits), (conv_came, bits, member * width // size, size)]
            for member, size in members
        ]
        for members in (((0, width), (1, width)), ((2, width), (3, width), (4, 128)))
    ]
    conv_sent, conv_got = send_on(
        [(order[0], members) for members, order in zip(conv_members, orders)], bits
    )
    conv_got = [got for got, _ in conv_got]

    one_got = after(one_got, conv_sent)
    one_streams = [
        terms + [plain(got, without(bits, *order[:2]))]
        for terms, got, order in zip(one_terms, one_got, orders)
    ]
    _, one_streams = side_by_side(one_streams, lower[2 : top - 1], turned_slots)
    ((one_all, _),) = combine(info, turned_slots, [(None, one_streams)], flip=True)
    one_done = upper_sum(one_all)

    down_got = after(down_got, one_all)
    down_streams = [
        terms + [plain(got, without(down_bits, *order[:2]))]
        for terms, got, order in zip(down_terms, down_got, orders)
    ]
    down_sent, down_streams = side_by_side(down_streams, lower[2:])
    out_came = after(out_came, down_sent)
    block_out = (hidden_res[:rows] + out_keep + out_came).astype(jnp.bfloat16)

    down_streams = gated(down_streams, block_out)
    part, down_last = settle(info, slots, [(down_streams, (jnp.float32, jnp.bfloat16))])
    pairs = [
        (source * 2 + side, (source ^ (1 << top)) * 2 + side)
        for source in range(chips)
        for side in range(2)
        if (source >> top) & 1 != side
    ]
    down_far = lax.ppermute(down_last, AXES, pairs)

    conv_got = after(conv_got, down_last)
    for index, (members, order) in enumerate(zip(conv_members, orders)):
        edge = 0
        for terms in members:
            size = terms[0][3]
            terms.append((conv_got[index], without(bits, order[0]), edge // size, size))
            edge += size
    conv_sent, conv_two = send_on(
        [(order[1], members) for members, order in zip(conv_members, orders)], bits
    )
    conv_two = [got for got, _ in conv_two]

    quarter = after(quarter, conv_sent)
    edge = counts[1] * TILE
    two_terms = [[(quarter, bits[2:], block, edge)] for block in range(2)]
    two_sent, two_got = send_on(
        [(order[0], [terms]) for terms, order in zip(two_terms, orders)], bits[2:]
    )
    two_got = [got for got, _ in two_got]
    conv_two = after(conv_two, two_sent)
    conv_streams = []
    for members, got, order in zip(conv_members, conv_two, orders):
        edge = 0
        for terms in members:
            size = terms[0][3]
            conv_streams.append(terms + [(got, without(bits, *order[:2]), edge // size, size)])
            edge += size
    _, conv_streams = side_by_side(conv_streams, lower[2 : top - 1])
    ((conv_all, _),) = combine(info, slots, [(None, conv_streams)])
    conv_done = upper_sum(conv_all)
    two_got = after(two_got, conv_all)
    two_terms = [
        terms + [plain(got, without(bits[2:], order[0]))]
        for terms, got, order in zip(two_terms, two_got, orders)
    ]
    two_sent, two_got = send_on(
        [(order[1], [terms]) for terms, order in zip(two_terms, orders)], bits[2:]
    )
    two_streams = [terms + [plain(*got)] for terms, got in zip(two_terms, two_got)]
    _, two_streams = side_by_side(two_streams, lower[2 : top - 1])

    part, down_far = after((part, down_far), conv_all)
    part = part + down_far.astype(jnp.float32)
    part = part.reshape(2, -1, width)
    down_out = jnp.where(
        coords[top] == core, take(part, core, 0), partner(take(part, 1 - core, 0))
    )
    b_out, out_out, c_out, x_out, vectors = (
        [(conv_done, [], member * width // size, size)]
        for member, size in enumerate([width] * 4 + [128])
    )
    in_out, out_out, vectors = settle(
        info,
        slots,
        [
            ([b_out, c_out, x_out], (jnp.float32,)),
            ([out_out], (jnp.float32,)),
            ([vectors], (jnp.float32,)),
        ],
    )

    gate_tiles = [tile for tile in range(counts[0])] + [tiles + tile for tile in range(counts[0])]
    for tile in range(counts[1]):
        gate_tiles += [counts[0] + tile, tiles + counts[0] + tile]
    kept, send = finish(info, slots, [[plain(one_done, [])]] + two_streams, gate_tiles)
    other = partner(send)
    gate_out = both(kept[:, :hidden], other[:, :hidden], 1)
    up_out = both(kept[:, hidden:], other[:, hidden:], 1)
    return (
        block_out,
        input_grad,
        vectors[:, 0],
        in_out,
        vectors[:, 2:5],
        out_out,
        vectors[:, 1],
        gate_out,
        up_out,
        down_out,
    )


def solution(mesh):
    placed = (
        P(AXES, None),
        P(AXES, None),
        P(),
        P("wa"),
        P("wa", None),
        P("wa", None),
        P("wa", None),
        P("wa"),
        P("wa", None),
        P("wa", None),
        P("wa", None),
    )
    return jax.shard_map(
        local,
        mesh=mesh,
        in_specs=placed,
        out_specs=(
            P(AXES, None),
            P(AXES, None),
            P(AXES),
            P(AXES, None),
            P(AXES, None),
            P(AXES, None),
            P(AXES),
            P(AXES, None),
            P(AXES, None),
            P(AXES, None),
        ),
        check_vma=False,
    )
```

```python
import functools
import math

import jax
import jax.numpy as jnp
from jax import lax
from jax.experimental import pallas as pl
from jax.experimental.pallas import tpu as pltpu
from jax.sharding import PartitionSpec as P

epsilon = 1e-05
AXES = ("seq", "wa")
HALO = 16
TILE = 256
VMEM_LIMIT = 63 * 2**20
NN = ((1,), (0,))
NT = ((1,), (1,))
TN = ((0,), (0,))


def shifted(value, steps):
    count = lax.axis_size(AXES)
    first, last = (max(0, -steps), min(count, count - steps))
    return lax.ppermute(value, AXES, [(source, source + steps) for source in range(first, last)])


def partner(value):
    return lax.ppermute(value, "wa", [(0, 1), (1, 0)])


def across(value, bit):
    count = lax.axis_size("seq")
    return lax.ppermute(value, "seq", [(place, place ^ (1 << bit)) for place in range(count)])


def dot(left, right, dims):
    return lax.dot_general(left, right, (dims, ((), ())), preferred_element_type=jnp.float32)


def take(value, index, axis):
    return lax.dynamic_index_in_dim(value, index, axis, keepdims=False)


def total(terms):
    result = terms[0].astype(jnp.float32)
    for term in terms[1:]:
        result = result + term.astype(jnp.float32)
    return result


def chosen(test, value, other):
    return jnp.where(test, value, other)


def swapped(value):
    half = value.shape[1] // 2
    return jnp.concatenate([value[:, half:], value[:, :half]], axis=1)


def params(**extra):
    return dict(
        compiler_params=pltpu.CompilerParams(vmem_limit_bytes=VMEM_LIMIT),
        cost_estimate=pl.CostEstimate(flops=1000, bytes_accessed=1000, transcendentals=0),
        **extra,
    )


def conv_rows(mixed, keep_one, keep_two, taps, count):
    now = mixed[pl.ds(HALO, count), :]
    one = mixed[pl.ds(HALO - 1, count), :] * keep_one
    two = mixed[pl.ds(HALO - 2, count), :] * keep_two
    conv = taps[2:3, :] * now + taps[3:4, :] * one + taps[4:5, :] * two
    return now, one, two, conv


def join_rows(weights, own, other):
    half = own[0].shape[0]
    for index, (upper, lower) in enumerate(zip(own, other)):
        weights[:half, index * TILE : (index + 1) * TILE] = upper[...]
        weights[half:, index * TILE : (index + 1) * TILE] = lower[...]


def forward_kernel(
    info,
    tokens,
    before,
    after,
    small,
    taps,
    keeps,
    own_b,
    own_c,
    own_x,
    other_b,
    other_c,
    other_x,
    out_own,
    out_other,
    b_ref,
    c_ref,
    x_ref,
    hidden,
    norm_own,
    norm_send,
    normed,
    weights,
    mixed,
    gated,
    total_ref,
):
    step = pl.program_id(0)
    first_core = info[0] == 0
    rows, width = tokens.shape
    half = width // 2
    ext = rows + HALO

    @pl.when(step == 0)
    def _():
        for start, ref in ((0, before), (HALO, tokens), (HALO + rows, after)):
            resid = ref[:, :width].astype(jnp.float32)
            scale = lax.rsqrt(jnp.mean(resid * resid, axis=-1, keepdims=True) + epsilon)
            norm = resid * scale * small[0:1, :]
            place = pl.ds(start, ref.shape[0])
            normed[place, :half] = chosen(first_core, norm[:, :half], norm[:, half:]).astype(
                jnp.bfloat16
            )
            normed[place, half:] = chosen(first_core, norm[:, half:], norm[:, :half]).astype(
                jnp.bfloat16
            )
        total_ref[:rows, :] = tokens[...].astype(jnp.float32)
        total_ref[rows:, :] = after[:, :width].astype(jnp.float32)

    join_rows(weights, (own_b, own_c, own_x), (other_b, other_c, other_x))
    proj = dot(normed[...], weights[...], NN)
    b_part, c_part, x_part = proj[:, :TILE], proj[:, TILE : 2 * TILE], proj[:, 2 * TILE :]
    b_ref[...] = b_part
    c_ref[...] = c_part
    x_ref[...] = x_part
    mixed[...] = b_part * x_part
    conv = conv_rows(mixed, keeps[:, 0:1], keeps[:, 1:2], taps, ext)[3]
    gated[...] = (c_ref[pl.ds(HALO, ext), :] * conv).astype(jnp.bfloat16)
    here = pl.num_programs(0) // 2

    @pl.when(step < here)
    def _():
        total_ref[...] += dot(gated[...], out_own[...], NN)

    @pl.when(step >= here)
    def _():
        total_ref[...] += dot(gated[...], out_other[...], NN)

    @pl.when(step == pl.num_programs(0) - 1)
    def _():
        resid = total_ref[...]
        hidden[...] = resid
        scale = lax.rsqrt(jnp.mean(resid * resid, axis=-1, keepdims=True) + epsilon)
        norm = resid * scale * small[1:2, :]
        low = chosen(first_core, norm[:, :half], norm[:, half:]).astype(jnp.bfloat16)
        high = chosen(first_core, norm[:, half:], norm[:, :half]).astype(jnp.bfloat16)
        norm_own[:, :half] = low
        norm_own[:, half:] = high
        norm_send[:, :half] = high
        norm_send[:, half:] = low


def channel_specs(width):
    steps = width // TILE
    half = width // 2

    def at(j, info):
        return lax.rem(info[0] * (steps // 2) + j, steps)

    thirds = [
        pl.BlockSpec((half, TILE), lambda j, info, k=k: (0, k * steps + at(j, info)))
        for k in range(3)
    ]
    out_own = pl.BlockSpec((TILE, width), lambda j, info: (jnp.minimum(j, steps // 2 - 1), 0))
    out_other = pl.BlockSpec((TILE, width), lambda j, info: (jnp.maximum(j - steps // 2, 0), 0))
    return steps, at, thirds * 2 + [out_own, out_other]


def fixed(*shape):
    return pl.BlockSpec(shape, lambda j, info: (0,) * len(shape))


def conv_forward(info, tokens, before, after, small, keeps, w_in, w_in_other, w_out, w_out_other):
    rows, width = tokens.shape
    ext = rows + HALO
    steps, at, weight_specs = channel_specs(width)
    column = pl.BlockSpec((ext + HALO, TILE), lambda j, info: (0, at(j, info)))
    return pl.pallas_call(
        forward_kernel,
        out_shape=[jax.ShapeDtypeStruct((ext + HALO, width), jnp.float32)] * 3
        + [jax.ShapeDtypeStruct((ext, width), jnp.float32)]
        + [jax.ShapeDtypeStruct((ext, width), jnp.bfloat16)] * 2,
        grid_spec=pltpu.PrefetchScalarGridSpec(
            num_scalar_prefetch=1,
            grid=(steps,),
            in_specs=[
                fixed(rows, width),
                fixed(HALO, width),
                fixed(*after.shape),
                fixed(*small.shape),
                pl.BlockSpec((small.shape[0], TILE), lambda j, info: (0, at(j, info))),
                fixed(*keeps.shape),
            ]
            + weight_specs,
            out_specs=[column] * 3 + [fixed(ext, width)] * 3,
            scratch_shapes=[
                pltpu.VMEM((ext + HALO, width), jnp.bfloat16),
                pltpu.VMEM((width, 3 * TILE), jnp.bfloat16),
                pltpu.VMEM((ext + HALO, TILE), jnp.float32),
                pltpu.VMEM((ext, TILE), jnp.bfloat16),
                pltpu.VMEM((ext, width), jnp.float32),
            ],
        ),
        name="conv_forward",
        **params(),
    )(
        info,
        tokens,
        before,
        after,
        small,
        small,
        keeps,
        *[w_in] * 3,
        *[w_in_other] * 3,
        w_out,
        w_out_other,
    )


def backward_kernel(
    info,
    tokens,
    hidden,
    cotangent,
    after,
    back,
    came,
    small,
    taps,
    keeps,
    b_ref,
    c_ref,
    x_ref,
    own_b,
    own_c,
    own_x,
    other_b,
    other_c,
    other_x,
    out_own,
    out_other,
    input_grad,
    send,
    b_keep,
    out_keep,
    c_keep,
    x_keep,
    vector_keep,
    vectors,
    d_hidden,
    d_branch,
    norm_in,
    d_norm_in,
    weights,
    mixed,
    d_gated,
    along_one,
    along_two,
    d_proj,
):
    step = pl.program_id(0)
    core = info[0]
    first_core = core == 0
    rows, width = tokens.shape
    half = width // 2
    ext = rows + HALO

    def token_norm():
        resid = tokens[...].astype(jnp.float32)
        scale = lax.rsqrt(jnp.mean(resid * resid, axis=-1, keepdims=True) + epsilon)
        return resid * scale, scale

    def back_through(grad, normed, scale, gain):
        inner = grad * gain
        return scale * (inner - normed * jnp.mean(inner * normed, axis=-1, keepdims=True))

    def in_order(own, other):
        return jnp.concatenate(
            [chosen(first_core, own, other), chosen(first_core, other, own)], axis=1
        )

    @pl.when(step == 0)
    def _():
        vectors[...] = jnp.zeros(vectors.shape, jnp.float32)
        grad = in_order(back[:, :half] + came[:, half:], back[:, half:] + came[:, :half])
        resid = hidden[...]
        scale = lax.rsqrt(jnp.mean(resid * resid, axis=-1, keepdims=True) + epsilon)
        normed = resid * scale
        vectors[1:2, :] = jnp.sum(grad[:rows] * normed[:rows], axis=0, keepdims=True)
        result = back_through(grad, normed, scale, small[1:2, :])
        result = result + jnp.concatenate([cotangent[...], after[...]], axis=0).astype(jnp.float32)
        d_hidden[...] = result
        d_branch[...] = result.astype(jnp.bfloat16)
        norm_in[...] = (token_norm()[0] * small[0:1, :]).astype(jnp.bfloat16)
        d_norm_in[...] = jnp.zeros(d_norm_in.shape, jnp.float32)

    here = pl.num_programs(0) // 2

    @pl.when(step < here)
    def _():
        d_gated[...] = dot(d_branch[...], out_own[...], NT)

    @pl.when(step >= here)
    def _():
        d_gated[...] = dot(d_branch[...], out_other[...], NT)

    join_rows(weights, (own_b, own_c, own_x), (other_b, other_c, other_x))
    mixed[...] = b_ref[...] * x_ref[...]
    now, one, two, conv = conv_rows(mixed, keeps[:, 0:1], keeps[:, 1:2], taps, ext)
    c_part = c_ref[pl.ds(HALO, ext), :]
    grad = d_gated[...]
    gated = (c_part[:rows] * conv[:rows]).astype(jnp.bfloat16)
    d_conv = grad * c_part
    block = lax.rem(core * here + step, pl.num_programs(0))
    lanes = pl.ds(pl.multiple_of(block * TILE, TILE), TILE)
    for index, view in enumerate((now, one, two)):
        vectors[2 + index : 3 + index, lanes] = jnp.sum(
            d_conv[:rows] * view[:rows], axis=0, keepdims=True
        )
    along_one[...] = keeps[:, 0:1] * d_conv * taps[3:4, :]
    along_two[...] = keeps[:, 1:2] * d_conv * taps[4:5, :]
    d_mixed = (
        taps[2:3, :] * d_conv[:rows] + along_one[pl.ds(1, rows), :] + along_two[pl.ds(2, rows), :]
    )
    d_proj[:, :TILE] = (d_mixed * x_ref[pl.ds(HALO, rows), :]).astype(jnp.bfloat16)
    d_proj[:, TILE : 2 * TILE] = (grad[:rows] * conv[:rows]).astype(jnp.bfloat16)
    d_proj[:, 2 * TILE :] = (d_mixed * b_ref[pl.ds(HALO, rows), :]).astype(jnp.bfloat16)
    out_grad = dot(gated, d_branch[:rows, :], TN)
    in_grad = dot(norm_in[...], d_proj[...], TN)
    d_norm_in[...] += dot(d_proj[...], weights[...], NT)
    groups, per, _ = send.shape
    few = groups // pl.num_programs(0)

    def divide(value, keep, group, at):
        pair = value.reshape(value.shape[0] // (2 * per), 2, per, value.shape[1]).astype(send.dtype)
        for side in range(2):

            @pl.when(core == side)
            def _():
                send[group, :, at] = pair[:, 1 - side]
                keep[...] = pair[:, side]

    every = slice(None)
    for index, keep in enumerate((b_keep, None, c_keep, x_keep)):
        if keep is None:
            divide(out_grad, out_keep, pl.ds(block * few, few), pl.ds(width, width))
        else:
            third = index and index - 1
            at = pl.multiple_of(index * width + block * TILE, TILE)
            divide(in_grad[:, third * TILE : (third + 1) * TILE], keep, every, pl.ds(at, TILE))

    @pl.when(step == pl.num_programs(0) - 1)
    def _():
        final = in_order(d_norm_in[:, :half], d_norm_in[:, half:])
        normed, scale = token_norm()
        vectors[0:1, :] = jnp.sum(final * normed, axis=0, keepdims=True)
        input_grad[...] = (
            d_hidden[:rows, :] + back_through(final, normed, scale, small[0:1, :])
        ).astype(jnp.bfloat16)
        divide(vectors[...].T, vector_keep, every, pl.ds(4 * width, vectors.shape[0]))


def conv_backward(
    info,
    tokens,
    hidden,
    cotangent,
    after,
    back,
    came,
    small,
    keeps,
    parts,
    w_in,
    w_in_other,
    w_out,
    w_out_other,
    devices,
):
    rows, width = tokens.shape
    ext = rows + HALO
    steps, at, weight_specs = channel_specs(width)
    column = pl.BlockSpec((ext + HALO, TILE), lambda j, info: (0, at(j, info)))
    per = width // devices
    kind = jnp.bfloat16 if per % 16 == 0 else jnp.float32
    groups = devices // 2
    by_columns = pl.BlockSpec((groups, per, TILE), lambda j, info: (0, 0, at(j, info)))
    by_rows = pl.BlockSpec((groups // steps, per, width), lambda j, info: (at(j, info), 0, 0))
    return pl.pallas_call(
        backward_kernel,
        out_shape=[
            jax.ShapeDtypeStruct((rows, width), jnp.bfloat16),
            jax.ShapeDtypeStruct((groups, per, 4 * width + 128), kind),
        ]
        + [jax.ShapeDtypeStruct((groups, per, width), kind)] * 4
        + [jax.ShapeDtypeStruct((groups, per, 128), kind)],
        grid_spec=pltpu.PrefetchScalarGridSpec(
            num_scalar_prefetch=1,
            grid=(steps,),
            in_specs=[
                fixed(rows, width),
                fixed(ext, width),
                fixed(rows, width),
                pl.BlockSpec((HALO, width), lambda j, info: (0, 1)),
                fixed(ext, width),
                fixed(ext, width),
                fixed(*small.shape),
                pl.BlockSpec((small.shape[0], TILE), lambda j, info: (0, at(j, info))),
                fixed(*keeps.shape),
            ]
            + [column] * 3
            + weight_specs,
            out_specs=[
                fixed(rows, width),
                fixed(groups, per, 4 * width + 128),
                by_columns,
                by_rows,
                by_columns,
                by_columns,
                fixed(groups, per, 128),
            ],
            scratch_shapes=[
                pltpu.VMEM((128, width), jnp.float32),
                pltpu.VMEM((ext, width), jnp.float32),
                pltpu.VMEM((ext, width), jnp.bfloat16),
                pltpu.VMEM((rows, width), jnp.bfloat16),
                pltpu.VMEM((rows, width), jnp.float32),
                pltpu.VMEM((width, 3 * TILE), jnp.bfloat16),
                pltpu.VMEM((ext + HALO, TILE), jnp.float32),
                pltpu.VMEM((ext, TILE), jnp.float32),
                pltpu.VMEM((ext, TILE), jnp.float32),
                pltpu.VMEM((ext, TILE), jnp.float32),
                pltpu.VMEM((rows, 3 * TILE), jnp.bfloat16),
            ],
        ),
        name="conv_backward",
        **params(),
    )(
        info,
        tokens,
        hidden,
        cotangent,
        after,
        back,
        came,
        small,
        small,
        keeps,
        *parts,
        *[w_in] * 3,
        *[w_in_other] * 3,
        w_out,
        w_out_other,
    )


def ffn_kernel(
    pieces,
    split,
    info,
    n_own,
    n_other,
    g_own,
    g_after,
    g_other,
    g_other_after,
    gate_own,
    gate_other,
    up_own,
    up_other,
    down_ref,
    act_ref,
    back_keep,
    back_send,
    gate_send,
    gate_keep,
    up_send,
    up_keep,
    whole,
    n_all,
    g_all,
    back,
    weights,
    grads,
):
    step = pl.program_id(0)
    rows = n_all.shape[0]
    block = g_own.shape[0]
    real = 2 * block
    tile = down_ref.shape[0]
    places = (
        (pl.ds(0, block), 0, pl.ds(0, block), g_own),
        (pl.ds(real, HALO), 0, pl.ds(block, HALO), g_after),
        (pl.ds(block, block), 1, pl.ds(0, block), g_other),
        (pl.ds(real + HALO, HALO), 1, pl.ds(block, HALO), g_other_after),
    )

    @pl.when(step == 0)
    def _():
        back[...] = jnp.zeros(back.shape, jnp.float32)
        for place, which, source, grad in places:
            n_all[place, :] = (n_own, n_other)[which][source, :]
            g_all[place, :] = grad[...]

    join_rows(weights, (gate_own, up_own), (gate_other, up_other))
    size = -(-rows // pieces // 16) * 16
    for start in range(0, rows, size):
        part = pl.ds(start, min(size, rows - start))
        proj = dot(n_all[part, :], weights[...], NN)
        d_act = dot(g_all[part, :], down_ref[...], NT)
        gate = proj[:, :tile]
        up_val = proj[:, tile:]
        sigma = 0.5 * jnp.tanh(0.5 * gate) + 0.5
        silu = gate * sigma
        act_ref[part, :] = (silu * up_val).astype(jnp.bfloat16)
        grads[part, tile:] = (d_act * silu).astype(jnp.bfloat16)
        grads[part, :tile] = (d_act * up_val * (sigma + silu * (1.0 - sigma))).astype(jnp.bfloat16)
        back[part, :] += dot(grads[part, :], weights[...], NT)
    summed = dot(n_all[:real, :], grads[:real, :], TN).astype(jnp.bfloat16)
    half = summed.shape[0] // 2
    for core in range(2):

        @pl.when(jnp.logical_and(step >= split, info[0] == core))
        def _():
            whole[:half, :] = summed[core * half : (core + 1) * half, :]
            whole[half:, :] = summed[(1 - core) * half : (2 - core) * half, :]

    for index, (send, keep) in enumerate(((gate_send, gate_keep), (up_send, up_keep))):
        groups, per, columns = send.shape
        pair = summed[:, index * tile : (index + 1) * tile].reshape(groups, 2, per, columns)
        for value in range(2):

            @pl.when(jnp.logical_and(step < split, info[1 + index] == value))
            def _():
                send[...] = pair[:, 1 - value]
                keep[...] = pair[:, value]

    @pl.when(step == pl.num_programs(0) - 1)
    def _():
        for place, which, source, _ in places:
            (back_keep, back_send)[which][source, :] = back[place, :]


def ffn(info, norms, grads, weights, down, split, pers):
    ext, width = norms[0].shape
    rows = 2 * ext
    half = width // 2
    count = down.shape[0] // TILE
    column = pl.BlockSpec((half, TILE), lambda j, info: (0, info[0] * count + j))
    shapes = [jax.ShapeDtypeStruct((rows, count * TILE), jnp.bfloat16)]
    specs = [pl.BlockSpec((rows, TILE), lambda j, info: (0, j))]
    for _ in range(2):
        shapes.append(jax.ShapeDtypeStruct((ext, width), jnp.float32))
        specs.append(fixed(ext, width))
    for per in pers:
        for _ in range(2):
            groups = width // (2 * per)
            shapes.append(jax.ShapeDtypeStruct((groups, per, split * TILE), jnp.bfloat16))
            specs.append(
                pl.BlockSpec(
                    (groups, per, TILE), lambda j, info: (0, 0, jnp.minimum(j, split - 1))
                )
            )
    shapes.append(jax.ShapeDtypeStruct((width, 2 * (count - split) * TILE), jnp.bfloat16))
    specs.append(pl.BlockSpec((width, 2 * TILE), lambda j, info: (0, jnp.maximum(j - split, 0))))
    after = pl.BlockSpec((HALO, width), lambda j, info: (0, 1))
    return pl.pallas_call(
        functools.partial(ffn_kernel, 2, split),
        out_shape=shapes,
        grid_spec=pltpu.PrefetchScalarGridSpec(
            num_scalar_prefetch=1,
            grid=(count,),
            in_specs=[fixed(ext, width)] * 2
            + [fixed(ext - HALO, width), after] * 2
            + [column] * 4
            + [pl.BlockSpec((TILE, width), lambda j, info: (j, 0))],
            out_specs=specs,
            scratch_shapes=[
                pltpu.VMEM((rows, width), jnp.bfloat16),
                pltpu.VMEM((rows, width), jnp.bfloat16),
                pltpu.VMEM((rows, width), jnp.float32),
                pltpu.VMEM((width, 2 * TILE), jnp.bfloat16),
                pltpu.VMEM((rows, 2 * TILE), jnp.bfloat16),
            ],
        ),
        name="ffn",
        **params(),
    )(info, *norms, *grads, *weights, down)


def down_kernel(
    info,
    act,
    g_own,
    g_other,
    down_ref,
    out_keep,
    out_send,
    low_send,
    low_keep,
    high_send,
    high_keep,
    rhs,
    grad,
):
    step = pl.program_id(0)
    block = out_keep.shape[0]
    real = 2 * block
    rhs[:block, :] = g_own[...]
    rhs[block:, :] = g_other[...]
    result = dot(act[:real, :], down_ref[...], NN)
    out_keep[...] = result[:block]
    out_send[...] = result[block:]
    grad[...] = dot(act[:real, :], rhs[...], TN).astype(grad.dtype)
    here = pl.num_programs(0) // 2
    outs = ((step < here, low_send, low_keep, info[1]), (step >= here, high_send, high_keep, info[2]))
    for now, send, keep, mine in outs:
        groups, per, _ = send.shape
        for value in range(2):

            @pl.when(jnp.logical_and(now, mine == value))
            def _():
                for group in range(groups):
                    start = 2 * group * per
                    send[group] = grad[pl.ds(start + (1 - value) * per, per), :]
                    keep[group] = grad[pl.ds(start + value * per, per), :]


def down_part(info, act, g_own, g_other, down, pers):
    hidden, width = down.shape
    steps = width // TILE
    here = steps // 2
    block = g_own.shape[0]
    kind = jnp.bfloat16 if min(pers) % 16 == 0 else jnp.float32
    tile = pl.BlockSpec((block, TILE), lambda j, info: (0, j))
    shapes = [jax.ShapeDtypeStruct((block, width), jnp.float32)] * 2
    specs = [tile] * 2
    for index, per in enumerate(pers):
        groups = hidden // (2 * per)
        for _ in range(2):
            shapes.append(jax.ShapeDtypeStruct((groups, per, width // 2), kind))
            if index == 0:
                specs.append(
                    pl.BlockSpec(
                        (groups, per, TILE), lambda j, info: (0, 0, jnp.minimum(j, here - 1))
                    )
                )
            else:
                specs.append(
                    pl.BlockSpec((groups, per, TILE), lambda j, info: (0, 0, jnp.maximum(j - here, 0)))
                )
    return pl.pallas_call(
        down_kernel,
        out_shape=shapes,
        grid_spec=pltpu.PrefetchScalarGridSpec(
            num_scalar_prefetch=1,
            grid=(steps,),
            in_specs=[
                fixed(*act.shape),
                tile,
                tile,
                pl.BlockSpec((hidden, TILE), lambda j, info: (0, j)),
            ],
            out_specs=specs,
            scratch_shapes=[
                pltpu.VMEM((2 * block, TILE), jnp.bfloat16),
                pltpu.VMEM((hidden, TILE), kind),
            ],
        ),
        name="down",
        **params(),
    )(info, act, g_own, g_other, down)


def combine_kernel(plan, info, *refs):
    refs = list(refs)
    inputs = [[[refs.pop(0) for _ in range(count)] for count in counts] for counts in plan]
    for members, out in zip(inputs, refs):
        edge = 0
        for terms in members:
            size = terms[0].shape[-1]
            value = terms[0][...].astype(jnp.float32)
            for term in terms[1:]:
                value = value + term[...].astype(jnp.float32)
            out[..., edge : edge + size] = value.reshape(out.shape[:-1] + (size,)).astype(out.dtype)
            edge += size


def combine(info, slots, jobs, flip=False):
    plan, arrays, specs, shapes, out_specs = [], [], [], [], []
    lefts = []
    for bit, members in jobs:
        common = members[0][0][1]
        for terms in members:
            for _, names, _, _ in terms:
                common = [name for name in common if name in names]
        lefts.append([name for name in common if name != bit])
    gridded = all(lefts)
    for (bit, members), left in zip(jobs, lefts):
        for terms in members:
            for array, names, block, size in terms:
                rows = array.size // array.shape[-1] >> len(names)
                arrays.append(array.reshape([2] * len(names) + [rows, array.shape[-1]]))
                shape, picks = [], []
                for name in names:
                    if name == bit:
                        shape.append(None)
                        picks.append(("other", slots[name]))
                    elif name not in left:
                        shape.append(None)
                        picks.append(("mine", slots[name]))
                    elif gridded and name == left[0]:
                        shape.append(None)
                        picks.append(("step", 0))
                    else:
                        shape.append(2)
                        picks.append(("all", 0))

                def index_map(j, info, picks=picks, block=block):
                    where = []
                    for kind, slot in picks:
                        if kind == "all":
                            where.append(0)
                        elif kind == "step":
                            where.append(lax.rem(j + info[0], 2) if flip else j)
                        else:
                            where.append(info[slot] if kind == "mine" else 1 - info[slot])
                    return (*where, 0, block)

                specs.append(pl.BlockSpec((*shape, rows, size), index_map))
        width = sum(terms[0][3] for terms in members)
        kind = jnp.bfloat16 if rows % 16 == 0 else jnp.float32
        outer = 1 << len(left)
        shapes.append(jax.ShapeDtypeStruct((outer, rows, width), kind))
        inner = outer // 2 if gridded else outer
        out_specs.append(pl.BlockSpec((inner, rows, width), lambda j, info: (j, 0, 0)))
        plan.append([len(terms) for terms in members])
    results = pl.pallas_call(
        functools.partial(combine_kernel, plan),
        out_shape=shapes,
        grid_spec=pltpu.PrefetchScalarGridSpec(
            num_scalar_prefetch=1,
            grid=(2 if gridded else 1,),
            in_specs=specs,
            out_specs=out_specs,
        ),
        name="combine",
        **params(),
    )(info, *arrays)
    return list(zip(results, lefts))


def finish_kernel(counts, tiles, info, *refs):
    *inputs, mine, send, scratch = refs
    place = 0
    for count in counts:
        value = inputs[0][...].astype(jnp.float32)
        for term in inputs[1:count]:
            value = value + term[...].astype(jnp.float32)
        inputs = inputs[count:]
        for tile in range(value.shape[1] // TILE):
            start = tiles[place] * TILE
            scratch[:, start : start + TILE] = value[:, tile * TILE : (tile + 1) * TILE]
            place += 1
    rows = mine.shape[0]
    for side, out in ((info[0], mine), (1 - info[0], send)):
        out[...] = scratch[pl.ds(pl.multiple_of(side * rows, rows), rows), :]


def picked(slots, terms):
    arrays, specs = [], []
    for array, names, block, size in terms:
        rows = array.size // array.shape[-1] >> len(names)
        arrays.append(array.reshape([2] * len(names) + [rows, array.shape[-1]]))
        specs.append(
            pl.BlockSpec(
                (*[None] * len(names), rows, size),
                lambda j, info, names=names, block=block: (
                    *[info[slots[name]] for name in names],
                    0,
                    block,
                ),
            )
        )
    return arrays, specs


def settle_kernel(plan, info, *refs):
    refs = list(refs)
    inputs = [[[refs.pop(0) for _ in range(count)] for count in counts] for counts, _ in plan]
    for members, (_, kinds) in zip(inputs, plan):
        if kinds is None:
            rows = members[0][0].shape[0]
            value = members[0][0][...].astype(jnp.float32)
            for term in members[0][1:]:
                value = value + term[...].astype(jnp.float32)
            across_rows = lax.broadcasted_iota(jnp.int32, (rows, rows), 0)
            across_columns = lax.broadcasted_iota(jnp.int32, (rows, rows), 1)
            for column in range(2):
                diagonal = jnp.where(
                    across_rows == across_columns, value[:, column : column + 1], 0.0
                )
                refs.pop(0)[...] = jnp.sum(diagonal, axis=0, keepdims=True)
            refs.pop(0)[...] = value[:, 2:5]
            continue
        outs = [refs.pop(0) for _ in kinds]
        edge = 0
        for terms in members:
            size = terms[0].shape[-1]
            value = terms[0][...].astype(jnp.float32)
            for term in terms[1:]:
                value = value + term[...].astype(jnp.float32)
            for out in outs:
                out[:, edge : edge + size] = value.astype(out.dtype)
            edge += size


def settle(info, slots, groups):
    arrays, specs, shapes, plan = [], [], [], []
    for members, kinds in groups:
        for terms in members:
            views, view_specs = picked(slots, terms)
            arrays += views
            specs += view_specs
        rows = views[0].shape[-2]
        width = sum(terms[0][3] for terms in members)
        if kinds is None:
            shapes += [jax.ShapeDtypeStruct((1, rows), jnp.float32)] * 2
            shapes.append(jax.ShapeDtypeStruct((rows, 3), jnp.float32))
        else:
            shapes += [jax.ShapeDtypeStruct((rows, width), kind) for kind in kinds]
        plan.append(([len(terms) for terms in members], kinds))
    return pl.pallas_call(
        functools.partial(settle_kernel, plan),
        out_shape=shapes,
        grid_spec=pltpu.PrefetchScalarGridSpec(
            num_scalar_prefetch=1,
            grid=(1,),
            in_specs=specs,
            out_specs=[fixed(*shape.shape) for shape in shapes],
        ),
        name="settle",
        **params(),
    )(info, *arrays)


def finish(info, slots, members, tiles):
    columns = len(tiles) * TILE
    arrays, specs = [], []
    for terms in members:
        views, view_specs = picked(slots, terms)
        rows = views[0].shape[-2]
        arrays += views
        specs += view_specs
    return pl.pallas_call(
        functools.partial(finish_kernel, [len(terms) for terms in members], tiles),
        out_shape=[jax.ShapeDtypeStruct((rows // 2, columns), jnp.float32)] * 2,
        grid_spec=pltpu.PrefetchScalarGridSpec(
            num_scalar_prefetch=1,
            grid=(1,),
            in_specs=specs,
            out_specs=[fixed(rows // 2, columns)] * 2,
            scratch_shapes=[pltpu.VMEM((rows, columns), jnp.float32)],
        ),
        name="finish",
        **params(),
    )(info, *arrays)


def local(
    tokens,
    cotangent,
    doc_lengths,
    norm_gain,
    in_weight,
    conv_taps,
    out_weight,
    ffn_gain,
    gate_weight,
    up_weight,
    down_weight,
):
    rows, width = tokens.shape
    hidden = down_weight.shape[0]
    chips = lax.axis_size("seq")
    top = chips.bit_length() - 2
    lower = list(range(top))
    bits = list(range(top, -1, -1))
    chip = lax.axis_index("seq")
    core = lax.axis_index("wa")
    coords = {bit: (chip >> bit) & 1 for bit in range(top + 1)}
    turned = dict(coords)
    turned[top] = coords[top] ^ core
    ordering = lax.optimization_barrier

    def after(value, *gates):
        return ordering((value, gates))[0]

    def ordered(low, high):
        return jnp.where(core == 0, low, high)

    def both(own, other, axis):
        return ordered(
            jnp.concatenate([own, other], axis=axis), jnp.concatenate([other, own], axis=axis)
        )

    w_in_other = partner(in_weight)
    w_out_other = partner(out_weight)
    small = jnp.concatenate([norm_gain[None], ffn_gain[None], conv_taps.T], axis=0)
    small = jnp.pad(small, ((0, 3), (0, 0)))
    small_other = partner(small)
    before_rows = shifted(tokens[rows - HALO :], 1)
    after_rows = shifted(jnp.concatenate([tokens[:HALO], cotangent[:HALO]], axis=1), -1)
    cot_other = partner(cotangent)
    after_other = partner(after_rows)
    early = (w_in_other, w_out_other, small_other, before_rows, cot_other, after_other)
    w_in_other, w_out_other, small_other, before_rows, cot_other, after_other = ordering(early)
    small = both(small, small_other, 1).astype(jnp.float32)
    gate_late, up_late = after((gate_weight, up_weight), early)
    gate_other = partner(gate_late)
    up_other = partner(up_late)

    place = lax.axis_index(AXES) * rows + jnp.arange(rows + HALO, dtype=jnp.int32)
    earlier = jnp.arange(doc_lengths.shape[0])
    earlier = earlier[:, None] < earlier[None, :]
    starts = jnp.sum(jnp.where(earlier, doc_lengths[:, None], 0), axis=0)
    first = jnp.any(place[:, None] == starts[None, :], axis=1)
    before = jnp.any((place - 1)[:, None] == starts[None, :], axis=1)
    keep_one = jnp.where(first, 0.0, 1.0)
    keep_two = jnp.where(jnp.logical_or(first, before), 0.0, 1.0)
    lane = lax.broadcasted_iota(jnp.int32, (rows + HALO, 128), 1)
    keeps = jnp.where(lane == 0, keep_one[:, None], keep_two[:, None]).astype(jnp.float32)
    info = [core] + [coords[bit] for bit in lower] + [coords[top], turned[top]]
    info = jnp.stack(info).astype(jnp.int32)

    *parts, hidden_res, norm_own, norm_send = conv_forward(
        info,
        tokens,
        before_rows,
        after_rows,
        small,
        keeps,
        in_weight,
        w_in_other,
        out_weight,
        w_out_other,
    )
    norm_other = partner(norm_send)
    norm_own, gate_other, up_other = ordering((norm_own, gate_other, up_other))
    per_chip = width // chips
    pers = (per_chip << lower[0], per_chip << lower[1])
    tiles = hidden // TILE
    split = tiles * 4 // 9
    counts = (split, tiles - split)
    orders = (lower, [lower[1], lower[0]] + lower[2:])

    act, back_keep, back_send, *one, whole = ffn(
        info,
        (norm_own, norm_other),
        (cotangent, after_rows, cot_other, after_other),
        (gate_weight, gate_other, up_weight, up_other),
        down_weight,
        split,
        pers,
    )
    one_x = across(one[0], orders[0][0])
    one_y = across(one[2], orders[1][0])
    came = partner(back_send)

    groups = [
        [low + (level << (top - 1)) for level in range(4)] for low in range(1 << (top - 1))
    ]
    quarter = lax.psum_scatter(
        whole, "seq", scatter_dimension=0, axis_index_groups=groups, tiled=True
    )

    slots = {bit: 1 + bit for bit in bits}
    turned_slots = dict(slots)
    turned_slots[top] = 2 + top

    def plain(array, names):
        return (array, names, 0, array.shape[-1])

    def gated(streams, *gates):
        held = after([terms[-1][0] for terms in streams], gates)
        return [
            terms[:-1] + [(array, *terms[-1][1:])] for terms, array in zip(streams, held)
        ]

    def without(names, *taken):
        return [name for name in names if name not in taken]

    def send_on(streams, names, use=slots):
        results = combine(info, use, streams)
        return [send for send, _ in results], [
            (across(send, bit), left) for (bit, _), (send, left) in zip(streams, results)
        ]

    def upper_sum(value):
        value = value.reshape(-1, value.shape[-1])
        return lax.psum_scatter(
            value, "seq", scatter_dimension=0, axis_index_groups=groups, tiled=True
        )

    down_pers = [2 * hidden // chips << bit for bit in (lower[0], lower[1])]
    out_keep, out_send, *down_halves = down_part(
        info, act, cotangent, cot_other, down_weight, down_pers
    )
    came, out_send, down_halves, one_x, one_y = ordering(
        (came, out_send, down_halves, one_x, one_y)
    )

    down_x = across(down_halves[0], orders[0][0])
    down_y = across(down_halves[2], orders[1][0])
    out_came = partner(out_send)
    one_terms = [
        [plain(keep, without(bits, order[0])), plain(got, without(bits, order[0]))]
        for keep, got, order in ((one[1], one_x, orders[0]), (one[3], one_y, orders[1]))
    ]
    one_sent, one_got = send_on(
        [(order[1], [terms]) for terms, order in zip(one_terms, orders)], bits, turned_slots
    )
    one_got = [got for got, _ in one_got]
    came = after(came, one_sent)

    def side_by_side(streams, order, use=slots):
        sent = None
        for bit in order:
            sent, ((got, left),) = send_on([(bit, streams)], None, use)
            edge, members = 0, []
            for terms in streams:
                size = terms[0][3]
                members.append(terms + [(got, left, edge, size)])
                edge += size
            for terms in members:
                array, left, edge, size = terms[-1]
                if edge % size:
                    array, edge = array[..., edge : edge + size], 0
                terms[-1] = (array, left, edge // size, size)
            streams = members
        return sent, streams

    input_grad, conv_send, *conv_keeps = conv_backward(
        info,
        tokens,
        hidden_res,
        cotangent,
        after_rows,
        back_keep,
        came,
        small,
        keeps,
        parts,
        in_weight,
        w_in_other,
        out_weight,
        w_out_other,
        2 * chips,
    )
    conv_send, conv_keeps, down_x, down_y, out_came = ordering(
        (conv_send, conv_keeps, down_x, down_y, out_came)
    )
    conv_came = partner(conv_send)

    down_bits = bits[1:]
    down_terms = [
        [plain(keep, without(down_bits, order[0])), plain(got, without(down_bits, order[0]))]
        for keep, got, order in (
            (down_halves[1], down_x, orders[0]),
            (down_halves[3], down_y, orders[1]),
        )
    ]
    down_sent, down_got = send_on(
        [(order[1], [terms]) for terms, order in zip(down_terms, orders)], down_bits
    )
    down_got = [got for got, _ in down_got]

    conv_came = after(conv_came, down_sent)
    conv_members = [
        [
            [plain(conv_keeps[member], bits), (conv_came, bits, member * width // size, size)]
            for member, size in members
        ]
        for members in (((0, width), (1, width)), ((2, width), (3, width), (4, 128)))
    ]
    conv_sent, conv_got = send_on(
        [(order[0], members) for members, order in zip(conv_members, orders)], bits
    )
    conv_got = [got for got, _ in conv_got]

    one_got = after(one_got, conv_sent)
    one_streams = [
        terms + [plain(got, without(bits, *order[:2]))]
        for terms, got, order in zip(one_terms, one_got, orders)
    ]
    _, one_streams = side_by_side(one_streams, lower[2 : top - 1], turned_slots)
    ((one_all, _),) = combine(info, turned_slots, [(None, one_streams)], flip=True)
    one_done = upper_sum(one_all)

    down_got = after(down_got, one_all)
    down_streams = [
        terms + [plain(got, without(down_bits, *order[:2]))]
        for terms, got, order in zip(down_terms, down_got, orders)
    ]
    down_sent, down_streams = side_by_side(down_streams, lower[2:])

    down_streams = gated(down_streams, down_sent)
    part, down_last = settle(info, slots, [(down_streams, (jnp.float32, jnp.bfloat16))])
    pairs = [
        (source * 2 + side, (source ^ (1 << top)) * 2 + side)
        for source in range(chips)
        for side in range(2)
        if (source >> top) & 1 != side
    ]
    down_far = lax.ppermute(down_last, AXES, pairs)

    conv_got = after(conv_got, down_last)
    for index, (members, order) in enumerate(zip(conv_members, orders)):
        edge = 0
        for terms in members:
            size = terms[0][3]
            terms.append((conv_got[index], without(bits, order[0]), edge // size, size))
            edge += size
    conv_sent, conv_two = send_on(
        [(order[1], members) for members, order in zip(conv_members, orders)], bits
    )
    conv_two = [got for got, _ in conv_two]

    quarter = after(quarter, conv_sent)
    edge = counts[1] * TILE
    two_terms = [[(quarter, bits[2:], block, edge)] for block in range(2)]
    two_sent, two_got = send_on(
        [(order[0], [terms]) for terms, order in zip(two_terms, orders)], bits[2:]
    )
    two_got = [got for got, _ in two_got]
    out_came = after(out_came, two_sent)
    block_out = (hidden_res[:rows] + out_keep + out_came).astype(jnp.bfloat16)
    conv_two = after(conv_two, two_sent, block_out)
    conv_streams = []
    for members, got, order in zip(conv_members, conv_two, orders):
        edge = 0
        for terms in members:
            size = terms[0][3]
            conv_streams.append(terms + [(got, without(bits, *order[:2]), edge // size, size)])
            edge += size
    _, conv_streams = side_by_side(conv_streams, lower[2 : top - 1])
    ((conv_all, _),) = combine(info, slots, [(None, conv_streams)])
    conv_done = upper_sum(conv_all)
    two_got = after(two_got, conv_all)
    two_terms = [
        terms + [plain(got, without(bits[2:], order[0]))]
        for terms, got, order in zip(two_terms, two_got, orders)
    ]
    two_sent, two_got = send_on(
        [(order[1], [terms]) for terms, order in zip(two_terms, orders)], bits[2:]
    )
    two_streams = [terms + [plain(*got)] for terms, got in zip(two_terms, two_got)]
    _, two_streams = side_by_side(two_streams, lower[2 : top - 1])

    part, down_far = after((part, down_far), conv_all)
    part = part + down_far.astype(jnp.float32)
    part = part.reshape(2, -1, width)
    down_out = jnp.where(
        coords[top] == core, take(part, core, 0), partner(take(part, 1 - core, 0))
    )
    b_out, out_out, c_out, x_out, vectors = (
        [(conv_done, [], member * width // size, size)]
        for member, size in enumerate([width] * 4 + [128])
    )
    in_out, out_out, gain_one_out, gain_two_out, taps_out = settle(
        info,
        slots,
        [
            ([b_out, c_out, x_out], (jnp.float32,)),
            ([out_out], (jnp.float32,)),
            ([vectors], None),
        ],
    )

    gate_tiles = [tile for tile in range(counts[0])] + [tiles + tile for tile in range(counts[0])]
    for tile in range(counts[1]):
        gate_tiles += [counts[0] + tile, tiles + counts[0] + tile]
    kept, send = finish(info, slots, [[plain(one_done, [])]] + two_streams, gate_tiles)
    other = partner(send)
    gate_out = both(kept[:, :hidden], other[:, :hidden], 1)
    up_out = both(kept[:, hidden:], other[:, hidden:], 1)
    return (
        block_out,
        input_grad,
        gain_one_out.reshape(-1),
        in_out,
        taps_out,
        out_out,
        gain_two_out.reshape(-1),
        gate_out,
        up_out,
        down_out,
    )


def solution(mesh):
    placed = (
        P(AXES, None),
        P(AXES, None),
        P(),
        P("wa"),
        P("wa", None),
        P("wa", None),
        P("wa", None),
        P("wa"),
        P("wa", None),
        P("wa", None),
        P("wa", None),
    )
    return jax.shard_map(
        local,
        mesh=mesh,
        in_specs=placed,
        out_specs=(
            P(AXES, None),
            P(AXES, None),
            P(AXES),
            P(AXES, None),
            P(AXES, None),
            P(AXES, None),
            P(AXES),
            P(AXES, None),
            P(AXES, None),
            P(AXES, None),
        ),
        check_vma=False,
    )
```

```python
import functools
import math

import jax
import jax.numpy as jnp
from jax import lax
from jax.experimental import pallas as pl
from jax.experimental.pallas import tpu as pltpu
from jax.sharding import PartitionSpec as P

epsilon = 1e-05
AXES = ("seq", "wa")
HALO = 16
TILE = 256
VMEM_LIMIT = 63 * 2**20
NN = ((1,), (0,))
NT = ((1,), (1,))
TN = ((0,), (0,))


def shifted(value, steps):
    count = lax.axis_size(AXES)
    first, last = (max(0, -steps), min(count, count - steps))
    return lax.ppermute(value, AXES, [(source, source + steps) for source in range(first, last)])


def partner(value):
    return lax.ppermute(value, "wa", [(0, 1), (1, 0)])


def across(value, bit):
    count = lax.axis_size("seq")
    return lax.ppermute(value, "seq", [(place, place ^ (1 << bit)) for place in range(count)])


def dot(left, right, dims):
    return lax.dot_general(left, right, (dims, ((), ())), preferred_element_type=jnp.float32)


def take(value, index, axis):
    return lax.dynamic_index_in_dim(value, index, axis, keepdims=False)


def total(terms):
    result = terms[0].astype(jnp.float32)
    for term in terms[1:]:
        result = result + term.astype(jnp.float32)
    return result


def chosen(test, value, other):
    return jnp.where(test, value, other)


def swapped(value):
    half = value.shape[1] // 2
    return jnp.concatenate([value[:, half:], value[:, :half]], axis=1)


def params(**extra):
    return dict(
        compiler_params=pltpu.CompilerParams(vmem_limit_bytes=VMEM_LIMIT),
        cost_estimate=pl.CostEstimate(flops=1000, bytes_accessed=1000, transcendentals=0),
        **extra,
    )


def conv_rows(mixed, keep_one, keep_two, taps, count):
    now = mixed[pl.ds(HALO, count), :]
    one = mixed[pl.ds(HALO - 1, count), :] * keep_one
    two = mixed[pl.ds(HALO - 2, count), :] * keep_two
    conv = taps[2:3, :] * now + taps[3:4, :] * one + taps[4:5, :] * two
    return now, one, two, conv


def join_rows(weights, own, other):
    half = own[0].shape[0]
    for index, (upper, lower) in enumerate(zip(own, other)):
        weights[:half, index * TILE : (index + 1) * TILE] = upper[...]
        weights[half:, index * TILE : (index + 1) * TILE] = lower[...]


def forward_kernel(
    info,
    tokens,
    before,
    after,
    small,
    taps,
    keeps,
    own_b,
    own_c,
    own_x,
    other_b,
    other_c,
    other_x,
    out_own,
    out_other,
    b_ref,
    c_ref,
    x_ref,
    hidden,
    norm_own,
    norm_send,
    normed,
    weights,
    mixed,
    gated,
    total_ref,
):
    step = pl.program_id(0)
    first_core = info[0] == 0
    rows, width = tokens.shape
    half = width // 2
    ext = rows + HALO

    @pl.when(step == 0)
    def _():
        for start, ref in ((0, before), (HALO, tokens), (HALO + rows, after)):
            resid = ref[:, :width].astype(jnp.float32)
            scale = lax.rsqrt(jnp.mean(resid * resid, axis=-1, keepdims=True) + epsilon)
            norm = resid * scale * small[0:1, :]
            place = pl.ds(start, ref.shape[0])
            normed[place, :half] = chosen(first_core, norm[:, :half], norm[:, half:]).astype(
                jnp.bfloat16
            )
            normed[place, half:] = chosen(first_core, norm[:, half:], norm[:, :half]).astype(
                jnp.bfloat16
            )
        total_ref[:rows, :] = tokens[...].astype(jnp.float32)
        total_ref[rows:, :] = after[:, :width].astype(jnp.float32)

    join_rows(weights, (own_b, own_c, own_x), (other_b, other_c, other_x))
    proj = dot(normed[...], weights[...], NN)
    b_part, c_part, x_part = proj[:, :TILE], proj[:, TILE : 2 * TILE], proj[:, 2 * TILE :]
    b_ref[...] = b_part
    c_ref[...] = c_part
    x_ref[...] = x_part
    mixed[...] = b_part * x_part
    conv = conv_rows(mixed, keeps[:, 0:1], keeps[:, 1:2], taps, ext)[3]
    gated[...] = (c_ref[pl.ds(HALO, ext), :] * conv).astype(jnp.bfloat16)
    here = pl.num_programs(0) // 2

    @pl.when(step < here)
    def _():
        total_ref[...] += dot(gated[...], out_own[...], NN)

    @pl.when(step >= here)
    def _():
        total_ref[...] += dot(gated[...], out_other[...], NN)

    @pl.when(step == pl.num_programs(0) - 1)
    def _():
        resid = total_ref[...]
        hidden[...] = resid
        scale = lax.rsqrt(jnp.mean(resid * resid, axis=-1, keepdims=True) + epsilon)
        norm = resid * scale * small[1:2, :]
        low = chosen(first_core, norm[:, :half], norm[:, half:]).astype(jnp.bfloat16)
        high = chosen(first_core, norm[:, half:], norm[:, :half]).astype(jnp.bfloat16)
        norm_own[:, :half] = low
        norm_own[:, half:] = high
        norm_send[:, :half] = high
        norm_send[:, half:] = low


def channel_specs(width):
    steps = width // TILE
    half = width // 2

    def at(j, info):
        return lax.rem(info[0] * (steps // 2) + j, steps)

    thirds = [
        pl.BlockSpec((half, TILE), lambda j, info, k=k: (0, k * steps + at(j, info)))
        for k in range(3)
    ]
    out_own = pl.BlockSpec((TILE, width), lambda j, info: (jnp.minimum(j, steps // 2 - 1), 0))
    out_other = pl.BlockSpec((TILE, width), lambda j, info: (jnp.maximum(j - steps // 2, 0), 0))
    return steps, at, thirds * 2 + [out_own, out_other]


def fixed(*shape):
    return pl.BlockSpec(shape, lambda j, info: (0,) * len(shape))


def conv_forward(info, tokens, before, after, small, keeps, w_in, w_in_other, w_out, w_out_other):
    rows, width = tokens.shape
    ext = rows + HALO
    steps, at, weight_specs = channel_specs(width)
    column = pl.BlockSpec((ext + HALO, TILE), lambda j, info: (0, at(j, info)))
    return pl.pallas_call(
        forward_kernel,
        out_shape=[jax.ShapeDtypeStruct((ext + HALO, width), jnp.float32)] * 3
        + [jax.ShapeDtypeStruct((ext, width), jnp.float32)]
        + [jax.ShapeDtypeStruct((ext, width), jnp.bfloat16)] * 2,
        grid_spec=pltpu.PrefetchScalarGridSpec(
            num_scalar_prefetch=1,
            grid=(steps,),
            in_specs=[
                fixed(rows, width),
                fixed(HALO, width),
                fixed(*after.shape),
                fixed(*small.shape),
                pl.BlockSpec((small.shape[0], TILE), lambda j, info: (0, at(j, info))),
                fixed(*keeps.shape),
            ]
            + weight_specs,
            out_specs=[column] * 3 + [fixed(ext, width)] * 3,
            scratch_shapes=[
                pltpu.VMEM((ext + HALO, width), jnp.bfloat16),
                pltpu.VMEM((width, 3 * TILE), jnp.bfloat16),
                pltpu.VMEM((ext + HALO, TILE), jnp.float32),
                pltpu.VMEM((ext, TILE), jnp.bfloat16),
                pltpu.VMEM((ext, width), jnp.float32),
            ],
        ),
        name="conv_forward",
        **params(),
    )(
        info,
        tokens,
        before,
        after,
        small,
        small,
        keeps,
        *[w_in] * 3,
        *[w_in_other] * 3,
        w_out,
        w_out_other,
    )


def backward_kernel(
    info,
    tokens,
    hidden,
    cotangent,
    after,
    back,
    came,
    small,
    taps,
    keeps,
    b_ref,
    c_ref,
    x_ref,
    own_b,
    own_c,
    own_x,
    other_b,
    other_c,
    other_x,
    out_own,
    out_other,
    input_grad,
    send,
    b_keep,
    out_keep,
    c_keep,
    x_keep,
    vector_keep,
    vectors,
    d_hidden,
    d_branch,
    norm_in,
    d_norm_in,
    weights,
    mixed,
    d_gated,
    along_one,
    along_two,
    d_proj,
):
    step = pl.program_id(0)
    core = info[0]
    first_core = core == 0
    rows, width = tokens.shape
    half = width // 2
    ext = rows + HALO

    def token_norm():
        resid = tokens[...].astype(jnp.float32)
        scale = lax.rsqrt(jnp.mean(resid * resid, axis=-1, keepdims=True) + epsilon)
        return resid * scale, scale

    def back_through(grad, normed, scale, gain):
        inner = grad * gain
        return scale * (inner - normed * jnp.mean(inner * normed, axis=-1, keepdims=True))

    def in_order(own, other):
        return jnp.concatenate(
            [chosen(first_core, own, other), chosen(first_core, other, own)], axis=1
        )

    @pl.when(step == 0)
    def _():
        vectors[...] = jnp.zeros(vectors.shape, jnp.float32)
        low, high = came[:, half:].astype(jnp.float32), came[:, :half].astype(jnp.float32)
        grad = in_order(back[:, :half] + low, back[:, half:] + high)
        resid = hidden[...]
        scale = lax.rsqrt(jnp.mean(resid * resid, axis=-1, keepdims=True) + epsilon)
        normed = resid * scale
        vectors[1:2, :] = jnp.sum(grad[:rows] * normed[:rows], axis=0, keepdims=True)
        result = back_through(grad, normed, scale, small[1:2, :])
        result = result + jnp.concatenate([cotangent[...], after[...]], axis=0).astype(jnp.float32)
        d_hidden[...] = result
        d_branch[...] = result.astype(jnp.bfloat16)
        norm_in[...] = (token_norm()[0] * small[0:1, :]).astype(jnp.bfloat16)
        d_norm_in[...] = jnp.zeros(d_norm_in.shape, jnp.float32)

    here = pl.num_programs(0) // 2

    @pl.when(step < here)
    def _():
        d_gated[...] = dot(d_branch[...], out_own[...], NT)

    @pl.when(step >= here)
    def _():
        d_gated[...] = dot(d_branch[...], out_other[...], NT)

    join_rows(weights, (own_b, own_c, own_x), (other_b, other_c, other_x))
    mixed[...] = b_ref[...] * x_ref[...]
    now, one, two, conv = conv_rows(mixed, keeps[:, 0:1], keeps[:, 1:2], taps, ext)
    c_part = c_ref[pl.ds(HALO, ext), :]
    grad = d_gated[...]
    gated = (c_part[:rows] * conv[:rows]).astype(jnp.bfloat16)
    d_conv = grad * c_part
    block = lax.rem(core * here + step, pl.num_programs(0))
    lanes = pl.ds(pl.multiple_of(block * TILE, TILE), TILE)
    for index, view in enumerate((now, one, two)):
        vectors[2 + index : 3 + index, lanes] = jnp.sum(
            d_conv[:rows] * view[:rows], axis=0, keepdims=True
        )
    along_one[...] = keeps[:, 0:1] * d_conv * taps[3:4, :]
    along_two[...] = keeps[:, 1:2] * d_conv * taps[4:5, :]
    d_mixed = (
        taps[2:3, :] * d_conv[:rows] + along_one[pl.ds(1, rows), :] + along_two[pl.ds(2, rows), :]
    )
    d_proj[:, :TILE] = (d_mixed * x_ref[pl.ds(HALO, rows), :]).astype(jnp.bfloat16)
    d_proj[:, TILE : 2 * TILE] = (grad[:rows] * conv[:rows]).astype(jnp.bfloat16)
    d_proj[:, 2 * TILE :] = (d_mixed * b_ref[pl.ds(HALO, rows), :]).astype(jnp.bfloat16)
    out_grad = dot(gated, d_branch[:rows, :], TN)
    in_grad = dot(norm_in[...], d_proj[...], TN)
    d_norm_in[...] += dot(d_proj[...], weights[...], NT)
    groups, per, _ = send.shape
    few = groups // pl.num_programs(0)

    def divide(value, keep, group, at):
        pair = value.reshape(value.shape[0] // (2 * per), 2, per, value.shape[1]).astype(send.dtype)
        for side in range(2):

            @pl.when(core == side)
            def _():
                send[group, :, at] = pair[:, 1 - side]
                keep[...] = pair[:, side]

    every = slice(None)
    for index, keep in enumerate((b_keep, None, c_keep, x_keep)):
        if keep is None:
            divide(out_grad, out_keep, pl.ds(block * few, few), pl.ds(width, width))
        else:
            third = index and index - 1
            at = pl.multiple_of(index * width + block * TILE, TILE)
            divide(in_grad[:, third * TILE : (third + 1) * TILE], keep, every, pl.ds(at, TILE))

    @pl.when(step == pl.num_programs(0) - 1)
    def _():
        final = in_order(d_norm_in[:, :half], d_norm_in[:, half:])
        normed, scale = token_norm()
        vectors[0:1, :] = jnp.sum(final * normed, axis=0, keepdims=True)
        input_grad[...] = (
            d_hidden[:rows, :] + back_through(final, normed, scale, small[0:1, :])
        ).astype(jnp.bfloat16)
        divide(vectors[...].T, vector_keep, every, pl.ds(4 * width, vectors.shape[0]))


def conv_backward(
    info,
    tokens,
    hidden,
    cotangent,
    after,
    back,
    came,
    small,
    keeps,
    parts,
    w_in,
    w_in_other,
    w_out,
    w_out_other,
    devices,
):
    rows, width = tokens.shape
    ext = rows + HALO
    steps, at, weight_specs = channel_specs(width)
    column = pl.BlockSpec((ext + HALO, TILE), lambda j, info: (0, at(j, info)))
    per = width // devices
    kind = jnp.bfloat16 if per % 16 == 0 else jnp.float32
    groups = devices // 2
    by_columns = pl.BlockSpec((groups, per, TILE), lambda j, info: (0, 0, at(j, info)))
    by_rows = pl.BlockSpec((groups // steps, per, width), lambda j, info: (at(j, info), 0, 0))
    return pl.pallas_call(
        backward_kernel,
        out_shape=[
            jax.ShapeDtypeStruct((rows, width), jnp.bfloat16),
            jax.ShapeDtypeStruct((groups, per, 4 * width + 128), kind),
        ]
        + [jax.ShapeDtypeStruct((groups, per, width), kind)] * 4
        + [jax.ShapeDtypeStruct((groups, per, 128), kind)],
        grid_spec=pltpu.PrefetchScalarGridSpec(
            num_scalar_prefetch=1,
            grid=(steps,),
            in_specs=[
                fixed(rows, width),
                fixed(ext, width),
                fixed(rows, width),
                pl.BlockSpec((HALO, width), lambda j, info: (0, 1)),
                fixed(ext, width),
                fixed(ext, width),
                fixed(*small.shape),
                pl.BlockSpec((small.shape[0], TILE), lambda j, info: (0, at(j, info))),
                fixed(*keeps.shape),
            ]
            + [column] * 3
            + weight_specs,
            out_specs=[
                fixed(rows, width),
                fixed(groups, per, 4 * width + 128),
                by_columns,
                by_rows,
                by_columns,
                by_columns,
                fixed(groups, per, 128),
            ],
            scratch_shapes=[
                pltpu.VMEM((128, width), jnp.float32),
                pltpu.VMEM((ext, width), jnp.float32),
                pltpu.VMEM((ext, width), jnp.bfloat16),
                pltpu.VMEM((rows, width), jnp.bfloat16),
                pltpu.VMEM((rows, width), jnp.float32),
                pltpu.VMEM((width, 3 * TILE), jnp.bfloat16),
                pltpu.VMEM((ext + HALO, TILE), jnp.float32),
                pltpu.VMEM((ext, TILE), jnp.float32),
                pltpu.VMEM((ext, TILE), jnp.float32),
                pltpu.VMEM((ext, TILE), jnp.float32),
                pltpu.VMEM((rows, 3 * TILE), jnp.bfloat16),
            ],
        ),
        name="conv_backward",
        **params(),
    )(
        info,
        tokens,
        hidden,
        cotangent,
        after,
        back,
        came,
        small,
        small,
        keeps,
        *parts,
        *[w_in] * 3,
        *[w_in_other] * 3,
        w_out,
        w_out_other,
    )


def ffn_kernel(
    pieces,
    split,
    info,
    n_own,
    n_other,
    g_own,
    g_after,
    g_other,
    g_other_after,
    gate_own,
    gate_other,
    up_own,
    up_other,
    down_ref,
    act_ref,
    back_keep,
    back_send,
    gate_send,
    gate_keep,
    up_send,
    up_keep,
    whole,
    n_all,
    g_all,
    back,
    weights,
    grads,
):
    step = pl.program_id(0)
    rows = n_all.shape[0]
    block = g_own.shape[0]
    real = 2 * block
    tile = down_ref.shape[0]
    places = (
        (pl.ds(0, block), 0, pl.ds(0, block), g_own),
        (pl.ds(real, HALO), 0, pl.ds(block, HALO), g_after),
        (pl.ds(block, block), 1, pl.ds(0, block), g_other),
        (pl.ds(real + HALO, HALO), 1, pl.ds(block, HALO), g_other_after),
    )

    @pl.when(step == 0)
    def _():
        back[...] = jnp.zeros(back.shape, jnp.float32)
        for place, which, source, grad in places:
            n_all[place, :] = (n_own, n_other)[which][source, :]
            g_all[place, :] = grad[...]

    join_rows(weights, (gate_own, up_own), (gate_other, up_other))
    size = -(-rows // pieces // 16) * 16
    for start in range(0, rows, size):
        part = pl.ds(start, min(size, rows - start))
        proj = dot(n_all[part, :], weights[...], NN)
        d_act = dot(g_all[part, :], down_ref[...], NT)
        gate = proj[:, :tile]
        up_val = proj[:, tile:]
        sigma = 0.5 * jnp.tanh(0.5 * gate) + 0.5
        silu = gate * sigma
        act_ref[part, :] = (silu * up_val).astype(jnp.bfloat16)
        grads[part, tile:] = (d_act * silu).astype(jnp.bfloat16)
        grads[part, :tile] = (d_act * up_val * (sigma + silu * (1.0 - sigma))).astype(jnp.bfloat16)
        back[part, :] += dot(grads[part, :], weights[...], NT)
    summed = dot(n_all[:real, :], grads[:real, :], TN).astype(jnp.bfloat16)
    half = summed.shape[0] // 2
    for core in range(2):

        @pl.when(jnp.logical_and(step >= split, info[0] == core))
        def _():
            whole[:half, :] = summed[core * half : (core + 1) * half, :]
            whole[half:, :] = summed[(1 - core) * half : (2 - core) * half, :]

    for index, (send, keep) in enumerate(((gate_send, gate_keep), (up_send, up_keep))):
        groups, per, columns = send.shape
        pair = summed[:, index * tile : (index + 1) * tile].reshape(groups, 2, per, columns)
        for value in range(2):

            @pl.when(jnp.logical_and(step < split, info[1 + index] == value))
            def _():
                send[...] = pair[:, 1 - value]
                keep[...] = pair[:, value]

    @pl.when(step == pl.num_programs(0) - 1)
    def _():
        for place, which, source, _ in places:
            out = (back_keep, back_send)[which]
            out[source, :] = back[place, :].astype(out.dtype)


def ffn(info, norms, grads, weights, down, split, pers):
    ext, width = norms[0].shape
    rows = 2 * ext
    half = width // 2
    count = down.shape[0] // TILE
    column = pl.BlockSpec((half, TILE), lambda j, info: (0, info[0] * count + j))
    shapes = [jax.ShapeDtypeStruct((rows, count * TILE), jnp.bfloat16)]
    specs = [pl.BlockSpec((rows, TILE), lambda j, info: (0, j))]
    for kind in (jnp.float32, jnp.bfloat16):
        shapes.append(jax.ShapeDtypeStruct((ext, width), kind))
        specs.append(fixed(ext, width))
    for per in pers:
        for _ in range(2):
            groups = width // (2 * per)
            shapes.append(jax.ShapeDtypeStruct((groups, per, split * TILE), jnp.bfloat16))
            specs.append(
                pl.BlockSpec(
                    (groups, per, TILE), lambda j, info: (0, 0, jnp.minimum(j, split - 1))
                )
            )
    shapes.append(jax.ShapeDtypeStruct((width, 2 * (count - split) * TILE), jnp.bfloat16))
    specs.append(pl.BlockSpec((width, 2 * TILE), lambda j, info: (0, jnp.maximum(j - split, 0))))
    after = pl.BlockSpec((HALO, width), lambda j, info: (0, 1))
    return pl.pallas_call(
        functools.partial(ffn_kernel, 3, split),
        out_shape=shapes,
        grid_spec=pltpu.PrefetchScalarGridSpec(
            num_scalar_prefetch=1,
            grid=(count,),
            in_specs=[fixed(ext, width)] * 2
            + [fixed(ext - HALO, width), after] * 2
            + [column] * 4
            + [pl.BlockSpec((TILE, width), lambda j, info: (j, 0))],
            out_specs=specs,
            scratch_shapes=[
                pltpu.VMEM((rows, width), jnp.bfloat16),
                pltpu.VMEM((rows, width), jnp.bfloat16),
                pltpu.VMEM((rows, width), jnp.float32),
                pltpu.VMEM((width, 2 * TILE), jnp.bfloat16),
                pltpu.VMEM((rows, 2 * TILE), jnp.bfloat16),
            ],
        ),
        name="ffn",
        **params(),
    )(info, *norms, *grads, *weights, down)


def down_kernel(
    info,
    act,
    g_own,
    g_other,
    down_ref,
    out_keep,
    out_send,
    low_send,
    low_keep,
    high_send,
    high_keep,
    rhs,
    grad,
):
    step = pl.program_id(0)
    block = out_keep.shape[0]
    real = 2 * block
    rhs[:block, :] = g_own[...]
    rhs[block:, :] = g_other[...]
    result = dot(act[:real, :], down_ref[...], NN)
    out_keep[...] = result[:block]
    out_send[...] = result[block:].astype(out_send.dtype)
    grad[...] = dot(act[:real, :], rhs[...], TN).astype(grad.dtype)
    here = pl.num_programs(0) // 2
    outs = ((step < here, low_send, low_keep, info[1]), (step >= here, high_send, high_keep, info[2]))
    for now, send, keep, mine in outs:
        groups, per, _ = send.shape
        for value in range(2):

            @pl.when(jnp.logical_and(now, mine == value))
            def _():
                for group in range(groups):
                    start = 2 * group * per
                    send[group] = grad[pl.ds(start + (1 - value) * per, per), :]
                    keep[group] = grad[pl.ds(start + value * per, per), :]


def down_part(info, act, g_own, g_other, down, pers):
    hidden, width = down.shape
    steps = width // TILE
    here = steps // 2
    block = g_own.shape[0]
    kind = jnp.bfloat16 if min(pers) % 16 == 0 else jnp.float32
    tile = pl.BlockSpec((block, TILE), lambda j, info: (0, j))
    shapes = [jax.ShapeDtypeStruct((block, width), kind) for kind in (jnp.float32, jnp.bfloat16)]
    specs = [tile] * 2
    for index, per in enumerate(pers):
        groups = hidden // (2 * per)
        for _ in range(2):
            shapes.append(jax.ShapeDtypeStruct((groups, per, width // 2), kind))
            if index == 0:
                specs.append(
                    pl.BlockSpec(
                        (groups, per, TILE), lambda j, info: (0, 0, jnp.minimum(j, here - 1))
                    )
                )
            else:
                specs.append(
                    pl.BlockSpec((groups, per, TILE), lambda j, info: (0, 0, jnp.maximum(j - here, 0)))
                )
    return pl.pallas_call(
        down_kernel,
        out_shape=shapes,
        grid_spec=pltpu.PrefetchScalarGridSpec(
            num_scalar_prefetch=1,
            grid=(steps,),
            in_specs=[
                fixed(*act.shape),
                tile,
                tile,
                pl.BlockSpec((hidden, TILE), lambda j, info: (0, j)),
            ],
            out_specs=specs,
            scratch_shapes=[
                pltpu.VMEM((2 * block, TILE), jnp.bfloat16),
                pltpu.VMEM((hidden, TILE), kind),
            ],
        ),
        name="down",
        **params(),
    )(info, act, g_own, g_other, down)


def combine_kernel(plan, info, *refs):
    refs = list(refs)
    inputs = [[[refs.pop(0) for _ in range(count)] for count in counts] for counts in plan]
    for members, out in zip(inputs, refs):
        edge = 0
        for terms in members:
            size = terms[0].shape[-1]
            value = terms[0][...].astype(jnp.float32)
            for term in terms[1:]:
                value = value + term[...].astype(jnp.float32)
            out[..., edge : edge + size] = value.reshape(out.shape[:-1] + (size,)).astype(out.dtype)
            edge += size


def combine(info, slots, jobs, flip=False):
    plan, arrays, specs, shapes, out_specs = [], [], [], [], []
    lefts = []
    for bit, members in jobs:
        common = members[0][0][1]
        for terms in members:
            for _, names, _, _ in terms:
                common = [name for name in common if name in names]
        lefts.append([name for name in common if name != bit])
    gridded = all(lefts)
    for (bit, members), left in zip(jobs, lefts):
        for terms in members:
            for array, names, block, size in terms:
                rows = array.size // array.shape[-1] >> len(names)
                arrays.append(array.reshape([2] * len(names) + [rows, array.shape[-1]]))
                shape, picks = [], []
                for name in names:
                    if name == bit:
                        shape.append(None)
                        picks.append(("other", slots[name]))
                    elif name not in left:
                        shape.append(None)
                        picks.append(("mine", slots[name]))
                    elif gridded and name == left[0]:
                        shape.append(None)
                        picks.append(("step", 0))
                    else:
                        shape.append(2)
                        picks.append(("all", 0))

                def index_map(j, info, picks=picks, block=block):
                    where = []
                    for kind, slot in picks:
                        if kind == "all":
                            where.append(0)
                        elif kind == "step":
                            where.append(lax.rem(j + info[0], 2) if flip else j)
                        else:
                            where.append(info[slot] if kind == "mine" else 1 - info[slot])
                    return (*where, 0, block)

                specs.append(pl.BlockSpec((*shape, rows, size), index_map))
        width = sum(terms[0][3] for terms in members)
        kind = jnp.bfloat16 if rows % 16 == 0 else jnp.float32
        outer = 1 << len(left)
        shapes.append(jax.ShapeDtypeStruct((outer, rows, width), kind))
        inner = outer // 2 if gridded else outer
        out_specs.append(pl.BlockSpec((inner, rows, width), lambda j, info: (j, 0, 0)))
        plan.append([len(terms) for terms in members])
    results = pl.pallas_call(
        functools.partial(combine_kernel, plan),
        out_shape=shapes,
        grid_spec=pltpu.PrefetchScalarGridSpec(
            num_scalar_prefetch=1,
            grid=(2 if gridded else 1,),
            in_specs=specs,
            out_specs=out_specs,
        ),
        name="combine",
        **params(),
    )(info, *arrays)
    return list(zip(results, lefts))


def finish_kernel(counts, tiles, info, *refs):
    *inputs, mine, send, scratch = refs
    place = 0
    for count in counts:
        value = inputs[0][...].astype(jnp.float32)
        for term in inputs[1:count]:
            value = value + term[...].astype(jnp.float32)
        inputs = inputs[count:]
        for tile in range(value.shape[1] // TILE):
            start = tiles[place] * TILE
            scratch[:, start : start + TILE] = value[:, tile * TILE : (tile + 1) * TILE]
            place += 1
    rows = mine.shape[0]
    for side, out in ((info[0], mine), (1 - info[0], send)):
        out[...] = scratch[pl.ds(pl.multiple_of(side * rows, rows), rows), :]


def picked(slots, terms):
    arrays, specs = [], []
    for array, names, block, size in terms:
        rows = array.size // array.shape[-1] >> len(names)
        arrays.append(array.reshape([2] * len(names) + [rows, array.shape[-1]]))
        specs.append(
            pl.BlockSpec(
                (*[None] * len(names), rows, size),
                lambda j, info, names=names, block=block: (
                    *[info[slots[name]] for name in names],
                    0,
                    block,
                ),
            )
        )
    return arrays, specs


def settle_kernel(plan, info, *refs):
    refs = list(refs)
    inputs = [[[refs.pop(0) for _ in range(count)] for count in counts] for counts, _ in plan]
    for members, (_, kinds) in zip(inputs, plan):
        if kinds is None:
            rows = members[0][0].shape[0]
            value = members[0][0][...].astype(jnp.float32)
            for term in members[0][1:]:
                value = value + term[...].astype(jnp.float32)
            across_rows = lax.broadcasted_iota(jnp.int32, (rows, rows), 0)
            across_columns = lax.broadcasted_iota(jnp.int32, (rows, rows), 1)
            for column in range(2):
                diagonal = jnp.where(
                    across_rows == across_columns, value[:, column : column + 1], 0.0
                )
                refs.pop(0)[...] = jnp.sum(diagonal, axis=0, keepdims=True)
            refs.pop(0)[...] = value[:, 2:5]
            continue
        outs = [refs.pop(0) for _ in kinds]
        edge = 0
        for terms in members:
            size = terms[0].shape[-1]
            value = terms[0][...].astype(jnp.float32)
            for term in terms[1:]:
                value = value + term[...].astype(jnp.float32)
            for out in outs:
                out[:, edge : edge + size] = value.astype(out.dtype)
            edge += size


def settle(info, slots, groups):
    arrays, specs, shapes, plan = [], [], [], []
    for members, kinds in groups:
        for terms in members:
            views, view_specs = picked(slots, terms)
            arrays += views
            specs += view_specs
        rows = views[0].shape[-2]
        width = sum(terms[0][3] for terms in members)
        if kinds is None:
            shapes += [jax.ShapeDtypeStruct((1, rows), jnp.float32)] * 2
            shapes.append(jax.ShapeDtypeStruct((rows, 3), jnp.float32))
        else:
            shapes += [jax.ShapeDtypeStruct((rows, width), kind) for kind in kinds]
        plan.append(([len(terms) for terms in members], kinds))
    return pl.pallas_call(
        functools.partial(settle_kernel, plan),
        out_shape=shapes,
        grid_spec=pltpu.PrefetchScalarGridSpec(
            num_scalar_prefetch=1,
            grid=(1,),
            in_specs=specs,
            out_specs=[fixed(*shape.shape) for shape in shapes],
        ),
        name="settle",
        **params(),
    )(info, *arrays)


def finish(info, slots, members, tiles):
    columns = len(tiles) * TILE
    arrays, specs = [], []
    for terms in members:
        views, view_specs = picked(slots, terms)
        rows = views[0].shape[-2]
        arrays += views
        specs += view_specs
    return pl.pallas_call(
        functools.partial(finish_kernel, [len(terms) for terms in members], tiles),
        out_shape=[jax.ShapeDtypeStruct((rows // 2, columns), jnp.float32)] * 2,
        grid_spec=pltpu.PrefetchScalarGridSpec(
            num_scalar_prefetch=1,
            grid=(1,),
            in_specs=specs,
            out_specs=[fixed(rows // 2, columns)] * 2,
            scratch_shapes=[pltpu.VMEM((rows, columns), jnp.float32)],
        ),
        name="finish",
        **params(),
    )(info, *arrays)


def local(
    tokens,
    cotangent,
    doc_lengths,
    norm_gain,
    in_weight,
    conv_taps,
    out_weight,
    ffn_gain,
    gate_weight,
    up_weight,
    down_weight,
):
    rows, width = tokens.shape
    hidden = down_weight.shape[0]
    chips = lax.axis_size("seq")
    top = chips.bit_length() - 2
    lower = list(range(top))
    bits = list(range(top, -1, -1))
    chip = lax.axis_index("seq")
    core = lax.axis_index("wa")
    coords = {bit: (chip >> bit) & 1 for bit in range(top + 1)}
    turned = dict(coords)
    turned[top] = coords[top] ^ core
    ordering = lax.optimization_barrier

    def after(value, *gates):
        return ordering((value, gates))[0]

    def ordered(low, high):
        return jnp.where(core == 0, low, high)

    def both(own, other, axis):
        return ordered(
            jnp.concatenate([own, other], axis=axis), jnp.concatenate([other, own], axis=axis)
        )

    w_in_other = partner(in_weight)
    w_out_other = partner(out_weight)
    small = jnp.concatenate([norm_gain[None], ffn_gain[None], conv_taps.T], axis=0)
    small = jnp.pad(small, ((0, 3), (0, 0)))
    small_other = partner(small)
    before_rows = shifted(tokens[rows - HALO :], 1)
    after_rows = shifted(jnp.concatenate([tokens[:HALO], cotangent[:HALO]], axis=1), -1)
    cot_other = partner(cotangent)
    after_other = partner(after_rows)
    early = (w_in_other, w_out_other, small_other, before_rows, cot_other, after_other)
    w_in_other, w_out_other, small_other, before_rows, cot_other, after_other = ordering(early)
    small = both(small, small_other, 1).astype(jnp.float32)
    gate_late, up_late = after((gate_weight, up_weight), early)
    gate_other = partner(gate_late)
    up_other = partner(up_late)

    place = lax.axis_index(AXES) * rows + jnp.arange(rows + HALO, dtype=jnp.int32)
    earlier = jnp.arange(doc_lengths.shape[0])
    earlier = earlier[:, None] < earlier[None, :]
    starts = jnp.sum(jnp.where(earlier, doc_lengths[:, None], 0), axis=0)
    first = jnp.any(place[:, None] == starts[None, :], axis=1)
    before = jnp.any((place - 1)[:, None] == starts[None, :], axis=1)
    keep_one = jnp.where(first, 0.0, 1.0)
    keep_two = jnp.where(jnp.logical_or(first, before), 0.0, 1.0)
    lane = lax.broadcasted_iota(jnp.int32, (rows + HALO, 128), 1)
    keeps = jnp.where(lane == 0, keep_one[:, None], keep_two[:, None]).astype(jnp.float32)
    info = [core] + [coords[bit] for bit in lower] + [coords[top], turned[top]]
    info = jnp.stack(info).astype(jnp.int32)

    *parts, hidden_res, norm_own, norm_send = conv_forward(
        info,
        tokens,
        before_rows,
        after_rows,
        small,
        keeps,
        in_weight,
        w_in_other,
        out_weight,
        w_out_other,
    )
    norm_other = partner(norm_send)
    norm_own, gate_other, up_other = ordering((norm_own, gate_other, up_other))
    per_chip = width // chips
    pers = (per_chip << lower[0], per_chip << lower[1])
    tiles = hidden // TILE
    split = tiles * 4 // 9
    counts = (split, tiles - split)
    orders = (lower, [lower[1], lower[0]] + lower[2:])

    act, back_keep, back_send, *one, whole = ffn(
        info,
        (norm_own, norm_other),
        (cotangent, after_rows, cot_other, after_other),
        (gate_weight, gate_other, up_weight, up_other),
        down_weight,
        split,
        pers,
    )
    one_x = across(one[0], orders[0][0])
    one_y = across(one[2], orders[1][0])
    came = partner(back_send)

    groups = [
        [low + (level << (top - 1)) for level in range(4)] for low in range(1 << (top - 1))
    ]
    quarter = lax.psum_scatter(
        whole, "seq", scatter_dimension=0, axis_index_groups=groups, tiled=True
    )

    slots = {bit: 1 + bit for bit in bits}
    turned_slots = dict(slots)
    turned_slots[top] = 2 + top

    def plain(array, names):
        return (array, names, 0, array.shape[-1])

    def gated(streams, *gates):
        held = after([terms[-1][0] for terms in streams], gates)
        return [
            terms[:-1] + [(array, *terms[-1][1:])] for terms, array in zip(streams, held)
        ]

    def without(names, *taken):
        return [name for name in names if name not in taken]

    def send_on(streams, names, use=slots):
        results = combine(info, use, streams)
        return [send for send, _ in results], [
            (across(send, bit), left) for (bit, _), (send, left) in zip(streams, results)
        ]

    def upper_sum(value):
        value = value.reshape(-1, value.shape[-1])
        return lax.psum_scatter(
            value, "seq", scatter_dimension=0, axis_index_groups=groups, tiled=True
        )

    down_pers = [2 * hidden // chips << bit for bit in (lower[0], lower[1])]
    out_keep, out_send, *down_halves = down_part(
        info, act, cotangent, cot_other, down_weight, down_pers
    )
    came, out_send, down_halves, one_x, one_y = ordering(
        (came, out_send, down_halves, one_x, one_y)
    )

    down_x = across(down_halves[0], orders[0][0])
    down_y = across(down_halves[2], orders[1][0])
    out_came = partner(out_send)
    one_terms = [
        [plain(keep, without(bits, order[0])), plain(got, without(bits, order[0]))]
        for keep, got, order in ((one[1], one_x, orders[0]), (one[3], one_y, orders[1]))
    ]
    one_sent, one_got = send_on(
        [(order[1], [terms]) for terms, order in zip(one_terms, orders)], bits, turned_slots
    )
    one_got = [got for got, _ in one_got]
    came = after(came, one_sent)

    def side_by_side(streams, order, use=slots):
        sent = None
        for bit in order:
            sent, ((got, left),) = send_on([(bit, streams)], None, use)
            edge, members = 0, []
            for terms in streams:
                size = terms[0][3]
                members.append(terms + [(got, left, edge, size)])
                edge += size
            for terms in members:
                array, left, edge, size = terms[-1]
                if edge % size:
                    array, edge = array[..., edge : edge + size], 0
                terms[-1] = (array, left, edge // size, size)
            streams = members
        return sent, streams

    input_grad, conv_send, *conv_keeps = conv_backward(
        info,
        tokens,
        hidden_res,
        cotangent,
        after_rows,
        back_keep,
        came,
        small,
        keeps,
        parts,
        in_weight,
        w_in_other,
        out_weight,
        w_out_other,
        2 * chips,
    )
    conv_send, conv_keeps, down_x, down_y, out_came = ordering(
        (conv_send, conv_keeps, down_x, down_y, out_came)
    )
    conv_came = partner(conv_send)

    down_bits = bits[1:]
    down_terms = [
        [plain(keep, without(down_bits, order[0])), plain(got, without(down_bits, order[0]))]
        for keep, got, order in (
            (down_halves[1], down_x, orders[0]),
            (down_halves[3], down_y, orders[1]),
        )
    ]
    down_sent, down_got = send_on(
        [(order[1], [terms]) for terms, order in zip(down_terms, orders)], down_bits
    )
    down_got = [got for got, _ in down_got]

    conv_came = after(conv_came, down_sent)
    conv_members = [
        [
            [plain(conv_keeps[member], bits), (conv_came, bits, member * width // size, size)]
            for member, size in members
        ]
        for members in (((0, width), (1, width)), ((2, width), (3, width), (4, 128)))
    ]
    conv_sent, conv_got = send_on(
        [(order[0], members) for members, order in zip(conv_members, orders)], bits
    )
    conv_got = [got for got, _ in conv_got]

    one_got = after(one_got, conv_sent)
    one_streams = [
        terms + [plain(got, without(bits, *order[:2]))]
        for terms, got, order in zip(one_terms, one_got, orders)
    ]
    _, one_streams = side_by_side(one_streams, lower[2 : top - 1], turned_slots)
    ((one_all, _),) = combine(info, turned_slots, [(None, one_streams)], flip=True)
    one_done = upper_sum(one_all)

    down_got = after(down_got, one_all)
    down_streams = [
        terms + [plain(got, without(down_bits, *order[:2]))]
        for terms, got, order in zip(down_terms, down_got, orders)
    ]
    down_sent, down_streams = side_by_side(down_streams, lower[2:])

    down_streams = gated(down_streams, down_sent)
    part, down_last = settle(info, slots, [(down_streams, (jnp.float32, jnp.bfloat16))])
    pairs = [
        (source * 2 + side, (source ^ (1 << top)) * 2 + side)
        for source in range(chips)
        for side in range(2)
        if (source >> top) & 1 != side
    ]
    down_far = lax.ppermute(down_last, AXES, pairs)

    conv_got = after(conv_got, down_last)
    for index, (members, order) in enumerate(zip(conv_members, orders)):
        edge = 0
        for terms in members:
            size = terms[0][3]
            terms.append((conv_got[index], without(bits, order[0]), edge // size, size))
            edge += size
    conv_sent, conv_two = send_on(
        [(order[1], members) for members, order in zip(conv_members, orders)], bits
    )
    conv_two = [got for got, _ in conv_two]

    quarter = after(quarter, conv_sent)
    edge = counts[1] * TILE
    two_terms = [[(quarter, bits[2:], block, edge)] for block in range(2)]
    two_sent, two_got = send_on(
        [(order[0], [terms]) for terms, order in zip(two_terms, orders)], bits[2:]
    )
    two_got = [got for got, _ in two_got]
    out_came = after(out_came, two_sent)
    block_out = (hidden_res[:rows] + out_keep + out_came).astype(jnp.bfloat16)
    conv_two = after(conv_two, two_sent, block_out)
    conv_streams = []
    for members, got, order in zip(conv_members, conv_two, orders):
        edge = 0
        for terms in members:
            size = terms[0][3]
            conv_streams.append(terms + [(got, without(bits, *order[:2]), edge // size, size)])
            edge += size
    _, conv_streams = side_by_side(conv_streams, lower[2 : top - 1])
    ((conv_all, _),) = combine(info, slots, [(None, conv_streams)])
    conv_done = upper_sum(conv_all)
    two_got = after(two_got, conv_all)
    two_terms = [
        terms + [plain(got, without(bits[2:], order[0]))]
        for terms, got, order in zip(two_terms, two_got, orders)
    ]
    two_sent, two_got = send_on(
        [(order[1], [terms]) for terms, order in zip(two_terms, orders)], bits[2:]
    )
    two_streams = [terms + [plain(*got)] for terms, got in zip(two_terms, two_got)]
    _, two_streams = side_by_side(two_streams, lower[2 : top - 1])

    part, down_far = after((part, down_far), conv_all)
    part = part + down_far.astype(jnp.float32)
    part = part.reshape(2, -1, width)
    down_out = jnp.where(
        coords[top] == core, take(part, core, 0), partner(take(part, 1 - core, 0))
    )
    b_out, out_out, c_out, x_out, vectors = (
        [(conv_done, [], member * width // size, size)]
        for member, size in enumerate([width] * 4 + [128])
    )
    in_out, out_out, gain_one_out, gain_two_out, taps_out = settle(
        info,
        slots,
        [
            ([b_out, c_out, x_out], (jnp.float32,)),
            ([out_out], (jnp.float32,)),
            ([vectors], None),
        ],
    )

    gate_tiles = [tile for tile in range(counts[0])] + [tiles + tile for tile in range(counts[0])]
    for tile in range(counts[1]):
        gate_tiles += [counts[0] + tile, tiles + counts[0] + tile]
    kept, send = finish(info, slots, [[plain(one_done, [])]] + two_streams, gate_tiles)
    other = partner(send)
    gate_out = both(kept[:, :hidden], other[:, :hidden], 1)
    up_out = both(kept[:, hidden:], other[:, hidden:], 1)
    return (
        block_out,
        input_grad,
        gain_one_out.reshape(-1),
        in_out,
        taps_out,
        out_out,
        gain_two_out.reshape(-1),
        gate_out,
        up_out,
        down_out,
    )


def solution(mesh):
    placed = (
        P(AXES, None),
        P(AXES, None),
        P(),
        P("wa"),
        P("wa", None),
        P("wa", None),
        P("wa", None),
        P("wa"),
        P("wa", None),
        P("wa", None),
        P("wa", None),
    )
    return jax.shard_map(
        local,
        mesh=mesh,
        in_specs=placed,
        out_specs=(
            P(AXES, None),
            P(AXES, None),
            P(AXES),
            P(AXES, None),
            P(AXES, None),
            P(AXES, None),
            P(AXES),
            P(AXES, None),
            P(AXES, None),
            P(AXES, None),
        ),
        check_vma=False,
    )
```

```python
import functools
import math

import jax
import jax.numpy as jnp
from jax import lax
from jax.experimental import pallas as pl
from jax.experimental.pallas import tpu as pltpu
from jax.sharding import PartitionSpec as P

epsilon = 1e-05
AXES = ("seq", "wa")
HALO = 16
TILE = 256
VMEM_LIMIT = 63 * 2**20
NN = ((1,), (0,))
NT = ((1,), (1,))
TN = ((0,), (0,))


def shifted(value, steps):
    count = lax.axis_size(AXES)
    first, last = (max(0, -steps), min(count, count - steps))
    return lax.ppermute(value, AXES, [(source, source + steps) for source in range(first, last)])


def partner(value):
    return lax.ppermute(value, "wa", [(0, 1), (1, 0)])


def across(value, bit):
    count = lax.axis_size("seq")
    return lax.ppermute(value, "seq", [(place, place ^ (1 << bit)) for place in range(count)])


def dot(left, right, dims):
    return lax.dot_general(left, right, (dims, ((), ())), preferred_element_type=jnp.float32)


def take(value, index, axis):
    return lax.dynamic_index_in_dim(value, index, axis, keepdims=False)


def total(terms):
    result = terms[0].astype(jnp.float32)
    for term in terms[1:]:
        result = result + term.astype(jnp.float32)
    return result


def chosen(test, value, other):
    return jnp.where(test, value, other)


def swapped(value):
    half = value.shape[1] // 2
    return jnp.concatenate([value[:, half:], value[:, :half]], axis=1)


def params(**extra):
    return dict(
        compiler_params=pltpu.CompilerParams(vmem_limit_bytes=VMEM_LIMIT),
        cost_estimate=pl.CostEstimate(flops=1000, bytes_accessed=1000, transcendentals=0),
        **extra,
    )


def conv_rows(mixed, keep_one, keep_two, taps, count):
    now = mixed[pl.ds(HALO, count), :]
    one = mixed[pl.ds(HALO - 1, count), :] * keep_one
    two = mixed[pl.ds(HALO - 2, count), :] * keep_two
    conv = taps[2:3, :] * now + taps[3:4, :] * one + taps[4:5, :] * two
    return now, one, two, conv


def join_rows(weights, own, other):
    half = own[0].shape[0]
    for index, (upper, lower) in enumerate(zip(own, other)):
        weights[:half, index * TILE : (index + 1) * TILE] = upper[...]
        weights[half:, index * TILE : (index + 1) * TILE] = lower[...]


def forward_kernel(
    info,
    tokens,
    before,
    after,
    small,
    taps,
    keeps,
    own_b,
    own_c,
    own_x,
    other_b,
    other_c,
    other_x,
    out_own,
    out_other,
    b_ref,
    c_ref,
    x_ref,
    hidden,
    norm_own,
    norm_send,
    normed,
    weights,
    mixed,
    gated,
    total_ref,
):
    step = pl.program_id(0)
    first_core = info[0] == 0
    rows, width = tokens.shape
    half = width // 2
    ext = rows + HALO

    @pl.when(step == 0)
    def _():
        for start, ref in ((0, before), (HALO, tokens), (HALO + rows, after)):
            resid = ref[:, :width].astype(jnp.float32)
            scale = lax.rsqrt(jnp.mean(resid * resid, axis=-1, keepdims=True) + epsilon)
            norm = resid * scale * small[0:1, :]
            place = pl.ds(start, ref.shape[0])
            normed[place, :half] = chosen(first_core, norm[:, :half], norm[:, half:]).astype(
                jnp.bfloat16
            )
            normed[place, half:] = chosen(first_core, norm[:, half:], norm[:, :half]).astype(
                jnp.bfloat16
            )
        total_ref[:rows, :] = tokens[...].astype(jnp.float32)
        total_ref[rows:, :] = after[:, :width].astype(jnp.float32)

    join_rows(weights, (own_b, own_c, own_x), (other_b, other_c, other_x))
    proj = dot(normed[...], weights[...], NN)
    b_part, c_part, x_part = proj[:, :TILE], proj[:, TILE : 2 * TILE], proj[:, 2 * TILE :]
    b_ref[...] = b_part.astype(b_ref.dtype)
    c_ref[...] = c_part.astype(c_ref.dtype)
    x_ref[...] = x_part.astype(x_ref.dtype)
    mixed[...] = b_part * x_part
    conv = conv_rows(mixed, keeps[:, 0:1], keeps[:, 1:2], taps, ext)[3]
    gated[...] = (c_part[HALO:, :] * conv).astype(jnp.bfloat16)
    here = pl.num_programs(0) // 2

    @pl.when(step < here)
    def _():
        total_ref[...] += dot(gated[...], out_own[...], NN)

    @pl.when(step >= here)
    def _():
        total_ref[...] += dot(gated[...], out_other[...], NN)

    @pl.when(step == pl.num_programs(0) - 1)
    def _():
        resid = total_ref[...]
        hidden[...] = resid
        scale = lax.rsqrt(jnp.mean(resid * resid, axis=-1, keepdims=True) + epsilon)
        norm = resid * scale * small[1:2, :]
        low = chosen(first_core, norm[:, :half], norm[:, half:]).astype(jnp.bfloat16)
        high = chosen(first_core, norm[:, half:], norm[:, :half]).astype(jnp.bfloat16)
        norm_own[:, :half] = low
        norm_own[:, half:] = high
        norm_send[:, :half] = high
        norm_send[:, half:] = low


def channel_specs(width):
    steps = width // TILE
    half = width // 2

    def at(j, info):
        return lax.rem(info[0] * (steps // 2) + j, steps)

    thirds = [
        pl.BlockSpec((half, TILE), lambda j, info, k=k: (0, k * steps + at(j, info)))
        for k in range(3)
    ]
    out_own = pl.BlockSpec((TILE, width), lambda j, info: (jnp.minimum(j, steps // 2 - 1), 0))
    out_other = pl.BlockSpec((TILE, width), lambda j, info: (jnp.maximum(j - steps // 2, 0), 0))
    return steps, at, thirds * 2 + [out_own, out_other]


def fixed(*shape):
    return pl.BlockSpec(shape, lambda j, info: (0,) * len(shape))


def conv_forward(info, tokens, before, after, small, keeps, w_in, w_in_other, w_out, w_out_other):
    rows, width = tokens.shape
    ext = rows + HALO
    steps, at, weight_specs = channel_specs(width)
    column = pl.BlockSpec((ext + HALO, TILE), lambda j, info: (0, at(j, info)))
    return pl.pallas_call(
        forward_kernel,
        out_shape=[jax.ShapeDtypeStruct((ext + HALO, width), jnp.bfloat16)] * 3
        + [jax.ShapeDtypeStruct((ext, width), jnp.float32)]
        + [jax.ShapeDtypeStruct((ext, width), jnp.bfloat16)] * 2,
        grid_spec=pltpu.PrefetchScalarGridSpec(
            num_scalar_prefetch=1,
            grid=(steps,),
            in_specs=[
                fixed(rows, width),
                fixed(HALO, width),
                fixed(*after.shape),
                fixed(*small.shape),
                pl.BlockSpec((small.shape[0], TILE), lambda j, info: (0, at(j, info))),
                fixed(*keeps.shape),
            ]
            + weight_specs,
            out_specs=[column] * 3 + [fixed(ext, width)] * 3,
            scratch_shapes=[
                pltpu.VMEM((ext + HALO, width), jnp.bfloat16),
                pltpu.VMEM((width, 3 * TILE), jnp.bfloat16),
                pltpu.VMEM((ext + HALO, TILE), jnp.float32),
                pltpu.VMEM((ext, TILE), jnp.bfloat16),
                pltpu.VMEM((ext, width), jnp.float32),
            ],
        ),
        name="conv_forward",
        **params(),
    )(
        info,
        tokens,
        before,
        after,
        small,
        small,
        keeps,
        *[w_in] * 3,
        *[w_in_other] * 3,
        w_out,
        w_out_other,
    )


def backward_kernel(
    info,
    tokens,
    hidden,
    cotangent,
    after,
    back,
    came,
    small,
    taps,
    keeps,
    b_ref,
    c_ref,
    x_ref,
    own_b,
    own_c,
    own_x,
    other_b,
    other_c,
    other_x,
    out_own,
    out_other,
    input_grad,
    send,
    b_keep,
    out_keep,
    c_keep,
    x_keep,
    vector_keep,
    vectors,
    d_hidden,
    d_branch,
    norm_in,
    d_norm_in,
    weights,
    mixed,
    d_gated,
    along_one,
    along_two,
    d_proj,
):
    step = pl.program_id(0)
    core = info[0]
    first_core = core == 0
    rows, width = tokens.shape
    half = width // 2
    ext = rows + HALO

    def token_norm():
        resid = tokens[...].astype(jnp.float32)
        scale = lax.rsqrt(jnp.mean(resid * resid, axis=-1, keepdims=True) + epsilon)
        return resid * scale, scale

    def back_through(grad, normed, scale, gain):
        inner = grad * gain
        return scale * (inner - normed * jnp.mean(inner * normed, axis=-1, keepdims=True))

    def in_order(own, other):
        return jnp.concatenate(
            [chosen(first_core, own, other), chosen(first_core, other, own)], axis=1
        )

    @pl.when(step == 0)
    def _():
        vectors[...] = jnp.zeros(vectors.shape, jnp.float32)
        low, high = came[:, half:].astype(jnp.float32), came[:, :half].astype(jnp.float32)
        grad = in_order(back[:, :half] + low, back[:, half:] + high)
        resid = hidden[...]
        scale = lax.rsqrt(jnp.mean(resid * resid, axis=-1, keepdims=True) + epsilon)
        normed = resid * scale
        vectors[1:2, :] = jnp.sum(grad[:rows] * normed[:rows], axis=0, keepdims=True)
        result = back_through(grad, normed, scale, small[1:2, :])
        result = result + jnp.concatenate([cotangent[...], after[...]], axis=0).astype(jnp.float32)
        d_hidden[...] = result
        d_branch[...] = result.astype(jnp.bfloat16)
        norm_in[...] = (token_norm()[0] * small[0:1, :]).astype(jnp.bfloat16)
        d_norm_in[...] = jnp.zeros(d_norm_in.shape, jnp.float32)

    here = pl.num_programs(0) // 2

    @pl.when(step < here)
    def _():
        d_gated[...] = dot(d_branch[...], out_own[...], NT)

    @pl.when(step >= here)
    def _():
        d_gated[...] = dot(d_branch[...], out_other[...], NT)

    join_rows(weights, (own_b, own_c, own_x), (other_b, other_c, other_x))
    mixed[...] = b_ref[...].astype(jnp.float32) * x_ref[...].astype(jnp.float32)
    now, one, two, conv = conv_rows(mixed, keeps[:, 0:1], keeps[:, 1:2], taps, ext)
    c_part = c_ref[pl.ds(HALO, ext), :].astype(jnp.float32)
    grad = d_gated[...]
    gated = (c_part[:rows] * conv[:rows]).astype(jnp.bfloat16)
    d_conv = grad * c_part
    block = lax.rem(core * here + step, pl.num_programs(0))
    lanes = pl.ds(pl.multiple_of(block * TILE, TILE), TILE)
    for index, view in enumerate((now, one, two)):
        vectors[2 + index : 3 + index, lanes] = jnp.sum(
            d_conv[:rows] * view[:rows], axis=0, keepdims=True
        )
    along_one[...] = keeps[:, 0:1] * d_conv * taps[3:4, :]
    along_two[...] = keeps[:, 1:2] * d_conv * taps[4:5, :]
    d_mixed = (
        taps[2:3, :] * d_conv[:rows] + along_one[pl.ds(1, rows), :] + along_two[pl.ds(2, rows), :]
    )
    d_proj[:, :TILE] = (d_mixed * x_ref[pl.ds(HALO, rows), :].astype(jnp.float32)).astype(jnp.bfloat16)
    d_proj[:, TILE : 2 * TILE] = (grad[:rows] * conv[:rows]).astype(jnp.bfloat16)
    d_proj[:, 2 * TILE :] = (d_mixed * b_ref[pl.ds(HALO, rows), :].astype(jnp.float32)).astype(jnp.bfloat16)
    out_grad = dot(gated, d_branch[:rows, :], TN)
    in_grad = dot(norm_in[...], d_proj[...], TN)
    d_norm_in[...] += dot(d_proj[...], weights[...], NT)
    groups, per, _ = send.shape
    few = groups // pl.num_programs(0)

    def divide(value, keep, group, at):
        pair = value.reshape(value.shape[0] // (2 * per), 2, per, value.shape[1]).astype(send.dtype)
        for side in range(2):

            @pl.when(core == side)
            def _():
                send[group, :, at] = pair[:, 1 - side]
                keep[...] = pair[:, side]

    every = slice(None)
    for index, keep in enumerate((b_keep, None, c_keep, x_keep)):
        if keep is None:
            divide(out_grad, out_keep, pl.ds(block * few, few), pl.ds(width, width))
        else:
            third = index and index - 1
            at = pl.multiple_of(index * width + block * TILE, TILE)
            divide(in_grad[:, third * TILE : (third + 1) * TILE], keep, every, pl.ds(at, TILE))

    @pl.when(step == pl.num_programs(0) - 1)
    def _():
        final = in_order(d_norm_in[:, :half], d_norm_in[:, half:])
        normed, scale = token_norm()
        vectors[0:1, :] = jnp.sum(final * normed, axis=0, keepdims=True)
        input_grad[...] = (
            d_hidden[:rows, :] + back_through(final, normed, scale, small[0:1, :])
        ).astype(jnp.bfloat16)
        divide(vectors[...].T, vector_keep, every, pl.ds(4 * width, vectors.shape[0]))


def conv_backward(
    info,
    tokens,
    hidden,
    cotangent,
    after,
    back,
    came,
    small,
    keeps,
    parts,
    w_in,
    w_in_other,
    w_out,
    w_out_other,
    devices,
):
    rows, width = tokens.shape
    ext = rows + HALO
    steps, at, weight_specs = channel_specs(width)
    column = pl.BlockSpec((ext + HALO, TILE), lambda j, info: (0, at(j, info)))
    per = width // devices
    kind = jnp.bfloat16 if per % 16 == 0 else jnp.float32
    groups = devices // 2
    by_columns = pl.BlockSpec((groups, per, TILE), lambda j, info: (0, 0, at(j, info)))
    by_rows = pl.BlockSpec((groups // steps, per, width), lambda j, info: (at(j, info), 0, 0))
    return pl.pallas_call(
        backward_kernel,
        out_shape=[
            jax.ShapeDtypeStruct((rows, width), jnp.bfloat16),
            jax.ShapeDtypeStruct((groups, per, 4 * width + 128), kind),
        ]
        + [jax.ShapeDtypeStruct((groups, per, width), kind)] * 4
        + [jax.ShapeDtypeStruct((groups, per, 128), kind)],
        grid_spec=pltpu.PrefetchScalarGridSpec(
            num_scalar_prefetch=1,
            grid=(steps,),
            in_specs=[
                fixed(rows, width),
                fixed(ext, width),
                fixed(rows, width),
                pl.BlockSpec((HALO, width), lambda j, info: (0, 1)),
                fixed(ext, width),
                fixed(ext, width),
                fixed(*small.shape),
                pl.BlockSpec((small.shape[0], TILE), lambda j, info: (0, at(j, info))),
                fixed(*keeps.shape),
            ]
            + [column] * 3
            + weight_specs,
            out_specs=[
                fixed(rows, width),
                fixed(groups, per, 4 * width + 128),
                by_columns,
                by_rows,
                by_columns,
                by_columns,
                fixed(groups, per, 128),
            ],
            scratch_shapes=[
                pltpu.VMEM((128, width), jnp.float32),
                pltpu.VMEM((ext, width), jnp.float32),
                pltpu.VMEM((ext, width), jnp.bfloat16),
                pltpu.VMEM((rows, width), jnp.bfloat16),
                pltpu.VMEM((rows, width), jnp.float32),
                pltpu.VMEM((width, 3 * TILE), jnp.bfloat16),
                pltpu.VMEM((ext + HALO, TILE), jnp.float32),
                pltpu.VMEM((ext, TILE), jnp.float32),
                pltpu.VMEM((ext, TILE), jnp.float32),
                pltpu.VMEM((ext, TILE), jnp.float32),
                pltpu.VMEM((rows, 3 * TILE), jnp.bfloat16),
            ],
        ),
        name="conv_backward",
        **params(),
    )(
        info,
        tokens,
        hidden,
        cotangent,
        after,
        back,
        came,
        small,
        small,
        keeps,
        *parts,
        *[w_in] * 3,
        *[w_in_other] * 3,
        w_out,
        w_out_other,
    )


def ffn_kernel(
    pieces,
    split,
    info,
    n_own,
    n_other,
    g_own,
    g_after,
    g_other,
    g_other_after,
    gate_own,
    gate_other,
    up_own,
    up_other,
    down_ref,
    act_ref,
    back_keep,
    back_send,
    gate_send,
    gate_keep,
    up_send,
    up_keep,
    whole,
    n_all,
    g_all,
    back,
    weights,
    grads,
):
    step = pl.program_id(0)
    rows = n_all.shape[0]
    block = g_own.shape[0]
    real = 2 * block
    tile = down_ref.shape[0]
    places = (
        (pl.ds(0, block), 0, pl.ds(0, block), g_own),
        (pl.ds(real, HALO), 0, pl.ds(block, HALO), g_after),
        (pl.ds(block, block), 1, pl.ds(0, block), g_other),
        (pl.ds(real + HALO, HALO), 1, pl.ds(block, HALO), g_other_after),
    )

    @pl.when(step == 0)
    def _():
        back[...] = jnp.zeros(back.shape, jnp.float32)
        for place, which, source, grad in places:
            n_all[place, :] = (n_own, n_other)[which][source, :]
            g_all[place, :] = grad[...]

    join_rows(weights, (gate_own, up_own), (gate_other, up_other))
    size = -(-rows // pieces // 16) * 16
    for start in range(0, rows, size):
        part = pl.ds(start, min(size, rows - start))
        proj = dot(n_all[part, :], weights[...], NN)
        d_act = dot(g_all[part, :], down_ref[...], NT)
        gate = proj[:, :tile]
        up_val = proj[:, tile:]
        sigma = 0.5 * jnp.tanh(0.5 * gate) + 0.5
        silu = gate * sigma
        act_ref[part, :] = (silu * up_val).astype(jnp.bfloat16)
        grads[part, tile:] = (d_act * silu).astype(jnp.bfloat16)
        grads[part, :tile] = (d_act * up_val * (sigma + silu * (1.0 - sigma))).astype(jnp.bfloat16)
        back[part, :] += dot(grads[part, :], weights[...], NT)
    summed = dot(n_all[:real, :], grads[:real, :], TN).astype(jnp.bfloat16)
    half = summed.shape[0] // 2
    for core in range(2):

        @pl.when(jnp.logical_and(step >= split, info[0] == core))
        def _():
            whole[:half, :] = summed[core * half : (core + 1) * half, :]
            whole[half:, :] = summed[(1 - core) * half : (2 - core) * half, :]

    for index, (send, keep) in enumerate(((gate_send, gate_keep), (up_send, up_keep))):
        groups, per, columns = send.shape
        pair = summed[:, index * tile : (index + 1) * tile].reshape(groups, 2, per, columns)
        for value in range(2):

            @pl.when(jnp.logical_and(step < split, info[1 + index] == value))
            def _():
                send[...] = pair[:, 1 - value]
                keep[...] = pair[:, value]

    @pl.when(step == pl.num_programs(0) - 1)
    def _():
        for place, which, source, _ in places:
            out = (back_keep, back_send)[which]
            out[source, :] = back[place, :].astype(out.dtype)


def ffn(info, norms, grads, weights, down, split, pers):
    ext, width = norms[0].shape
    rows = 2 * ext
    half = width // 2
    count = down.shape[0] // TILE
    column = pl.BlockSpec((half, TILE), lambda j, info: (0, info[0] * count + j))
    shapes = [jax.ShapeDtypeStruct((rows, count * TILE), jnp.bfloat16)]
    specs = [pl.BlockSpec((rows, TILE), lambda j, info: (0, j))]
    for kind in (jnp.float32, jnp.bfloat16):
        shapes.append(jax.ShapeDtypeStruct((ext, width), kind))
        specs.append(fixed(ext, width))
    for per in pers:
        for _ in range(2):
            groups = width // (2 * per)
            shapes.append(jax.ShapeDtypeStruct((groups, per, split * TILE), jnp.bfloat16))
            specs.append(
                pl.BlockSpec(
                    (groups, per, TILE), lambda j, info: (0, 0, jnp.minimum(j, split - 1))
                )
            )
    shapes.append(jax.ShapeDtypeStruct((width, 2 * (count - split) * TILE), jnp.bfloat16))
    specs.append(pl.BlockSpec((width, 2 * TILE), lambda j, info: (0, jnp.maximum(j - split, 0))))
    after = pl.BlockSpec((HALO, width), lambda j, info: (0, 1))
    return pl.pallas_call(
        functools.partial(ffn_kernel, 3, split),
        out_shape=shapes,
        grid_spec=pltpu.PrefetchScalarGridSpec(
            num_scalar_prefetch=1,
            grid=(count,),
            in_specs=[fixed(ext, width)] * 2
            + [fixed(ext - HALO, width), after] * 2
            + [column] * 4
            + [pl.BlockSpec((TILE, width), lambda j, info: (j, 0))],
            out_specs=specs,
            scratch_shapes=[
                pltpu.VMEM((rows, width), jnp.bfloat16),
                pltpu.VMEM((rows, width), jnp.bfloat16),
                pltpu.VMEM((rows, width), jnp.float32),
                pltpu.VMEM((width, 2 * TILE), jnp.bfloat16),
                pltpu.VMEM((rows, 2 * TILE), jnp.bfloat16),
            ],
        ),
        name="ffn",
        **params(),
    )(info, *norms, *grads, *weights, down)


def down_kernel(
    info,
    act,
    g_own,
    g_other,
    down_ref,
    out_keep,
    out_send,
    low_send,
    low_keep,
    high_send,
    high_keep,
    rhs,
    grad,
):
    step = pl.program_id(0)
    block = out_keep.shape[0]
    real = 2 * block
    rhs[:block, :] = g_own[...]
    rhs[block:, :] = g_other[...]
    result = dot(act[:real, :], down_ref[...], NN)
    out_keep[...] = result[:block]
    out_send[...] = result[block:].astype(out_send.dtype)
    grad[...] = dot(act[:real, :], rhs[...], TN).astype(grad.dtype)
    here = pl.num_programs(0) // 2
    outs = ((step < here, low_send, low_keep, info[1]), (step >= here, high_send, high_keep, info[2]))
    for now, send, keep, mine in outs:
        groups, per, _ = send.shape
        for value in range(2):

            @pl.when(jnp.logical_and(now, mine == value))
            def _():
                for group in range(groups):
                    start = 2 * group * per
                    send[group] = grad[pl.ds(start + (1 - value) * per, per), :]
                    keep[group] = grad[pl.ds(start + value * per, per), :]


def down_part(info, act, g_own, g_other, down, pers):
    hidden, width = down.shape
    steps = width // TILE
    here = steps // 2
    block = g_own.shape[0]
    kind = jnp.bfloat16 if min(pers) % 16 == 0 else jnp.float32
    tile = pl.BlockSpec((block, TILE), lambda j, info: (0, j))
    shapes = [jax.ShapeDtypeStruct((block, width), kind) for kind in (jnp.float32, jnp.bfloat16)]
    specs = [tile] * 2
    for index, per in enumerate(pers):
        groups = hidden // (2 * per)
        for _ in range(2):
            shapes.append(jax.ShapeDtypeStruct((groups, per, width // 2), kind))
            if index == 0:
                specs.append(
                    pl.BlockSpec(
                        (groups, per, TILE), lambda j, info: (0, 0, jnp.minimum(j, here - 1))
                    )
                )
            else:
                specs.append(
                    pl.BlockSpec((groups, per, TILE), lambda j, info: (0, 0, jnp.maximum(j - here, 0)))
                )
    return pl.pallas_call(
        down_kernel,
        out_shape=shapes,
        grid_spec=pltpu.PrefetchScalarGridSpec(
            num_scalar_prefetch=1,
            grid=(steps,),
            in_specs=[
                fixed(*act.shape),
                tile,
                tile,
                pl.BlockSpec((hidden, TILE), lambda j, info: (0, j)),
            ],
            out_specs=specs,
            scratch_shapes=[
                pltpu.VMEM((2 * block, TILE), jnp.bfloat16),
                pltpu.VMEM((hidden, TILE), kind),
            ],
        ),
        name="down",
        **params(),
    )(info, act, g_own, g_other, down)


def combine_kernel(plan, info, *refs):
    refs = list(refs)
    inputs = [[[refs.pop(0) for _ in range(count)] for count in counts] for counts in plan]
    for members, out in zip(inputs, refs):
        edge = 0
        for terms in members:
            size = terms[0].shape[-1]
            value = terms[0][...].astype(jnp.float32)
            for term in terms[1:]:
                value = value + term[...].astype(jnp.float32)
            out[..., edge : edge + size] = value.reshape(out.shape[:-1] + (size,)).astype(out.dtype)
            edge += size


def combine(info, slots, jobs, flip=False):
    plan, arrays, specs, shapes, out_specs = [], [], [], [], []
    lefts = []
    for bit, members in jobs:
        common = members[0][0][1]
        for terms in members:
            for _, names, _, _ in terms:
                common = [name for name in common if name in names]
        lefts.append([name for name in common if name != bit])
    gridded = all(lefts)
    for (bit, members), left in zip(jobs, lefts):
        for terms in members:
            for array, names, block, size in terms:
                rows = array.size // array.shape[-1] >> len(names)
                arrays.append(array.reshape([2] * len(names) + [rows, array.shape[-1]]))
                shape, picks = [], []
                for name in names:
                    if name == bit:
                        shape.append(None)
                        picks.append(("other", slots[name]))
                    elif name not in left:
                        shape.append(None)
                        picks.append(("mine", slots[name]))
                    elif gridded and name == left[0]:
                        shape.append(None)
                        picks.append(("step", 0))
                    else:
                        shape.append(2)
                        picks.append(("all", 0))

                def index_map(j, info, picks=picks, block=block):
                    where = []
                    for kind, slot in picks:
                        if kind == "all":
                            where.append(0)
                        elif kind == "step":
                            where.append(lax.rem(j + info[0], 2) if flip else j)
                        else:
                            where.append(info[slot] if kind == "mine" else 1 - info[slot])
                    return (*where, 0, block)

                specs.append(pl.BlockSpec((*shape, rows, size), index_map))
        width = sum(terms[0][3] for terms in members)
        kind = jnp.bfloat16 if rows % 16 == 0 else jnp.float32
        outer = 1 << len(left)
        shapes.append(jax.ShapeDtypeStruct((outer, rows, width), kind))
        inner = outer // 2 if gridded else outer
        out_specs.append(pl.BlockSpec((inner, rows, width), lambda j, info: (j, 0, 0)))
        plan.append([len(terms) for terms in members])
    results = pl.pallas_call(
        functools.partial(combine_kernel, plan),
        out_shape=shapes,
        grid_spec=pltpu.PrefetchScalarGridSpec(
            num_scalar_prefetch=1,
            grid=(2 if gridded else 1,),
            in_specs=specs,
            out_specs=out_specs,
        ),
        name="combine",
        **params(),
    )(info, *arrays)
    return list(zip(results, lefts))


def finish_kernel(counts, tiles, info, *refs):
    *inputs, mine, send, scratch = refs
    place = 0
    for count in counts:
        value = inputs[0][...].astype(jnp.float32)
        for term in inputs[1:count]:
            value = value + term[...].astype(jnp.float32)
        inputs = inputs[count:]
        for tile in range(value.shape[1] // TILE):
            start = tiles[place] * TILE
            scratch[:, start : start + TILE] = value[:, tile * TILE : (tile + 1) * TILE]
            place += 1
    rows = mine.shape[0]
    for side, out in ((info[0], mine), (1 - info[0], send)):
        out[...] = scratch[pl.ds(pl.multiple_of(side * rows, rows), rows), :]


def picked(slots, terms):
    arrays, specs = [], []
    for array, names, block, size in terms:
        rows = array.size // array.shape[-1] >> len(names)
        arrays.append(array.reshape([2] * len(names) + [rows, array.shape[-1]]))
        specs.append(
            pl.BlockSpec(
                (*[None] * len(names), rows, size),
                lambda j, info, names=names, block=block: (
                    *[info[slots[name]] for name in names],
                    0,
                    block,
                ),
            )
        )
    return arrays, specs


def settle_kernel(plan, info, *refs):
    refs = list(refs)
    inputs = [[[refs.pop(0) for _ in range(count)] for count in counts] for counts, _ in plan]
    for members, (_, kinds) in zip(inputs, plan):
        if kinds is None:
            rows = members[0][0].shape[0]
            value = members[0][0][...].astype(jnp.float32)
            for term in members[0][1:]:
                value = value + term[...].astype(jnp.float32)
            across_rows = lax.broadcasted_iota(jnp.int32, (rows, rows), 0)
            across_columns = lax.broadcasted_iota(jnp.int32, (rows, rows), 1)
            for column in range(2):
                diagonal = jnp.where(
                    across_rows == across_columns, value[:, column : column + 1], 0.0
                )
                refs.pop(0)[...] = jnp.sum(diagonal, axis=0, keepdims=True)
            refs.pop(0)[...] = value[:, 2:5]
            continue
        outs = [refs.pop(0) for _ in kinds]
        edge = 0
        for terms in members:
            size = terms[0].shape[-1]
            value = terms[0][...].astype(jnp.float32)
            for term in terms[1:]:
                value = value + term[...].astype(jnp.float32)
            for out in outs:
                out[:, edge : edge + size] = value.astype(out.dtype)
            edge += size


def settle(info, slots, groups):
    arrays, specs, shapes, plan = [], [], [], []
    for members, kinds in groups:
        for terms in members:
            views, view_specs = picked(slots, terms)
            arrays += views
            specs += view_specs
        rows = views[0].shape[-2]
        width = sum(terms[0][3] for terms in members)
        if kinds is None:
            shapes += [jax.ShapeDtypeStruct((1, rows), jnp.float32)] * 2
            shapes.append(jax.ShapeDtypeStruct((rows, 3), jnp.float32))
        else:
            shapes += [jax.ShapeDtypeStruct((rows, width), kind) for kind in kinds]
        plan.append(([len(terms) for terms in members], kinds))
    return pl.pallas_call(
        functools.partial(settle_kernel, plan),
        out_shape=shapes,
        grid_spec=pltpu.PrefetchScalarGridSpec(
            num_scalar_prefetch=1,
            grid=(1,),
            in_specs=specs,
            out_specs=[fixed(*shape.shape) for shape in shapes],
        ),
        name="settle",
        **params(),
    )(info, *arrays)


def finish(info, slots, members, tiles):
    columns = len(tiles) * TILE
    arrays, specs = [], []
    for terms in members:
        views, view_specs = picked(slots, terms)
        rows = views[0].shape[-2]
        arrays += views
        specs += view_specs
    return pl.pallas_call(
        functools.partial(finish_kernel, [len(terms) for terms in members], tiles),
        out_shape=[jax.ShapeDtypeStruct((rows // 2, columns), jnp.float32)] * 2,
        grid_spec=pltpu.PrefetchScalarGridSpec(
            num_scalar_prefetch=1,
            grid=(1,),
            in_specs=specs,
            out_specs=[fixed(rows // 2, columns)] * 2,
            scratch_shapes=[pltpu.VMEM((rows, columns), jnp.float32)],
        ),
        name="finish",
        **params(),
    )(info, *arrays)


def local(
    tokens,
    cotangent,
    doc_lengths,
    norm_gain,
    in_weight,
    conv_taps,
    out_weight,
    ffn_gain,
    gate_weight,
    up_weight,
    down_weight,
):
    rows, width = tokens.shape
    hidden = down_weight.shape[0]
    chips = lax.axis_size("seq")
    top = chips.bit_length() - 2
    lower = list(range(top))
    bits = list(range(top, -1, -1))
    chip = lax.axis_index("seq")
    core = lax.axis_index("wa")
    coords = {bit: (chip >> bit) & 1 for bit in range(top + 1)}
    turned = dict(coords)
    turned[top] = coords[top] ^ core
    ordering = lax.optimization_barrier

    def after(value, *gates):
        return ordering((value, gates))[0]

    def ordered(low, high):
        return jnp.where(core == 0, low, high)

    def both(own, other, axis):
        return ordered(
            jnp.concatenate([own, other], axis=axis), jnp.concatenate([other, own], axis=axis)
        )

    w_in_other = partner(in_weight)
    w_out_other = partner(out_weight)
    small = jnp.concatenate([norm_gain[None], ffn_gain[None], conv_taps.T], axis=0)
    small = jnp.pad(small, ((0, 3), (0, 0)))
    small_other = partner(small)
    before_rows = shifted(tokens[rows - HALO :], 1)
    after_rows = shifted(jnp.concatenate([tokens[:HALO], cotangent[:HALO]], axis=1), -1)
    cot_other = partner(cotangent)
    after_other = partner(after_rows)
    early = (w_in_other, w_out_other, small_other, before_rows, cot_other, after_other)
    w_in_other, w_out_other, small_other, before_rows, cot_other, after_other = ordering(early)
    small = both(small, small_other, 1).astype(jnp.float32)
    gate_late, up_late = after((gate_weight, up_weight), early)
    gate_other = partner(gate_late)
    up_other = partner(up_late)

    place = lax.axis_index(AXES) * rows + jnp.arange(rows + HALO, dtype=jnp.int32)
    earlier = jnp.arange(doc_lengths.shape[0])
    earlier = earlier[:, None] < earlier[None, :]
    starts = jnp.sum(jnp.where(earlier, doc_lengths[:, None], 0), axis=0)
    first = jnp.any(place[:, None] == starts[None, :], axis=1)
    before = jnp.any((place - 1)[:, None] == starts[None, :], axis=1)
    keep_one = jnp.where(first, 0.0, 1.0)
    keep_two = jnp.where(jnp.logical_or(first, before), 0.0, 1.0)
    lane = lax.broadcasted_iota(jnp.int32, (rows + HALO, 128), 1)
    keeps = jnp.where(lane == 0, keep_one[:, None], keep_two[:, None]).astype(jnp.float32)
    info = [core] + [coords[bit] for bit in lower] + [coords[top], turned[top]]
    info = jnp.stack(info).astype(jnp.int32)

    *parts, hidden_res, norm_own, norm_send = conv_forward(
        info,
        tokens,
        before_rows,
        after_rows,
        small,
        keeps,
        in_weight,
        w_in_other,
        out_weight,
        w_out_other,
    )
    norm_other = partner(norm_send)
    norm_own, gate_other, up_other = ordering((norm_own, gate_other, up_other))
    per_chip = width // chips
    pers = (per_chip << lower[0], per_chip << lower[1])
    tiles = hidden // TILE
    split = tiles * 4 // 9
    counts = (split, tiles - split)
    orders = (lower, [lower[1], lower[0]] + lower[2:])

    act, back_keep, back_send, *one, whole = ffn(
        info,
        (norm_own, norm_other),
        (cotangent, after_rows, cot_other, after_other),
        (gate_weight, gate_other, up_weight, up_other),
        down_weight,
        split,
        pers,
    )
    one_x = across(one[0], orders[0][0])
    one_y = across(one[2], orders[1][0])
    came = partner(back_send)

    groups = [
        [low + (level << (top - 1)) for level in range(4)] for low in range(1 << (top - 1))
    ]
    quarter = lax.psum_scatter(
        whole, "seq", scatter_dimension=0, axis_index_groups=groups, tiled=True
    )

    slots = {bit: 1 + bit for bit in bits}
    turned_slots = dict(slots)
    turned_slots[top] = 2 + top

    def plain(array, names):
        return (array, names, 0, array.shape[-1])

    def gated(streams, *gates):
        held = after([terms[-1][0] for terms in streams], gates)
        return [
            terms[:-1] + [(array, *terms[-1][1:])] for terms, array in zip(streams, held)
        ]

    def without(names, *taken):
        return [name for name in names if name not in taken]

    def send_on(streams, names, use=slots):
        results = combine(info, use, streams)
        return [send for send, _ in results], [
            (across(send, bit), left) for (bit, _), (send, left) in zip(streams, results)
        ]

    def upper_sum(value):
        value = value.reshape(-1, value.shape[-1])
        return lax.psum_scatter(
            value, "seq", scatter_dimension=0, axis_index_groups=groups, tiled=True
        )

    down_pers = [2 * hidden // chips << bit for bit in (lower[0], lower[1])]
    out_keep, out_send, *down_halves = down_part(
        info, act, cotangent, cot_other, down_weight, down_pers
    )
    came, out_send, down_halves, one_x, one_y = ordering(
        (came, out_send, down_halves, one_x, one_y)
    )

    down_x = across(down_halves[0], orders[0][0])
    down_y = across(down_halves[2], orders[1][0])
    out_came = partner(out_send)
    one_terms = [
        [plain(keep, without(bits, order[0])), plain(got, without(bits, order[0]))]
        for keep, got, order in ((one[1], one_x, orders[0]), (one[3], one_y, orders[1]))
    ]
    one_sent, one_got = send_on(
        [(order[1], [terms]) for terms, order in zip(one_terms, orders)], bits, turned_slots
    )
    one_got = [got for got, _ in one_got]
    came = after(came, one_sent)

    def side_by_side(streams, order, use=slots):
        sent = None
        for bit in order:
            sent, ((got, left),) = send_on([(bit, streams)], None, use)
            edge, members = 0, []
            for terms in streams:
                size = terms[0][3]
                members.append(terms + [(got, left, edge, size)])
                edge += size
            for terms in members:
                array, left, edge, size = terms[-1]
                if edge % size:
                    array, edge = array[..., edge : edge + size], 0
                terms[-1] = (array, left, edge // size, size)
            streams = members
        return sent, streams

    input_grad, conv_send, *conv_keeps = conv_backward(
        info,
        tokens,
        hidden_res,
        cotangent,
        after_rows,
        back_keep,
        came,
        small,
        keeps,
        parts,
        in_weight,
        w_in_other,
        out_weight,
        w_out_other,
        2 * chips,
    )
    conv_send, conv_keeps, down_x, down_y = ordering((conv_send, conv_keeps, down_x, down_y))
    conv_came = partner(conv_send)

    down_bits = bits[1:]
    down_terms = [
        [plain(keep, without(down_bits, order[0])), plain(got, without(down_bits, order[0]))]
        for keep, got, order in (
            (down_halves[1], down_x, orders[0]),
            (down_halves[3], down_y, orders[1]),
        )
    ]
    down_sent, down_got = send_on(
        [(order[1], [terms]) for terms, order in zip(down_terms, orders)], down_bits
    )
    down_got = [got for got, _ in down_got]

    conv_came = after(conv_came, down_sent)
    conv_members = [
        [
            [plain(conv_keeps[member], bits), (conv_came, bits, member * width // size, size)]
            for member, size in members
        ]
        for members in (((0, width), (1, width)), ((2, width), (3, width), (4, 128)))
    ]
    conv_sent, conv_got = send_on(
        [(order[0], members) for members, order in zip(conv_members, orders)], bits
    )
    conv_got = [got for got, _ in conv_got]

    one_got = after(one_got, conv_sent)
    one_streams = [
        terms + [plain(got, without(bits, *order[:2]))]
        for terms, got, order in zip(one_terms, one_got, orders)
    ]
    _, one_streams = side_by_side(one_streams, lower[2 : top - 1], turned_slots)
    ((one_all, _),) = combine(info, turned_slots, [(None, one_streams)], flip=True)
    one_done = upper_sum(one_all)

    down_got = after(down_got, one_all)
    down_streams = [
        terms + [plain(got, without(down_bits, *order[:2]))]
        for terms, got, order in zip(down_terms, down_got, orders)
    ]
    down_sent, down_streams = side_by_side(down_streams, lower[2:])

    down_streams = gated(down_streams, down_sent)
    part, down_last = settle(info, slots, [(down_streams, (jnp.float32, jnp.bfloat16))])
    pairs = [
        (source * 2 + side, (source ^ (1 << top)) * 2 + side)
        for source in range(chips)
        for side in range(2)
        if (source >> top) & 1 != side
    ]
    down_far = lax.ppermute(down_last, AXES, pairs)

    conv_got = after(conv_got, down_last)
    for index, (members, order) in enumerate(zip(conv_members, orders)):
        edge = 0
        for terms in members:
            size = terms[0][3]
            terms.append((conv_got[index], without(bits, order[0]), edge // size, size))
            edge += size
    conv_sent, conv_two = send_on(
        [(order[1], members) for members, order in zip(conv_members, orders)], bits
    )
    conv_two = [got for got, _ in conv_two]

    quarter = after(quarter, conv_sent)
    edge = counts[1] * TILE
    two_terms = [[(quarter, bits[2:], block, edge)] for block in range(2)]
    two_sent, two_got = send_on(
        [(order[0], [terms]) for terms, order in zip(two_terms, orders)], bits[2:]
    )
    two_got = [got for got, _ in two_got]
    out_came = after(out_came, two_sent)
    block_out = (hidden_res[:rows] + out_keep + out_came).astype(jnp.bfloat16)
    conv_two = after(conv_two, two_sent, block_out)
    conv_streams = []
    for members, got, order in zip(conv_members, conv_two, orders):
        edge = 0
        for terms in members:
            size = terms[0][3]
            conv_streams.append(terms + [(got, without(bits, *order[:2]), edge // size, size)])
            edge += size
    _, conv_streams = side_by_side(conv_streams, lower[2 : top - 1])
    ((conv_all, _),) = combine(info, slots, [(None, conv_streams)])
    conv_done = upper_sum(conv_all)
    two_got = after(two_got, conv_all)
    two_terms = [
        terms + [plain(got, without(bits[2:], order[0]))]
        for terms, got, order in zip(two_terms, two_got, orders)
    ]
    two_sent, two_got = send_on(
        [(order[1], [terms]) for terms, order in zip(two_terms, orders)], bits[2:]
    )
    two_streams = [terms + [plain(*got)] for terms, got in zip(two_terms, two_got)]
    _, two_streams = side_by_side(two_streams, lower[2 : top - 1])

    part, down_far = after((part, down_far), conv_all)
    part = part + down_far.astype(jnp.float32)
    part = part.reshape(2, -1, width)
    down_out = jnp.where(
        coords[top] == core, take(part, core, 0), partner(take(part, 1 - core, 0))
    )
    b_out, out_out, c_out, x_out, vectors = (
        [(conv_done, [], member * width // size, size)]
        for member, size in enumerate([width] * 4 + [128])
    )
    in_out, out_out, gain_one_out, gain_two_out, taps_out = settle(
        info,
        slots,
        [
            ([b_out, c_out, x_out], (jnp.float32,)),
            ([out_out], (jnp.float32,)),
            ([vectors], None),
        ],
    )

    gate_tiles = [tile for tile in range(counts[0])] + [tiles + tile for tile in range(counts[0])]
    for tile in range(counts[1]):
        gate_tiles += [counts[0] + tile, tiles + counts[0] + tile]
    kept, send = finish(info, slots, [[plain(one_done, [])]] + two_streams, gate_tiles)
    other = partner(send)
    gate_out = both(kept[:, :hidden], other[:, :hidden], 1)
    up_out = both(kept[:, hidden:], other[:, hidden:], 1)
    return (
        block_out,
        input_grad,
        gain_one_out.reshape(-1),
        in_out,
        taps_out,
        out_out,
        gain_two_out.reshape(-1),
        gate_out,
        up_out,
        down_out,
    )


def solution(mesh):
    placed = (
        P(AXES, None),
        P(AXES, None),
        P(),
        P("wa"),
        P("wa", None),
        P("wa", None),
        P("wa", None),
        P("wa"),
        P("wa", None),
        P("wa", None),
        P("wa", None),
    )
    return jax.shard_map(
        local,
        mesh=mesh,
        in_specs=placed,
        out_specs=(
            P(AXES, None),
            P(AXES, None),
            P(AXES),
            P(AXES, None),
            P(AXES, None),
            P(AXES, None),
            P(AXES),
            P(AXES, None),
            P(AXES, None),
            P(AXES, None),
        ),
        check_vma=False,
    )
```
